32 devices in a mesh: parts: 2 (over y), blk: 4 (over z), reader: 4 (over x, core), sub: 1.
Axes of the slice: x: 2, y: 2, z: 4, core: 2. Of those that a mesh axis runs over, the one named last changes fastest.
Arguments:
- images: bfloat16 [3072, 8192], P(('parts', 'blk', 'reader'), 'sub'), parts along dimension 0, may hold values from -40 to 40
- routes: int32 [3072, 2], P(('parts', 'blk', 'reader')), parts along dimension 0, may hold values from 0 to 3, all different within a row; in each aligned block of 96 rows (0 to 95, 96 to 191, ...) at most 96 rows name the same one
- projections: bfloat16 [8, 128, 8192], P(('parts', 'reader'), 'blk', 'sub'), parts along dimension 0, may hold values from -8 to 8
- noise_weights: float32 [16384], P(('parts', 'sub')), parts along dimension 0, may hold values from 0.3 to 3
Outputs:
- weighted_sums: float32 [8, 128, 8192], P(('parts', 'reader'), 'blk', 'sub'), parts along dimension 0
- normalizer: float32 [3072], P(('parts', 'blk', 'reader')), parts along dimension 0
The draws below stay inside these ranges and needn't reach their ends.
There are 2 independent parts, one for each index of `parts`. The reference program is written for one: setup_inputs(seed, part) draws one part's arguments, and reference() takes and returns one part's arrays. A program takes and returns all parts, laid end to end along the dimension named above; each array names one. Nothing has to cross between parts.
Inputs may be any that keep to these rules, and one draw needn't show every extreme that they name: `routes`: each row names 2 different class groups. In the rows of one device (aligned blocks of 96 rows) no group is named by more than 96 rows, a bound that some block reaches.
All inputs are finite; a program needn't handle non-finite values.
Results may differ from the reference program's by a relative error of at most 0.019.
Values may be sent and summed in bfloat16 or wider, within the bound.
A program may use at most 64 MiB of HBM per device.

```python
import math
import jax
import jax.numpy as jnp
import numpy as np
from jax import lax

COEF = 8192
PART_DEV = 96
TOP = 2
GROUPS = 4
GREFS = 128
CAP = 96
RECV = 384
PARTICLES = 1536
N_BLK = 4
N_READER = 4


def projection_values(key):
    folded = jax.random.fold_in(key, 101)
    scale_key, vector_key = jax.random.split(folded)
    scales = jnp.exp(jax.random.uniform(scale_key, (GROUPS, GREFS, 1), jnp.float32, math.log(0.6), math.log(6.0)))
    vectors = jax.random.truncated_normal(vector_key, -4.0, 4.0, (GROUPS, GREFS, COEF), jnp.float32)
    return jnp.clip(scales * vectors * COEF ** (-0.5), -8.0, 8.0)


def draw_projections(key, part):
    return projection_values(key).astype(jnp.bfloat16)


def draw_images(key, part):
    folded = jax.random.fold_in(key, 202)
    key_list = jax.random.split(folded, 2)
    row_scale = jnp.exp(jax.random.uniform(key_list[0], (PARTICLES, 1), jnp.float32, math.log(0.3), math.log(3.0)))
    values = row_scale * jax.random.truncated_normal(key_list[1], -6.0, 6.0, (PARTICLES, COEF), jnp.float32)
    return jnp.clip(values, -40.0, 40.0).astype(jnp.bfloat16)


def deal_out(rng, own, number, rows, number_of, top, bound, slope):
    ranking = jax.random.permutation(rng, number_of)
    crowded, usual = shares(number_of, rows * top, bound, slope, True), shares(number_of, rows * top, bound, slope, False)
    places = jnp.arange(number_of)

    def named(sizes, rotation):
        used = int((sizes > 0).sum())
        fixed = max(1, used // 4)
        passed = fixed + (places - fixed + rotation * (used - fixed)) % max(1, number_of - fixed)
        return jnp.zeros((number_of,), jnp.int32).at[ranking[jnp.where(places < fixed, places, passed)]].set(jnp.asarray(sizes, jnp.int32))

    sizes = jnp.where(number % 4 == 0, named(crowded, number // 4), named(usual, number - number // 4 - 1))
    mixed = jax.random.permutation(jax.random.fold_in(own, 3), number_of)
    giver, receiver = mixed[0:number_of // 2 * 2:2], mixed[1:number_of // 2 * 2:2]
    slack = jnp.minimum(sizes[giver] - 1, bound - sizes[receiver]) // 2
    slack = jnp.where((giver == ranking[0]) | (receiver == ranking[0]) | (sizes[receiver] == 0), 0, jnp.maximum(slack, 0))
    passed = jax.random.randint(jax.random.fold_in(own, 4), (number_of // 2,), 0, 1 << 20) % (slack + 1)
    sizes = sizes.at[giver].add(-passed).at[receiver].add(passed)
    members = jnp.searchsorted(jnp.cumsum(sizes), jnp.arange(rows * top), side="right").astype(jnp.int32)
    listing = members.reshape(top, rows).T
    listing = listing[jax.random.permutation(jax.random.fold_in(own, 1), rows)]
    rotation = jax.random.randint(jax.random.fold_in(own, 2), (rows, 1), 0, top)
    return jnp.take_along_axis(listing, (jnp.arange(top)[None, :] + rotation) % top, axis=1)


def shares(amount, total, bound, skew, full):
    loads = [(1 << 20) // math.isqrt(rank ** skew) + 1 for rank in range(1, amount + 1)]
    largest = bound if full else min(bound, max(-(-total // amount), total * loads[0] // sum(loads)))
    least = 1 if total - largest >= amount - 1 else 0
    holding, spare = [largest] + [least] * (amount - 1), total - largest - least * (amount - 1)
    while spare > 0:
        movable = [i for i in range(1, amount) if holding[i] < largest] or [i for i in range(1, amount) if holding[i] < bound]
        pool, remaining = sum([loads[i] for i in movable]), spare
        for i in movable:
            extra = min(bound - holding[i], max(1, remaining * loads[i] // pool), spare)
            holding[i] = holding[i] + extra
            spare = spare - extra
    return np.array(holding)


def setup_inputs(seed: int = 0, part: int = 0) -> dict:
    keys = jax.random.split(jax.random.key(seed), 5)
    part_keys = jax.random.split(jax.random.fold_in(keys[4], part), 5)
    images = draw_images(jax.random.fold_in(jax.random.fold_in(keys[4], part), 71), part)
    routes_keys = jax.random.split(jax.random.fold_in(part_keys[1], 1), PARTICLES // PART_DEV)
    routes_turns = jax.random.permutation(jax.random.fold_in(part_keys[1], 3), PARTICLES // PART_DEV)
    routes = jax.vmap(lambda own, number: deal_out(jax.random.fold_in(part_keys[1], 2), own, number, PART_DEV, N_READER, TOP, CAP, 2))(routes_keys, routes_turns).reshape((PARTICLES, TOP))
    projections = draw_projections(jax.random.fold_in(jax.random.fold_in(keys[4], part), 71), part)
    noise_weights = jnp.clip(jnp.exp(jax.random.uniform(part_keys[3], (COEF,), jnp.float32, math.log(0.3), math.log(3.0))), 0.3, 3.0)
    return dict(images=images, routes=routes, projections=projections, noise_weights=noise_weights)


def combine_stats(row_peaks, row_totals):
    highest = jnp.max(row_peaks, axis=-1)
    spread = row_totals * jnp.exp(row_peaks - highest[..., None])
    return highest + jnp.log(jnp.sum(spread, axis=-1))


def reference(images, routes, projections, noise_weights):
    scaled = projections.astype(jnp.float32) * noise_weights[None, None, :]
    weighted = scaled.astype(jnp.bfloat16)
    penalty = 0.5 * jnp.sum(scaled * projections.astype(jnp.float32), axis=2)
    row_count = N_READER * PART_DEV
    image_rows = images.reshape(N_BLK, row_count, COEF)
    route_rows = routes.reshape(N_BLK, row_count, TOP)
    group_numbers = jnp.arange(GROUPS, dtype=jnp.int32)
    row_numbers = jnp.arange(row_count, dtype=jnp.int32)

    def one_row(running, inputs):
        block_images, block_routes = inputs

        def score_group(group_id):
            member = jnp.any(block_routes == group_id, axis=1)
            ordering = jnp.argsort(jnp.where(member, 0, 1).astype(jnp.int32), stable=True)[:RECV].astype(jnp.int32)
            chosen = block_images[ordering]
            scores = jnp.dot(chosen, weighted[group_id].T, preferred_element_type=jnp.float32) - penalty[group_id][None, :]
            row_peak = jnp.max(scores, axis=1)
            row_total = jnp.sum(jnp.exp(scores - row_peak[:, None]), axis=1)
            full_peak = jnp.zeros((row_count,), jnp.float32).at[ordering].set(row_peak)
            full_total = jnp.zeros((row_count,), jnp.float32).at[ordering].set(row_total)
            return scores, ordering, member[ordering], full_peak, full_total

        score_table, order_table, live_table, peak_table, total_table = lax.map(score_group, group_numbers)
        picked_peaks = peak_table[block_routes, row_numbers[:, None]]
        picked_totals = total_table[block_routes, row_numbers[:, None]]
        particle_norm = combine_stats(picked_peaks, picked_totals)

        def back_group(inputs):
            scores, ordering, live_slot = inputs
            slot_norm = particle_norm[ordering]
            exponent = jnp.where(live_slot[:, None], scores - slot_norm[:, None], -jnp.inf)
            posterior = jnp.exp(exponent).astype(jnp.bfloat16)
            chosen = block_images[ordering]
            partial_value = jnp.dot(posterior.T, chosen, preferred_element_type=jnp.float32)
            return partial_value.astype(jnp.bfloat16)

        partials = lax.map(back_group, (score_table, order_table, live_table))
        partials = lax.optimization_barrier(partials)
        return running + partials.astype(jnp.float32), particle_norm

    initial = jnp.zeros((GROUPS, GREFS, COEF), jnp.float32)
    total_sums, norm_rows = lax.scan(one_row, initial, (image_rows, route_rows))
    return total_sums, norm_rows.reshape(PARTICLES)
```

```python
from functools import partial

import jax
import jax.numpy as jnp
from jax import lax
from jax.experimental import pallas as pl
from jax.experimental.pallas import tpu as pltpu
from jax.sharding import PartitionSpec as P

MESH = pl.DeviceIdType.MESH


def from_behind(block, axis, distance):
    devices = range(lax.axis_size(axis))
    route = [((i - distance) % len(devices), i) for i in devices]
    return lax.ppermute(block, axis, route)


def slot_positions(route_block):
    flat = route_block.reshape(-1)
    order = jnp.arange(flat.shape[0], dtype=jnp.int32)
    earlier = (order[None, :] < order[:, None]) & (flat[None, :] == flat[:, None])
    return jnp.sum(earlier.astype(jnp.int32), axis=1).reshape(route_block.shape)


def combine_stats(row_peaks, row_totals):
    highest = jnp.max(row_peaks, axis=-1)
    spread = row_totals * jnp.exp(row_peaks - highest[..., None])
    return highest + jnp.log(jnp.sum(spread, axis=-1))


def routed(images, routes, projections, noise_weights):
    groups = lax.axis_size("reader")
    cycle_size = lax.axis_size("blk")
    my_group = lax.axis_index("reader")
    my_member = lax.axis_index("blk")
    per_device, top_count = routes.shape
    half_width = images.shape[1]
    capacity = min(per_device, 2 * per_device * top_count // groups)
    slot_count = groups * capacity
    ref_count = projections.shape[1]
    all_refs = ref_count * cycle_size
    anchor = jnp.zeros((), jnp.int32)
    own_index = slot_positions(routes)
    own_target = routes * capacity + own_index
    sources = jnp.broadcast_to(jnp.arange(per_device, dtype=jnp.int32)[:, None], routes.shape)
    picker = (
        jnp.full((slot_count,), per_device, jnp.int32)
        .at[own_target.reshape(-1)]
        .set(sources.reshape(-1))
    )
    padded = jnp.concatenate([images, jnp.zeros((1, half_width), images.dtype)], axis=0)
    outgoing = padded[picker].reshape(groups, capacity, half_width)
    received = lax.all_to_all(outgoing, "reader", split_axis=0, concat_axis=0, tiled=True).reshape(
        slot_count, half_width
    )
    every_route = lax.all_gather(routes, "reader", axis=0, tiled=True).reshape(
        groups, per_device, top_count
    )
    every_index = jax.vmap(slot_positions)(every_route)
    senders = jnp.arange(groups, dtype=jnp.int32)[:, None, None]
    landing = jnp.where(every_route == my_group, senders * capacity + every_index, slot_count)
    live_slot = jnp.zeros((slot_count,), jnp.int32).at[landing.reshape(-1)].set(1, mode="drop") > 0

    def score_block(ref_block):
        scaled = ref_block.astype(jnp.float32) * noise_weights[None, :]
        weighted = scaled.astype(jnp.bfloat16)
        penalty = 0.5 * jnp.sum(scaled * ref_block.astype(jnp.float32), axis=1)
        partial_scores = lax.dot_general(
            weighted, received, (((1,), (1,)), ((), ())), preferred_element_type=jnp.float32
        )
        return partial_scores - penalty[:, None]

    def cycle_turn(rotation, carry):
        ref_block, score_table = carry
        position = (my_member - rotation) % cycle_size
        score_table = lax.dynamic_update_slice(
            score_table, score_block(ref_block)[None], (position, anchor, anchor)
        )
        ref_block = from_behind(ref_block, "blk", 1)
        return (ref_block, score_table)

    empty_table = jnp.zeros((cycle_size, ref_count, slot_count), jnp.float32)
    ref_block, score_table = lax.fori_loop(
        0, cycle_size - 1, cycle_turn, (projections[0], empty_table)
    )
    position = (my_member + 1) % cycle_size
    score_table = lax.dynamic_update_slice(
        score_table, score_block(ref_block)[None], (position, anchor, anchor)
    )
    score_table = lax.psum(score_table, "sub")
    scores = score_table.reshape(all_refs, slot_count)
    row_peak = jnp.max(scores, axis=0)
    row_total = jnp.sum(jnp.exp(scores - row_peak[None, :]), axis=0)
    back_peak, back_total = (
        lax.all_to_all(
            row_peak.reshape(groups, capacity), "reader", split_axis=0, concat_axis=0, tiled=True
        ),
        lax.all_to_all(
            row_total.reshape(groups, capacity), "reader", split_axis=0, concat_axis=0, tiled=True
        ),
    )
    normalizer = combine_stats(
        back_peak.reshape(-1)[own_target], back_total.reshape(-1)[own_target]
    )
    outgoing_norm = (
        jnp.zeros((slot_count,), jnp.float32)
        .at[own_target.reshape(-1)]
        .set(jnp.repeat(normalizer, top_count))
    )
    slot_norm = lax.all_to_all(
        outgoing_norm.reshape(groups, capacity), "reader", split_axis=0, concat_axis=0, tiled=True
    ).reshape(slot_count)
    exponent = jnp.where(live_slot[None, :], scores - slot_norm[None, :], -jnp.inf)
    posterior = jnp.exp(exponent).astype(jnp.bfloat16)
    summed = lax.psum_scatter(
        jnp.dot(posterior, received, preferred_element_type=jnp.float32).astype(jnp.bfloat16),
        "blk",
        scatter_dimension=0,
        tiled=True,
    ).astype(jnp.float32)
    return (summed[None], normalizer)


def paired(
    images, routes_in, proj, noise_in,
    out, norm,
    routes, noise, X, XF, PR, S, SR, QP, QO, QF, QT, QTF, PROD, TE, RE, TM, RM, TI, RI, O,
    loc, px_snd, pb_snd, pm_snd, pc_snd, p_rcv, xx_snd, xc_snd, x_rcv, xf_snd, xfc_snd, xf_rcv,
    s_snd, s_rcv, q_snd, q_rcv, qf_snd, qf_rcv, e_snd, e_rcv, m_snd, m_rcv, i_snd, i_rcv,
    own_snd, o_snd, o_rcv,
):
    r = lax.axis_index("reader")
    b = lax.axis_index("blk")
    x, c = r // 2, r % 2
    rx, rc = (r + 2) % 4, x * 2 + 1 - c
    rd = (rc + 2) % 4
    side = b // 2
    inner, end = 1 + side, 3 * side
    far_inner, far_end = 2 - side, 3 - 3 * side
    buddy, across = inner + end - b, 3 - b
    is_end = b == end
    is_inner = b == inner
    rows = images.shape[0]
    refs = proj.shape[0]
    H = X.shape[4 - 1]
    F = H // 2
    T, tile = O.shape[0], O.shape[3]
    TF = F // tile
    width = 4 * refs
    halves = (0, 1)

    def remote(src, dst, snd, rcv, **where):
        return pltpu.make_async_remote_copy(
            src_ref=src, dst_ref=dst, send_sem=snd, recv_sem=rcv,
            device_id=where, device_id_type=MESH,
        )

    def arrived(dst, sem):
        remote(dst, dst, sem, sem, reader=rx).wait_recv()

    def columns(i, h):
        return pl.ds(pl.multiple_of(i * H + h * F, F), F)

    def part(src, g, h):
        return PR.at[src, g, :, pl.ds(h * F, F)]

    def own_piece(h):
        return proj.at[:, columns(x, h)]

    def proj_x(h):
        return remote(proj.at[:, columns(1 - x, h)], part(b, r, h), px_snd.at[h], p_rcv.at[b, r, h], reader=rx)

    def to_core(piece, src, g, h):
        return remote(piece, part(src, g, h), pc_snd.at[src, g, h], p_rcv.at[src, g, h], reader=rc)

    def to_buddy(piece, src, g, h):
        return remote(piece, part(src, g, h), pb_snd.at[src, g, h], p_rcv.at[src, g, h], blk=buddy)

    def to_across(piece, src, g, h):
        return remote(piece, part(src, g, h), pm_snd.at[src, g, h], p_rcv.at[src, g, h], blk=across)

    def image_x(h):
        return remote(
            images.at[:, columns(1 - x, h)], X.at[c, x, :, pl.ds(h * F, F)],
            xx_snd.at[h], x_rcv.at[c, x, h], reader=rx,
        )

    def own_image_core():
        return remote(
            images.at[:, pl.ds(pl.multiple_of(x * H, H), H)], X.at[c, x],
            xc_snd.at[0], x_rcv.at[c, x, 0], reader=rc,
        )

    def other_image_core():
        return remote(X.at[c, 1 - x], X.at[c, 1 - x], xc_snd.at[1], x_rcv.at[c, 1 - x, 0], reader=rc)

    def own_far():
        return remote(images.at[:, columns(x, 0)], XF.at[c, x], xf_snd.at[0], xf_rcv.at[c, x], blk=buddy)

    def other_far():
        return remote(
            X.at[c, 1 - x, :, pl.ds(0, F)], XF.at[c, 1 - x], xf_snd.at[1], xf_rcv.at[c, 1 - x], blk=buddy
        )

    def far_core(i):
        return remote(XF.at[c, i], XF.at[c, i], xfc_snd.at[i], xf_rcv.at[c, i], reader=rc)

    def score_copy(src):
        return remote(S.at[src, 1 - x], SR.at[src], s_snd.at[src], s_rcv.at[src], reader=rx)

    def post_copy(k):
        source, to = ((QP.at[:, c, x], rx), (QO, rc), (QO, rd))[k]
        return remote(source, QP.at[:, c, x], q_snd.at[k], q_rcv.at[c, x], reader=to)

    def post_far(i, j):
        return remote(QP.at[:, i, j], QF.at[:, i, j], qf_snd.at[i, j], qf_rcv.at[i, j], blk=buddy)

    def end_copy(k, t):
        return remote(TE.at[k, t], RE.at[k, t], e_snd.at[k, t], e_rcv.at[k, t], blk=buddy)

    def middle_copy(k, t):
        return remote(TM.at[k, t], RM.at[k, t], m_snd.at[k, t], m_rcv.at[k, t], blk=across)

    def inner_copy(t):
        return remote(TI.at[t], RI.at[t], i_snd.at[t], i_rcv.at[t], blk=buddy)

    def out_span(i, t):
        return out.at[:, pl.ds(pl.multiple_of(i * H + t * tile, tile), tile)]

    def out_x(src, t):
        return remote(src.at[t, 1 - x], out_span(x, t), o_snd.at[t], o_rcv.at[t], reader=rx)

    def out_own(src, t):
        return pltpu.make_async_copy(src.at[t, x], out_span(x, t), own_snd.at[t])

    own_proj = pltpu.make_async_copy(proj.at[:, pl.ds(pl.multiple_of(x * H, H), H)], PR.at[b, r], loc.at[0])
    own_image = pltpu.make_async_copy(
        images.at[:, pl.ds(pl.multiple_of(x * H, H), H)], X.at[c, x], loc.at[1]
    )
    noise_copy = pltpu.make_async_copy(
        noise_in.at[pl.ds(pl.multiple_of(x * H, H), H)], noise, loc.at[2]
    )
    routes_copy = pltpu.make_async_copy(routes_in, routes, loc.at[3])

    barrier = pltpu.get_barrier_semaphore()
    for k in (rx, rc, rd):
        pl.semaphore_signal(barrier, inc=1, device_id={"reader": k}, device_id_type=MESH)
    pl.semaphore_signal(barrier, inc=1, device_id={"blk": buddy}, device_id_type=MESH)

    @pl.when(is_inner)
    def _():
        pl.semaphore_signal(barrier, inc=1, device_id={"blk": across}, device_id_type=MESH)

    own_proj.start()
    own_image.start()
    noise_copy.start()
    routes_copy.start()
    pl.semaphore_wait(barrier, 4 + is_inner.astype(jnp.int32))

    for h in halves:
        proj_x(h).start()
        to_buddy(own_piece(h), b, r, h).start()

        @pl.when(is_inner)
        def _():
            to_across(own_piece(h), b, r, h).start()

    for h in halves:
        to_core(own_piece(h), b, r, h).start()
    own_image_core().start()
    for h in halves:
        piece = part(b, rx, h)
        arrived(piece, p_rcv.at[b, rx, h])
        to_buddy(piece, b, rx, h).start()

        @pl.when(is_inner)
        def _():
            to_across(piece, b, rx, h).start()

        image_x(h).start()
        to_core(piece, b, rx, h).start()

    pieces = ((r, 0), (r, 1), (rx, 0), (rx, 1))

    @pl.when(is_end)
    def _():
        own_far().start()
        for g, h in pieces:
            arrived(part(buddy, g, h), p_rcv.at[buddy, g, h])
            to_core(part(buddy, g, h), buddy, g, h).start()
        arrived(X.at[c, 1 - x, :, pl.ds(0, F)], x_rcv.at[c, 1 - x, 0])
        other_far().start()
        for g, h in pieces:
            arrived(part(far_inner, g, h), p_rcv.at[far_inner, g, h])
            to_core(part(far_inner, g, h), far_inner, g, h).start()
        arrived(X.at[c, 1 - x, :, pl.ds(F, F)], x_rcv.at[c, 1 - x, 1])

    @pl.when(is_inner)
    def _():
        for g, h in pieces:
            piece = part(buddy, g, h)
            arrived(piece, p_rcv.at[buddy, g, h])
            to_across(piece, buddy, g, h).start()
            to_core(piece, buddy, g, h).start()
            piece = part(far_inner, g, h)
            arrived(piece, p_rcv.at[far_inner, g, h])
            to_buddy(piece, far_inner, g, h).start()
            to_core(piece, far_inner, g, h).start()
        for g, h in pieces:
            piece = part(far_end, g, h)
            arrived(piece, p_rcv.at[far_end, g, h])
            to_buddy(piece, far_end, g, h).start()
            to_core(piece, far_end, g, h).start()
        for h in halves:
            arrived(X.at[c, 1 - x, :, pl.ds(h * F, F)], x_rcv.at[c, 1 - x, h])

    other_image_core().start()
    own_proj.wait()
    own_image.wait()
    noise_copy.wait()
    routes_copy.wait()

    def score_half(src, h):
        scores = jnp.zeros((2 * rows, width), jnp.float32)
        penalty = jnp.zeros((width, 128), jnp.float32)
        for t in range(TF):
            cut = pl.ds(h * F + t * tile, tile)
            refs_f = PR[src, :, :, cut].reshape(width, tile).astype(jnp.float32)
            scaled = refs_f * noise[cut][None, :]
            scores = scores + lax.dot_general(
                X[c, :, :, cut].reshape(2 * rows, tile), scaled.astype(jnp.bfloat16),
                (((1,), (1,)), ((), ())), preferred_element_type=jnp.float32,
            )
            squares = scaled * refs_f
            for lane in range(0, tile, 128):
                penalty = penalty + squares[:, lane : lane + 128]
        penalty_row = lax.dot_general(
            jnp.full((8, 128), 0.5, jnp.float32), penalty,
            (((1,), (1,)), ((), ())), preferred_element_type=jnp.float32,
            precision=lax.Precision.HIGHEST,
        )
        scores = (scores - penalty_row[0:1]).reshape(2, rows, width)
        S[src] = scores if h == 0 else S[src] + scores

    def from_core(src, h):
        for g in (rc, rd):
            arrived(part(src, g, h), p_rcv.at[src, g, h])

    def score_source(i, carry):
        src = jnp.where(i == 0, b, jnp.where(i == 1, buddy, far_inner))
        for h in halves:
            from_core(src, h)
            score_half(src, h)
        score_copy(src).start()
        return carry

    lax.fori_loop(0, 3, score_source, 0)
    for h in halves:
        @pl.when(is_end)
        def _():
            for g, k in (pieces[:3], pieces[3:])[h]:
                piece = part(far_end, g, k)
                arrived(piece, p_rcv.at[far_end, g, k])
                to_core(piece, far_end, g, k).start()

        from_core(far_end, h)
        score_half(far_end, h)
    score_copy(far_end).start()

    lane = lax.broadcasted_iota(jnp.int32, (rows, width), 1)
    lane_group = lane // refs
    diagonal = lax.broadcasted_iota(jnp.int32, (rows, rows), 0) == lax.broadcasted_iota(
        jnp.int32, (rows, rows), 1
    )

    def column(row):
        return jnp.sum(jnp.where(diagonal, row, 0.0), axis=1, keepdims=True).astype(jnp.int32)

    names = routes[...].astype(jnp.float32)
    named = (column(names[0:1]) == lane_group) | (column(names[1:2]) == lane_group)
    chunks = []
    for d in range(4):
        arrived(SR.at[d], s_rcv.at[d])
        chunks.append(jnp.where(named, S[d, x] + SR[d], -jnp.inf))
    highest = jnp.maximum(jnp.maximum(chunks[0], chunks[1]), jnp.maximum(chunks[2], chunks[3]))
    highest = jnp.max(highest, axis=1, keepdims=True)
    spread = [jnp.exp(chunk - highest) for chunk in chunks]
    total = jnp.sum((spread[0] + spread[1]) + (spread[2] + spread[3]), axis=1, keepdims=True)
    normalizer = highest + jnp.log(total)
    norm[...] = jnp.broadcast_to(normalizer, norm.shape)
    even = lane_group % 2 == 0
    for p in halves:
        low = jnp.exp(chunks[2 * p] - normalizer)
        high = jnp.exp(chunks[2 * p + 1] - normalizer)
        zero = jnp.where(even, low, pltpu.roll(high, refs, 1))
        one = jnp.where(even, pltpu.roll(low, width - refs, 1), high)
        QP[p, c, x] = jnp.where(c == 0, zero, one).astype(jnp.bfloat16)
        QO[p] = jnp.where(c == 0, one, zero).astype(jnp.bfloat16)
    for k in (2, 0, 1):
        post_copy(k).start()

    @pl.when(is_end)
    def _():
        post_far(c, x).start()

    for i, j in ((1 - c, x), (c, 1 - x), (1 - c, 1 - x)):
        arrived(QP.at[:, i, j], q_rcv.at[i, j])

        @pl.when(is_end)
        def _():
            post_far(i, j).start()

    def turned(block):
        flat = block.reshape(4 * rows, width).astype(jnp.float32)
        return flat.T.astype(jnp.bfloat16)

    for p in halves:
        QT[p] = turned(QP[p])
    for i in range(2):
        arrived(X.at[1 - c, i], x_rcv.at[1 - c, i, 0])

    def product(left, right):
        return lax.dot_general(
            left.reshape(2 * width, 4 * rows), right.reshape(4 * rows, tile),
            (((1,), (0,)), ((), ())), preferred_element_type=jnp.float32,
        )

    def span(t):
        return pl.ds(pl.multiple_of(t * tile, tile), tile)

    def near(t):
        return product(QT[...], X[:, :, :, span(t)])

    def keep(t, value):
        PROD[t] = value.reshape(2, 2, 2, refs, tile)

    def own(t, d):
        return PROD[t, d // 2, :, d % 2]

    def f32(value):
        return value.astype(jnp.float32)

    @pl.when(is_end)
    def _():
        def send(t, carry):
            keep(t, near(t))
            for k, d in enumerate((far_inner, far_end, inner)):
                TE[k, t - TF] = own(t, d).astype(jnp.bfloat16)
                end_copy(k, t - TF).start()
            return carry

        def pass_on(t, carry):
            arrived(RI.at[t], i_rcv.at[t])
            out_x(RI, t).start()
            out_own(RI, t).start()
            return carry

        def finish(t, carry):
            arrived(RI.at[t], i_rcv.at[t])
            O[t] = (own(t, end) + f32(RI[t])).astype(jnp.bfloat16)
            out_x(O, t).start()
            out_own(O, t).start()
            return carry

        lax.fori_loop(TF, T, send, 0)
        lax.fori_loop(0, TF, pass_on, 0)
        lax.fori_loop(TF, T, finish, 0)

    @pl.when(is_inner)
    def _():
        for i in range(2):
            arrived(XF.at[c, i], xf_rcv.at[c, i])
            far_core(i).start()
        for i in range(2):
            arrived(XF.at[1 - c, i], xf_rcv.at[1 - c, i])
        for i in range(2):
            for j in range(2):
                arrived(QF.at[:, i, j], qf_rcv.at[i, j])
        for p in halves:
            QTF[p] = turned(QF[p])

        def outward(t, both):
            total = near(t)
            if both:
                total = total + product(QTF[...], XF[:, :, :, span(t)])
            keep(t, total)
            for k, d in enumerate((far_inner, far_end)):
                value = own(t, d)
                if not both:
                    arrived(RE.at[k, t - TF], e_rcv.at[k, t - TF])
                    value = value + f32(RE[k, t - TF])
                TM[k, t] = value.astype(jnp.bfloat16)
                middle_copy(k, t).start()

        def inward(t):
            arrived(RM.at[1, t], m_rcv.at[1, t])
            TI[t] = (own(t, end) + f32(RM[1, t])).astype(jnp.bfloat16)
            inner_copy(t).start()
            arrived(RM.at[0, t], m_rcv.at[0, t])

            @pl.when(t < TF)
            def _():
                O[t] = (own(t, inner) + f32(RM[0, t])).astype(jnp.bfloat16)

            @pl.when(t >= TF)
            def _():
                arrived(RE.at[2, t - TF], e_rcv.at[2, t - TF])
                O[t] = (own(t, inner) + f32(RM[0, t]) + f32(RE[2, t - TF])).astype(jnp.bfloat16)

            out_x(O, t).start()
            out_own(O, t).start()

        def first(t, carry):
            outward(t, True)

            @pl.when(t >= 2)
            def _():
                inward(t - 2)

            return carry

        def second(t, carry):
            outward(t, False)
            inward(t - 2)
            return carry

        def last(t, carry):
            inward(t)
            return carry

        lax.fori_loop(0, TF, first, 0)
        lax.fori_loop(TF, T, second, 0)
        lax.fori_loop(T - 2, T, last, 0)

    for h in halves:
        proj_x(h).wait_send()
        image_x(h).wait_send()
    own_image_core().wait_send()
    other_image_core().wait_send()
    for k in range(3):
        post_copy(k).wait_send()

    def sent(src, carry):
        score_copy(src).wait_send()
        for g, h in pieces:
            piece = part(src, g, h)
            to_core(piece, src, g, h).wait_send()

            @pl.when((src == b) | (is_inner & (src != buddy)))
            def _():
                to_buddy(piece, src, g, h).wait_send()

            @pl.when(is_inner & ((src == b) | (src == buddy)))
            def _():
                to_across(piece, src, g, h).wait_send()

        return carry

    lax.fori_loop(0, 4, sent, 0)

    @pl.when(is_end)
    def _():
        own_far().wait_send()
        other_far().wait_send()
        for i in range(2):
            for j in range(2):
                post_far(i, j).wait_send()

        def gone(t, carry):
            for k in range(3):
                end_copy(k, t).wait_send()
            return carry

        lax.fori_loop(0, T - TF, gone, 0)

    @pl.when(is_inner)
    def _():
        for i in range(2):
            far_core(i).wait_send()

        def gone(t, carry):
            for k in range(2):
                middle_copy(k, t).wait_send()
            inner_copy(t).wait_send()
            return carry

        lax.fori_loop(0, T, gone, 0)

    def done(t, carry):
        out_own(O, t).wait()
        out_x(O, t).wait_send()
        arrived(out_span(1 - x, t), o_rcv.at[t])
        return carry

    lax.fori_loop(0, T, done, 0)


def paired_halves(images, routes, projections, noise_weights):
    rows, coef = images.shape
    refs = projections.shape[1]
    H, width = coef // 2, 4 * refs
    F = H // 2
    tile = min(F, 512)
    T, TF = H // tile, F // tile
    TN = T - TF
    dma = pltpu.SemaphoreType.DMA
    bf16, f32 = jnp.bfloat16, jnp.float32
    piece = (2, refs, tile)
    sums, norm = pl.pallas_call(
        paired,
        out_shape=(
            jax.ShapeDtypeStruct((refs, coef), bf16),
            jax.ShapeDtypeStruct((rows, 128), f32),
        ),
        in_specs=[pl.BlockSpec(memory_space=pltpu.HBM)] * 4,
        out_specs=(
            pl.BlockSpec(memory_space=pl.ANY),
            pl.BlockSpec(memory_space=pltpu.VMEM),
        ),
        scratch_shapes=[
            pltpu.VMEM((2, rows), jnp.int32),
            pltpu.VMEM((H,), f32),
            pltpu.VMEM((2, 2, rows, H), bf16),
            pltpu.VMEM((2, 2, rows, F), bf16),
            pltpu.VMEM((4, 4, refs, H), bf16),
            pltpu.VMEM((4, 2, rows, width), f32),
            pltpu.VMEM((4, rows, width), f32),
            pltpu.VMEM((2, 2, 2, rows, width), bf16),
            pltpu.VMEM((2, rows, width), bf16),
            pltpu.VMEM((2, 2, 2, rows, width), bf16),
            pltpu.VMEM((2, width, 4 * rows), bf16),
            pltpu.VMEM((2, width, 4 * rows), bf16),
            pltpu.VMEM((T, 2, 2, 2, refs, tile), f32),
            pltpu.VMEM((3, TN) + piece, bf16),
            pltpu.VMEM((3, TN) + piece, bf16),
            pltpu.VMEM((2, T) + piece, bf16),
            pltpu.VMEM((2, T) + piece, bf16),
            pltpu.VMEM((T,) + piece, bf16),
            pltpu.VMEM((T,) + piece, bf16),
            pltpu.VMEM((T,) + piece, bf16),
            dma((4,)), dma((2,)), dma((4, 4, 2)), dma((4, 4, 2)), dma((4, 4, 2)), dma((4, 4, 2)),
            dma((2,)), dma((2,)), dma((2, 2, 2)), dma((2,)), dma((2,)), dma((2, 2)),
            dma((4,)), dma((4,)), dma((3,)), dma((2, 2)), dma((2, 2)), dma((2, 2)),
            dma((3, TN)), dma((3, TN)), dma((2, T)), dma((2, T)), dma((T,)), dma((T,)),
            dma((T,)), dma((T,)), dma((T,)),
        ],
        compiler_params=pltpu.CompilerParams(
            collective_id=0, has_side_effects=True, vmem_limit_bytes=64 * 1024 * 1024 - 65536
        ),
        cost_estimate=pl.CostEstimate(
            flops=4 * 4 * rows * 4 * width * H // 2, bytes_accessed=4 * rows * coef, transcendentals=0
        ),
    )(images, routes.T, projections[0], noise_weights)
    return (sums.astype(f32)[None], norm[:, 0])


def solution(mesh):
    sizes = dict(mesh.shape)
    direct = sizes["sub"] == 1 and sizes["reader"] == 4 and sizes["blk"] == 4
    return jax.shard_map(
        paired_halves if direct else routed,
        mesh=mesh,
        in_specs=(
            P(("parts", "blk", "reader"), "sub"),
            P(("parts", "blk", "reader"), None),
            P(("parts", "reader"), "blk", "sub"),
            P(("parts", "sub")),
        ),
        out_specs=(P(("parts", "reader"), "blk", "sub"), P(("parts", "blk", "reader"))),
        check_vma=False,
    )
```

```python
from functools import partial

import jax
import jax.numpy as jnp
from jax import lax
from jax.experimental import pallas as pl
from jax.experimental.pallas import tpu as pltpu
from jax.sharding import PartitionSpec as P

MESH = pl.DeviceIdType.MESH


def from_behind(block, axis, distance):
    devices = range(lax.axis_size(axis))
    route = [((i - distance) % len(devices), i) for i in devices]
    return lax.ppermute(block, axis, route)


def slot_positions(route_block):
    flat = route_block.reshape(-1)
    order = jnp.arange(flat.shape[0], dtype=jnp.int32)
    earlier = (order[None, :] < order[:, None]) & (flat[None, :] == flat[:, None])
    return jnp.sum(earlier.astype(jnp.int32), axis=1).reshape(route_block.shape)


def combine_stats(row_peaks, row_totals):
    highest = jnp.max(row_peaks, axis=-1)
    spread = row_totals * jnp.exp(row_peaks - highest[..., None])
    return highest + jnp.log(jnp.sum(spread, axis=-1))


def routed(images, routes, projections, noise_weights):
    groups = lax.axis_size("reader")
    cycle_size = lax.axis_size("blk")
    my_group = lax.axis_index("reader")
    my_member = lax.axis_index("blk")
    per_device, top_count = routes.shape
    half_width = images.shape[1]
    capacity = min(per_device, 2 * per_device * top_count // groups)
    slot_count = groups * capacity
    ref_count = projections.shape[1]
    all_refs = ref_count * cycle_size
    anchor = jnp.zeros((), jnp.int32)
    own_index = slot_positions(routes)
    own_target = routes * capacity + own_index
    sources = jnp.broadcast_to(jnp.arange(per_device, dtype=jnp.int32)[:, None], routes.shape)
    picker = (
        jnp.full((slot_count,), per_device, jnp.int32)
        .at[own_target.reshape(-1)]
        .set(sources.reshape(-1))
    )
    padded = jnp.concatenate([images, jnp.zeros((1, half_width), images.dtype)], axis=0)
    outgoing = padded[picker].reshape(groups, capacity, half_width)
    received = lax.all_to_all(outgoing, "reader", split_axis=0, concat_axis=0, tiled=True).reshape(
        slot_count, half_width
    )
    every_route = lax.all_gather(routes, "reader", axis=0, tiled=True).reshape(
        groups, per_device, top_count
    )
    every_index = jax.vmap(slot_positions)(every_route)
    senders = jnp.arange(groups, dtype=jnp.int32)[:, None, None]
    landing = jnp.where(every_route == my_group, senders * capacity + every_index, slot_count)
    live_slot = jnp.zeros((slot_count,), jnp.int32).at[landing.reshape(-1)].set(1, mode="drop") > 0

    def score_block(ref_block):
        scaled = ref_block.astype(jnp.float32) * noise_weights[None, :]
        weighted = scaled.astype(jnp.bfloat16)
        penalty = 0.5 * jnp.sum(scaled * ref_block.astype(jnp.float32), axis=1)
        partial_scores = lax.dot_general(
            weighted, received, (((1,), (1,)), ((), ())), preferred_element_type=jnp.float32
        )
        return partial_scores - penalty[:, None]

    def cycle_turn(rotation, carry):
        ref_block, score_table = carry
        position = (my_member - rotation) % cycle_size
        score_table = lax.dynamic_update_slice(
            score_table, score_block(ref_block)[None], (position, anchor, anchor)
        )
        ref_block = from_behind(ref_block, "blk", 1)
        return (ref_block, score_table)

    empty_table = jnp.zeros((cycle_size, ref_count, slot_count), jnp.float32)
    ref_block, score_table = lax.fori_loop(
        0, cycle_size - 1, cycle_turn, (projections[0], empty_table)
    )
    position = (my_member + 1) % cycle_size
    score_table = lax.dynamic_update_slice(
        score_table, score_block(ref_block)[None], (position, anchor, anchor)
    )
    score_table = lax.psum(score_table, "sub")
    scores = score_table.reshape(all_refs, slot_count)
    row_peak = jnp.max(scores, axis=0)
    row_total = jnp.sum(jnp.exp(scores - row_peak[None, :]), axis=0)
    back_peak, back_total = (
        lax.all_to_all(
            row_peak.reshape(groups, capacity), "reader", split_axis=0, concat_axis=0, tiled=True
        ),
        lax.all_to_all(
            row_total.reshape(groups, capacity), "reader", split_axis=0, concat_axis=0, tiled=True
        ),
    )
    normalizer = combine_stats(
        back_peak.reshape(-1)[own_target], back_total.reshape(-1)[own_target]
    )
    outgoing_norm = (
        jnp.zeros((slot_count,), jnp.float32)
        .at[own_target.reshape(-1)]
        .set(jnp.repeat(normalizer, top_count))
    )
    slot_norm = lax.all_to_all(
        outgoing_norm.reshape(groups, capacity), "reader", split_axis=0, concat_axis=0, tiled=True
    ).reshape(slot_count)
    exponent = jnp.where(live_slot[None, :], scores - slot_norm[None, :], -jnp.inf)
    posterior = jnp.exp(exponent).astype(jnp.bfloat16)
    summed = lax.psum_scatter(
        jnp.dot(posterior, received, preferred_element_type=jnp.float32).astype(jnp.bfloat16),
        "blk",
        scatter_dimension=0,
        tiled=True,
    ).astype(jnp.float32)
    return (summed[None], normalizer)


def paired(
    images, routes_in, proj, noise_in,
    out, norm,
    routes, noise, X, XF, PR, S, SR, SF, FR, QP, QO, QF, QT, QTF, PROD, TE, RE, TM, RM, TI, RI, O,
    loc, px_snd, pb_snd, pm_snd, pc_snd, p_rcv, xx_snd, xc_snd, x_rcv, xf_snd, xfc_snd, xf_rcv,
    s_snd, s_rcv, f_snd, f_rcv, q_snd, q_rcv, qf_snd, qf_rcv, e_snd, e_rcv, m_snd, m_rcv, i_snd, i_rcv,
    own_snd, o_snd, o_rcv,
):
    r = lax.axis_index("reader")
    b = lax.axis_index("blk")
    x, c = r // 2, r % 2
    rx, rc = (r + 2) % 4, x * 2 + 1 - c
    rd = (rc + 2) % 4
    side = b // 2
    inner, end = 1 + side, 3 * side
    far_inner, far_end = 2 - side, 3 - 3 * side
    buddy, across = inner + end - b, 3 - b
    is_end = b == end
    is_inner = b == inner
    rows = images.shape[0]
    refs = proj.shape[0]
    H = X.shape[4 - 1]
    F = H // 2
    T, tile = O.shape[0], O.shape[3]
    TF = F // tile
    cuts = score_cuts(T)
    low, mid = (n * tile for n in cuts)
    width = 4 * refs
    halves = (0, 1)
    whole = ((0, mid), (mid, H - mid))
    short = ((low, mid - low), (mid, H - mid))
    strips = ((0, low), (low, H - low))
    far_strips = ((0, low), (low, F - low))

    def remote(src, dst, snd, rcv, **where):
        return pltpu.make_async_remote_copy(
            src_ref=src, dst_ref=dst, send_sem=snd, recv_sem=rcv,
            device_id=where, device_id_type=MESH,
        )

    def arrived(dst, sem):
        remote(dst, dst, sem, sem, reader=rx).wait_recv()

    def columns(i, cut):
        return pl.ds(pl.multiple_of(i * H + cut[0], tile), cut[1])

    def part(src, g, cut):
        return PR.at[src, g, :, pl.ds(*cut)]

    def own_piece(h):
        return proj.at[:, columns(x, whole[h])]

    def proj_x(h):
        return remote(
            proj.at[:, columns(1 - x, whole[h])], part(b, r, whole[h]), px_snd.at[h], p_rcv.at[b, r, h], reader=rx
        )

    def to_core(piece, src, g, h, cut):
        return remote(piece, part(src, g, cut), pc_snd.at[src, g, h], p_rcv.at[src, g, h], reader=rc)

    def to_buddy(piece, src, g, h, cut):
        return remote(piece, part(src, g, cut), pb_snd.at[src, g, h], p_rcv.at[src, g, h], blk=buddy)

    def to_across(piece, src, g, h):
        return remote(piece, part(src, g, whole[h]), pm_snd.at[src, g, h], p_rcv.at[src, g, h], blk=across)

    def image_x(h):
        return remote(
            images.at[:, columns(1 - x, strips[h])], X.at[c, x, :, pl.ds(*strips[h])],
            xx_snd.at[h], x_rcv.at[c, x, h], reader=rx,
        )

    def own_image_core():
        return remote(
            images.at[:, pl.ds(pl.multiple_of(x * H, H), H)], X.at[c, x],
            xc_snd.at[0], x_rcv.at[c, x, 0], reader=rc,
        )

    def other_image_core():
        return remote(X.at[c, 1 - x], X.at[c, 1 - x], xc_snd.at[1], x_rcv.at[c, 1 - x, 0], reader=rc)

    def own_far(h):
        return remote(
            images.at[:, columns(x, far_strips[h])], XF.at[c, x, :, pl.ds(*far_strips[h])],
            xf_snd.at[0, h], xf_rcv.at[c, x, h], blk=buddy,
        )

    def other_far(h):
        return remote(
            X.at[c, 1 - x, :, pl.ds(*far_strips[h])], XF.at[c, 1 - x, :, pl.ds(*far_strips[h])],
            xf_snd.at[1, h], xf_rcv.at[c, 1 - x, h], blk=buddy,
        )

    def far_core(i):
        return remote(XF.at[c, i], XF.at[c, i], xfc_snd.at[i], xf_rcv.at[c, i, 0], reader=rc)

    def score_copy(src):
        return remote(S.at[src, 1 - x], SR.at[src], s_snd.at[src], s_rcv.at[src], reader=rx)

    def far_score(k, i):
        if i == 0:
            return remote(SF.at[k, x], FR.at[k, x], f_snd.at[k, 0], f_rcv.at[k, x], blk=buddy)
        return remote(SF.at[k, 1 - x], FR.at[k, x], f_snd.at[k, 1], f_rcv.at[k, x], blk=buddy, reader=rx)

    def post_copy(k):
        source, to = ((QP.at[:, c, x], rx), (QO, rc), (QO, rd))[k]
        return remote(source, QP.at[:, c, x], q_snd.at[k], q_rcv.at[c, x], reader=to)

    def post_far(i, j):
        return remote(QP.at[:, i, j], QF.at[:, i, j], qf_snd.at[i, j], qf_rcv.at[i, j], blk=buddy)

    def end_copy(k, t):
        return remote(TE.at[k, t], RE.at[k, t], e_snd.at[k, t], e_rcv.at[k, t], blk=buddy)

    def middle_copy(k, t):
        return remote(TM.at[k, t], RM.at[k, t], m_snd.at[k, t], m_rcv.at[k, t], blk=across)

    def inner_copy(t):
        return remote(TI.at[t], RI.at[t], i_snd.at[t], i_rcv.at[t], blk=buddy)

    def out_span(i, t):
        return out.at[:, pl.ds(pl.multiple_of(i * H + t * tile, tile), tile)]

    def out_x(src, t):
        return remote(src.at[t, 1 - x], out_span(x, t), o_snd.at[t], o_rcv.at[t], reader=rx)

    def out_own(src, t):
        return pltpu.make_async_copy(src.at[t, x], out_span(x, t), own_snd.at[t])

    own_proj = pltpu.make_async_copy(proj.at[:, pl.ds(pl.multiple_of(x * H, H), H)], PR.at[b, r], loc.at[0])
    own_image = pltpu.make_async_copy(
        images.at[:, pl.ds(pl.multiple_of(x * H, H), H)], X.at[c, x], loc.at[1]
    )
    noise_copy = pltpu.make_async_copy(
        noise_in.at[pl.ds(pl.multiple_of(x * H, H), H)], noise, loc.at[2]
    )
    routes_copy = pltpu.make_async_copy(routes_in, routes, loc.at[3])

    barrier = pltpu.get_barrier_semaphore()
    for k in (rx, rc, rd):
        pl.semaphore_signal(barrier, inc=1, device_id={"reader": k}, device_id_type=MESH)
    pl.semaphore_signal(barrier, inc=1, device_id={"blk": buddy}, device_id_type=MESH)
    pl.semaphore_signal(barrier, inc=1, device_id={"blk": buddy, "reader": rx}, device_id_type=MESH)

    @pl.when(is_inner)
    def _():
        pl.semaphore_signal(barrier, inc=1, device_id={"blk": across}, device_id_type=MESH)

    own_proj.start()
    own_image.start()
    noise_copy.start()
    routes_copy.start()
    pl.semaphore_wait(barrier, 5 + is_inner.astype(jnp.int32))

    for h in halves:
        proj_x(h).start()
        to_buddy(own_piece(h), b, r, h, whole[h]).start()

        @pl.when(is_inner)
        def _():
            to_across(own_piece(h), b, r, h).start()

    for h in halves:
        to_core(own_piece(h), b, r, h, whole[h]).start()
    own_image_core().start()
    for h in halves:
        piece = part(b, rx, whole[h])
        arrived(piece, p_rcv.at[b, rx, h])
        to_buddy(piece, b, rx, h, whole[h]).start()

        @pl.when(is_inner)
        def _():
            to_across(piece, b, rx, h).start()

        image_x(h).start()
        to_core(piece, b, rx, h, whole[h]).start()

    pieces = ((r, 0), (r, 1), (rx, 0), (rx, 1))

    def other_image(h):
        arrived(X.at[c, 1 - x, :, pl.ds(*strips[h])], x_rcv.at[c, 1 - x, h])

    def hand_over(src, g, h, cut):
        piece = part(src, g, cut)
        arrived(piece, p_rcv.at[src, g, h])
        to_core(piece, src, g, h, cut).start()

    @pl.when(is_end)
    def _():
        own_far(0).start()
        for g, h in pieces:
            hand_over(buddy, g, h, whole[h])
        other_image(0)
        other_far(0).start()
        own_far(1).start()
        for g, h in pieces:
            hand_over(far_inner, g, h, short[h])
        other_image(1)
        other_far(1).start()

    @pl.when(is_inner)
    def _():
        for g, h in pieces:
            hand_over(buddy, g, h, whole[h])
            to_across(part(buddy, g, whole[h]), buddy, g, h).start()
            hand_over(far_inner, g, h, whole[h])
            to_buddy(part(far_inner, g, short[h]), far_inner, g, h, short[h]).start()
        for g, h in pieces:
            hand_over(far_end, g, h, whole[h])
            to_buddy(part(far_end, g, short[h]), far_end, g, h, short[h]).start()
        for h in halves:
            other_image(h)

    other_image_core().start()
    own_proj.wait()
    own_image.wait()
    noise_copy.wait()
    routes_copy.wait()

    def scores_of(block, src, tiles):
        scores = jnp.zeros((2 * rows, width), jnp.float32)
        penalty = jnp.zeros((width, 128), jnp.float32)
        for t in tiles:
            cut = pl.ds(t * tile, tile)
            refs_f = PR[src, :, :, cut].reshape(width, tile).astype(jnp.float32)
            scaled = refs_f * noise[cut][None, :]
            scores = scores + lax.dot_general(
                block[c, :, :, cut].reshape(2 * rows, tile), scaled.astype(jnp.bfloat16),
                (((1,), (1,)), ((), ())), preferred_element_type=jnp.float32,
            )
            squares = scaled * refs_f
            for lane in range(0, tile, 128):
                penalty = penalty + squares[:, lane : lane + 128]
        penalty_row = lax.dot_general(
            jnp.full((8, 128), 0.5, jnp.float32), penalty,
            (((1,), (1,)), ((), ())), preferred_element_type=jnp.float32,
            precision=lax.Precision.HIGHEST,
        )
        return (scores - penalty_row[0:1]).reshape(2, rows, width)

    def from_core(src, h, cut):
        for g in (rc, rd):
            arrived(part(src, g, cut), p_rcv.at[src, g, h])

    @pl.when(is_inner)
    def _():
        for i in (x, 1 - x):
            arrived(XF.at[c, i, :, pl.ds(*far_strips[0])], xf_rcv.at[c, i, 0])

        def far_source(k, carry):
            src = jnp.where(k == 0, far_inner, far_end)
            for h in halves:
                from_core(src, h, whole[h])
            SF[k] = scores_of(XF, src, range(cuts[0]))
            for i in (1, 0):
                far_score(k, i).start()
            return carry

        lax.fori_loop(0, 2, far_source, 0)

    def score_source(i, carry):
        src = jnp.where(i == 0, b, jnp.where(i == 1, buddy, jnp.where(i == 2, far_inner, far_end)))

        @pl.when(i < 2)
        def _():
            for h in halves:
                from_core(src, h, whole[h])

        @pl.when((i < 2) | is_inner)
        def _():
            S[src] = scores_of(X, src, range(cuts[0]))

        @pl.when((i >= 2) & is_end)
        def _():
            @pl.when(i == 3)
            def _():
                for g, h in pieces[:3]:
                    hand_over(src, g, h, short[h])

            from_core(src, 0, short[0])
            S[src] = jnp.zeros((2, rows, width), jnp.float32)

        S[src] = S[src] + scores_of(X, src, range(cuts[0], cuts[1]))

        @pl.when((i >= 2) & is_end)
        def _():
            @pl.when(i == 3)
            def _():
                for g, h in pieces[3:]:
                    hand_over(src, g, h, short[h])

            from_core(src, 1, short[1])

        S[src] = S[src] + scores_of(X, src, range(cuts[1], T))
        score_copy(src).start()
        return carry

    lax.fori_loop(0, 4, score_source, 0)

    @pl.when(is_end)
    def _():
        for k, src in enumerate((far_inner, far_end)):
            for i in range(2):
                arrived(FR.at[k, i], f_rcv.at[k, i])
            S[src, x] = S[src, x] + FR[k, 0] + FR[k, 1]

    lane = lax.broadcasted_iota(jnp.int32, (rows, width), 1)
    lane_group = lane // refs
    diagonal = lax.broadcasted_iota(jnp.int32, (rows, rows), 0) == lax.broadcasted_iota(
        jnp.int32, (rows, rows), 1
    )

    def column(row):
        return jnp.sum(jnp.where(diagonal, row, 0.0), axis=1, keepdims=True).astype(jnp.int32)

    names = routes[...].astype(jnp.float32)
    named = (column(names[0:1]) == lane_group) | (column(names[1:2]) == lane_group)
    chunks = []
    for d in range(4):
        arrived(SR.at[d], s_rcv.at[d])
        chunks.append(jnp.where(named, S[d, x] + SR[d], -jnp.inf))
    highest = jnp.maximum(jnp.maximum(chunks[0], chunks[1]), jnp.maximum(chunks[2], chunks[3]))
    highest = jnp.max(highest, axis=1, keepdims=True)
    spread = [jnp.exp(chunk - highest) for chunk in chunks]
    total = jnp.sum((spread[0] + spread[1]) + (spread[2] + spread[3]), axis=1, keepdims=True)
    normalizer = highest + jnp.log(total)
    norm[...] = jnp.sum(jnp.where(diagonal, normalizer, 0.0), axis=0, keepdims=True)
    even = lane_group % 2 == 0
    for p in halves:
        low = jnp.exp(chunks[2 * p] - normalizer)
        high = jnp.exp(chunks[2 * p + 1] - normalizer)
        zero = jnp.where(even, low, pltpu.roll(high, refs, 1))
        one = jnp.where(even, pltpu.roll(low, width - refs, 1), high)
        QP[p, c, x] = jnp.where(c == 0, zero, one).astype(jnp.bfloat16)
        QO[p] = jnp.where(c == 0, one, zero).astype(jnp.bfloat16)
    for k in (2, 0, 1):
        post_copy(k).start()

    @pl.when(is_end)
    def _():
        post_far(c, x).start()

    for h in halves:
        proj_x(h).wait_send()
        image_x(h).wait_send()
    own_image_core().wait_send()
    other_image_core().wait_send()

    def sent(src, carry):
        score_copy(src).wait_send()
        near_source = (src == b) | (src == buddy)
        for g, h in pieces:
            @pl.when(near_source | is_inner)
            def _():
                piece = part(src, g, whole[h])
                to_core(piece, src, g, h, whole[h]).wait_send()

            @pl.when(src == b)
            def _():
                piece = part(src, g, whole[h])
                to_buddy(piece, src, g, h, whole[h]).wait_send()

            @pl.when((src != b) & (src != buddy))
            def _():
                piece = part(src, g, short[h])

                @pl.when(is_inner)
                def _():
                    to_buddy(piece, src, g, h, short[h]).wait_send()

                @pl.when(is_end)
                def _():
                    to_core(piece, src, g, h, short[h]).wait_send()

            @pl.when(is_inner & near_source)
            def _():
                to_across(part(src, g, whole[h]), src, g, h).wait_send()

        return carry

    lax.fori_loop(0, 4, sent, 0)
    for i, j in ((1 - c, x), (c, 1 - x), (1 - c, 1 - x)):
        arrived(QP.at[:, i, j], q_rcv.at[i, j])

        @pl.when(is_end)
        def _():
            post_far(i, j).start()

    def turned(block):
        flat = block.reshape(4 * rows, width).astype(jnp.float32)
        return flat.T.astype(jnp.bfloat16)

    for p in halves:
        QT[p] = turned(QP[p])
    for i in range(2):
        arrived(X.at[1 - c, i], x_rcv.at[1 - c, i, 0])

    def product(left, right):
        return lax.dot_general(
            left.reshape(2 * width, 4 * rows), right.reshape(4 * rows, tile),
            (((1,), (0,)), ((), ())), preferred_element_type=jnp.float32,
        )

    def span(t):
        return pl.ds(pl.multiple_of(t * tile, tile), tile)

    def near(t):
        return product(QT[...], X[:, :, :, span(t)])

    def keep(t, value):
        PROD[t] = value.reshape(2, 2, 2, refs, tile)

    def own(t, d):
        return PROD[t, d // 2, :, d % 2]

    def f32(value):
        return value.astype(jnp.float32)

    @pl.when(is_end)
    def _():
        def send(t, carry):
            keep(t, near(t))
            for k, d in ((1, far_end), (0, far_inner), (2, inner)):
                TE[k, t - TF] = own(t, d).astype(jnp.bfloat16)
                end_copy(k, t - TF).start()
            return carry

        def pass_on(t, carry):
            arrived(RI.at[t], i_rcv.at[t])
            out_x(RI, t).start()
            out_own(RI, t).start()
            return carry

        def finish(t, carry):
            arrived(RI.at[t], i_rcv.at[t])
            O[t] = (own(t, end) + f32(RI[t])).astype(jnp.bfloat16)
            out_x(O, t).start()
            out_own(O, t).start()
            return carry

        lax.fori_loop(TF, T, send, 0)
        lax.fori_loop(0, TF, pass_on, 0)
        lax.fori_loop(TF, T, finish, 0)

    @pl.when(is_inner)
    def _():
        for i in range(2):
            arrived(XF.at[c, i, :, pl.ds(*far_strips[1])], xf_rcv.at[c, i, 1])
            far_core(i).start()
        for i in range(2):
            arrived(XF.at[1 - c, i], xf_rcv.at[1 - c, i, 0])
        for i in range(2):
            for j in range(2):
                arrived(QF.at[:, i, j], qf_rcv.at[i, j])
        for p in halves:
            QTF[p] = turned(QF[p])

        def outward(k, d, t):
            @pl.when(t < TF)
            def _():
                TM[k, t] = own(t, d).astype(jnp.bfloat16)

            @pl.when(t >= TF)
            def _():
                arrived(RE.at[k, t - TF], e_rcv.at[k, t - TF])
                TM[k, t] = (own(t, d) + f32(RE[k, t - TF])).astype(jnp.bfloat16)

            middle_copy(k, t).start()

        def turn(t, carry):
            @pl.when(t < TF)
            def _():
                keep(t, near(t) + product(QTF[...], XF[:, :, :, span(t)]))

            @pl.when((t >= TF) & (t < T))
            def _():
                keep(t, near(t))

            @pl.when(t < T)
            def _():
                outward(1, far_end, t)

            @pl.when((t >= 2) & (t < T + 2))
            def _():
                outward(0, far_inner, t - 2)
                n = t - 2
                arrived(RM.at[1, n], m_rcv.at[1, n])
                TI[n] = (own(n, end) + f32(RM[1, n])).astype(jnp.bfloat16)
                inner_copy(n).start()

            @pl.when(t >= 4)
            def _():
                n = t - 4
                arrived(RM.at[0, n], m_rcv.at[0, n])
                total = own(n, inner) + f32(RM[0, n])

                @pl.when(n < TF)
                def _():
                    O[n] = total.astype(jnp.bfloat16)

                @pl.when(n >= TF)
                def _():
                    arrived(RE.at[2, n - TF], e_rcv.at[2, n - TF])
                    O[n] = (total + f32(RE[2, n - TF])).astype(jnp.bfloat16)

                out_x(O, n).start()
                out_own(O, n).start()

            return carry

        lax.fori_loop(0, T + 4, turn, 0)

    for k in range(3):
        post_copy(k).wait_send()

    @pl.when(is_end)
    def _():
        for h in halves:
            own_far(h).wait_send()
            other_far(h).wait_send()
        for i in range(2):
            for j in range(2):
                post_far(i, j).wait_send()

        def gone(t, carry):
            for k in range(3):
                end_copy(k, t).wait_send()
            return carry

        lax.fori_loop(0, T - TF, gone, 0)

    @pl.when(is_inner)
    def _():
        for i in range(2):
            far_core(i).wait_send()
            for k in range(2):
                far_score(k, i).wait_send()

        def gone(t, carry):
            for k in range(2):
                middle_copy(k, t).wait_send()
            inner_copy(t).wait_send()
            return carry

        lax.fori_loop(0, T, gone, 0)

    def done(t, carry):
        out_own(O, t).wait()
        out_x(O, t).wait_send()
        arrived(out_span(1 - x, t), o_rcv.at[t])
        return carry

    lax.fori_loop(0, T, done, 0)


def score_cuts(T):
    low = max(1, 3 * T // 8)
    return low, max(low + 1, 3 * T // 4)


def hand_out(sums_in, norm_in, sums_out, norm_out):
    sums_out[...] = sums_in[...].astype(jnp.float32)
    norm_out[...] = norm_in[...]


def paired_halves(images, routes, projections, noise_weights):
    rows, coef = images.shape
    refs = projections.shape[1]
    H, width = coef // 2, 4 * refs
    F = H // 2
    tile = min(F, 512)
    T, TF = H // tile, F // tile
    TN = T - TF
    dma = pltpu.SemaphoreType.DMA
    bf16, f32 = jnp.bfloat16, jnp.float32
    piece = (2, refs, tile)
    sums, norm = pl.pallas_call(
        paired,
        out_shape=(
            jax.ShapeDtypeStruct((refs, coef), bf16),
            jax.ShapeDtypeStruct((1, rows), f32),
        ),
        in_specs=[pl.BlockSpec(memory_space=pltpu.HBM)] * 4,
        out_specs=(
            pl.BlockSpec(memory_space=pl.ANY),
            pl.BlockSpec(memory_space=pltpu.VMEM),
        ),
        scratch_shapes=[
            pltpu.VMEM((2, rows), jnp.int32),
            pltpu.VMEM((H,), f32),
            pltpu.VMEM((2, 2, rows, H), bf16),
            pltpu.VMEM((2, 2, rows, F), bf16),
            pltpu.VMEM((4, 4, refs, H), bf16),
            pltpu.VMEM((4, 2, rows, width), f32),
            pltpu.VMEM((4, rows, width), f32),
            pltpu.VMEM((2, 2, rows, width), f32),
            pltpu.VMEM((2, 2, rows, width), f32),
            pltpu.VMEM((2, 2, 2, rows, width), bf16),
            pltpu.VMEM((2, rows, width), bf16),
            pltpu.VMEM((2, 2, 2, rows, width), bf16),
            pltpu.VMEM((2, width, 4 * rows), bf16),
            pltpu.VMEM((2, width, 4 * rows), bf16),
            pltpu.VMEM((T, 2, 2, 2, refs, tile), f32),
            pltpu.VMEM((3, TN) + piece, bf16),
            pltpu.VMEM((3, TN) + piece, bf16),
            pltpu.VMEM((2, T) + piece, bf16),
            pltpu.VMEM((2, T) + piece, bf16),
            pltpu.VMEM((T,) + piece, bf16),
            pltpu.VMEM((T,) + piece, bf16),
            pltpu.VMEM((T,) + piece, bf16),
            dma((4,)), dma((2,)), dma((4, 4, 2)), dma((4, 4, 2)), dma((4, 4, 2)), dma((4, 4, 2)),
            dma((2,)), dma((2,)), dma((2, 2, 2)), dma((2, 2)), dma((2,)), dma((2, 2, 2)),
            dma((4,)), dma((4,)), dma((2, 2)), dma((2, 2)), dma((3,)), dma((2, 2)), dma((2, 2)), dma((2, 2)),
            dma((3, TN)), dma((3, TN)), dma((2, T)), dma((2, T)), dma((T,)), dma((T,)),
            dma((T,)), dma((T,)), dma((T,)),
        ],
        compiler_params=pltpu.CompilerParams(
            collective_id=0, has_side_effects=True, vmem_limit_bytes=64 * 1024 * 1024 - 65536
        ),
        cost_estimate=pl.CostEstimate(
            flops=4 * 4 * rows * 4 * width * H // 2, bytes_accessed=4 * rows * coef, transcendentals=0
        ),
    )(images, routes.T, projections[0], noise_weights)
    block = 2048 if coef % 2048 == 0 else coef
    sums, norm = pl.pallas_call(
        hand_out,
        grid=(coef // block,),
        out_shape=(jax.ShapeDtypeStruct((refs, coef), f32), jax.ShapeDtypeStruct((1, rows), f32)),
        in_specs=[pl.BlockSpec((refs, block), lambda i: (0, i)), pl.BlockSpec((1, rows), lambda i: (0, 0))],
        out_specs=(pl.BlockSpec((refs, block), lambda i: (0, i)), pl.BlockSpec((1, rows), lambda i: (0, 0))),
    )(sums, norm)
    return (sums[None], norm[0])


def solution(mesh):
    sizes = dict(mesh.shape)
    direct = sizes["sub"] == 1 and sizes["reader"] == 4 and sizes["blk"] == 4
    return jax.shard_map(
        paired_halves if direct else routed,
        mesh=mesh,
        in_specs=(
            P(("parts", "blk", "reader"), "sub"),
            P(("parts", "blk", "reader"), None),
            P(("parts", "reader"), "blk", "sub"),
            P(("parts", "sub")),
        ),
        out_specs=(P(("parts", "reader"), "blk", "sub"), P(("parts", "blk", "reader"))),
        check_vma=False,
    )
```

```python
from functools import partial

import jax
import jax.numpy as jnp
from jax import lax
from jax.experimental import pallas as pl
from jax.experimental.pallas import tpu as pltpu
from jax.sharding import PartitionSpec as P

MESH = pl.DeviceIdType.MESH


def from_behind(block, axis, distance):
    devices = range(lax.axis_size(axis))
    route = [((i - distance) % len(devices), i) for i in devices]
    return lax.ppermute(block, axis, route)


def slot_positions(route_block):
    flat = route_block.reshape(-1)
    order = jnp.arange(flat.shape[0], dtype=jnp.int32)
    earlier = (order[None, :] < order[:, None]) & (flat[None, :] == flat[:, None])
    return jnp.sum(earlier.astype(jnp.int32), axis=1).reshape(route_block.shape)


def combine_stats(row_peaks, row_totals):
    highest = jnp.max(row_peaks, axis=-1)
    spread = row_totals * jnp.exp(row_peaks - highest[..., None])
    return highest + jnp.log(jnp.sum(spread, axis=-1))


def routed(images, routes, projections, noise_weights):
    groups = lax.axis_size("reader")
    cycle_size = lax.axis_size("blk")
    my_group = lax.axis_index("reader")
    my_member = lax.axis_index("blk")
    per_device, top_count = routes.shape
    half_width = images.shape[1]
    capacity = min(per_device, 2 * per_device * top_count // groups)
    slot_count = groups * capacity
    ref_count = projections.shape[1]
    all_refs = ref_count * cycle_size
    anchor = jnp.zeros((), jnp.int32)
    own_index = slot_positions(routes)
    own_target = routes * capacity + own_index
    sources = jnp.broadcast_to(jnp.arange(per_device, dtype=jnp.int32)[:, None], routes.shape)
    picker = (
        jnp.full((slot_count,), per_device, jnp.int32)
        .at[own_target.reshape(-1)]
        .set(sources.reshape(-1))
    )
    padded = jnp.concatenate([images, jnp.zeros((1, half_width), images.dtype)], axis=0)
    outgoing = padded[picker].reshape(groups, capacity, half_width)
    received = lax.all_to_all(outgoing, "reader", split_axis=0, concat_axis=0, tiled=True).reshape(
        slot_count, half_width
    )
    every_route = lax.all_gather(routes, "reader", axis=0, tiled=True).reshape(
        groups, per_device, top_count
    )
    every_index = jax.vmap(slot_positions)(every_route)
    senders = jnp.arange(groups, dtype=jnp.int32)[:, None, None]
    landing = jnp.where(every_route == my_group, senders * capacity + every_index, slot_count)
    live_slot = jnp.zeros((slot_count,), jnp.int32).at[landing.reshape(-1)].set(1, mode="drop") > 0

    def score_block(ref_block):
        scaled = ref_block.astype(jnp.float32) * noise_weights[None, :]
        weighted = scaled.astype(jnp.bfloat16)
        penalty = 0.5 * jnp.sum(scaled * ref_block.astype(jnp.float32), axis=1)
        partial_scores = lax.dot_general(
            weighted, received, (((1,), (1,)), ((), ())), preferred_element_type=jnp.float32
        )
        return partial_scores - penalty[:, None]

    def cycle_turn(rotation, carry):
        ref_block, score_table = carry
        position = (my_member - rotation) % cycle_size
        score_table = lax.dynamic_update_slice(
            score_table, score_block(ref_block)[None], (position, anchor, anchor)
        )
        ref_block = from_behind(ref_block, "blk", 1)
        return (ref_block, score_table)

    empty_table = jnp.zeros((cycle_size, ref_count, slot_count), jnp.float32)
    ref_block, score_table = lax.fori_loop(
        0, cycle_size - 1, cycle_turn, (projections[0], empty_table)
    )
    position = (my_member + 1) % cycle_size
    score_table = lax.dynamic_update_slice(
        score_table, score_block(ref_block)[None], (position, anchor, anchor)
    )
    score_table = lax.psum(score_table, "sub")
    scores = score_table.reshape(all_refs, slot_count)
    row_peak = jnp.max(scores, axis=0)
    row_total = jnp.sum(jnp.exp(scores - row_peak[None, :]), axis=0)
    back_peak, back_total = (
        lax.all_to_all(
            row_peak.reshape(groups, capacity), "reader", split_axis=0, concat_axis=0, tiled=True
        ),
        lax.all_to_all(
            row_total.reshape(groups, capacity), "reader", split_axis=0, concat_axis=0, tiled=True
        ),
    )
    normalizer = combine_stats(
        back_peak.reshape(-1)[own_target], back_total.reshape(-1)[own_target]
    )
    outgoing_norm = (
        jnp.zeros((slot_count,), jnp.float32)
        .at[own_target.reshape(-1)]
        .set(jnp.repeat(normalizer, top_count))
    )
    slot_norm = lax.all_to_all(
        outgoing_norm.reshape(groups, capacity), "reader", split_axis=0, concat_axis=0, tiled=True
    ).reshape(slot_count)
    exponent = jnp.where(live_slot[None, :], scores - slot_norm[None, :], -jnp.inf)
    posterior = jnp.exp(exponent).astype(jnp.bfloat16)
    summed = lax.psum_scatter(
        jnp.dot(posterior, received, preferred_element_type=jnp.float32).astype(jnp.bfloat16),
        "blk",
        scatter_dimension=0,
        tiled=True,
    ).astype(jnp.float32)
    return (summed[None], normalizer)


def paired(
    images, routes_in, proj, noise_in,
    out, norm,
    routes, noise, X, XF, PR, S, SR, SF, FR, QP, QO, QF, QT, QTF, PROD, TE, RE, TM, RM, TI, RI, O,
    loc, px_snd, pb_snd, pm_snd, pc_snd, p_rcv, xx_snd, xc_snd, x_rcv, xf_snd, xfc_snd, xf_rcv,
    s_snd, s_rcv, f_snd, f_rcv, q_snd, q_rcv, qf_snd, qf_rcv, e_snd, e_rcv, m_snd, m_rcv, i_snd, i_rcv,
    own_snd, o_snd, o_rcv,
):
    r = lax.axis_index("reader")
    b = lax.axis_index("blk")
    x, c = r // 2, r % 2
    rx, rc = (r + 2) % 4, x * 2 + 1 - c
    rd = (rc + 2) % 4
    side = b // 2
    inner, end = 1 + side, 3 * side
    far_inner, far_end = 2 - side, 3 - 3 * side
    buddy, across = inner + end - b, 3 - b
    is_end = b == end
    is_inner = b == inner
    rows = images.shape[0]
    refs = proj.shape[0]
    H = X.shape[4 - 1]
    F = H // 2
    T, tile = O.shape[0], O.shape[3]
    TF = F // tile
    cuts = score_cuts(T)
    low, mid = (n * tile for n in cuts)
    width = 4 * refs
    halves = (0, 1)
    whole = ((0, mid), (mid, H - mid))
    short = ((low, mid - low), (mid, H - mid))
    strips = ((0, low), (low, H - low))
    far_strips = ((0, low), (low, F - low))

    def remote(src, dst, snd, rcv, **where):
        return pltpu.make_async_remote_copy(
            src_ref=src, dst_ref=dst, send_sem=snd, recv_sem=rcv,
            device_id=where, device_id_type=MESH,
        )

    def arrived(dst, sem):
        remote(dst, dst, sem, sem, reader=rx).wait_recv()

    def columns(i, cut):
        return pl.ds(pl.multiple_of(i * H + cut[0], tile), cut[1])

    def part(src, g, cut):
        return PR.at[src, g, :, pl.ds(*cut)]

    def own_piece(h):
        return proj.at[:, columns(x, whole[h])]

    def proj_x(h):
        return remote(
            proj.at[:, columns(1 - x, whole[h])], part(b, r, whole[h]), px_snd.at[h], p_rcv.at[b, r, h], reader=rx
        )

    def to_core(piece, src, g, h, cut):
        return remote(piece, part(src, g, cut), pc_snd.at[src, g, h], p_rcv.at[src, g, h], reader=rc)

    def to_buddy(piece, src, g, h, cut):
        return remote(piece, part(src, g, cut), pb_snd.at[src, g, h], p_rcv.at[src, g, h], blk=buddy)

    def to_across(piece, src, g, h):
        return remote(piece, part(src, g, whole[h]), pm_snd.at[src, g, h], p_rcv.at[src, g, h], blk=across)

    def image_x(h):
        return remote(
            images.at[:, columns(1 - x, strips[h])], X.at[c, x, :, pl.ds(*strips[h])],
            xx_snd.at[h], x_rcv.at[c, x, h], reader=rx,
        )

    def own_image_core():
        return remote(
            images.at[:, pl.ds(pl.multiple_of(x * H, H), H)], X.at[c, x],
            xc_snd.at[0], x_rcv.at[c, x, 0], reader=rc,
        )

    def other_image_core():
        return remote(X.at[c, 1 - x], X.at[c, 1 - x], xc_snd.at[1], x_rcv.at[c, 1 - x, 0], reader=rc)

    def own_far(h):
        return remote(
            images.at[:, columns(x, far_strips[h])], XF.at[c, x, :, pl.ds(*far_strips[h])],
            xf_snd.at[0, h], xf_rcv.at[c, x, h], blk=buddy,
        )

    def other_far(h):
        return remote(
            X.at[c, 1 - x, :, pl.ds(*far_strips[h])], XF.at[c, 1 - x, :, pl.ds(*far_strips[h])],
            xf_snd.at[1, h], xf_rcv.at[c, 1 - x, h], blk=buddy,
        )

    def far_core(i):
        return remote(XF.at[c, i], XF.at[c, i], xfc_snd.at[i], xf_rcv.at[c, i, 0], reader=rc)

    def score_copy(src):
        return remote(S.at[src, 1 - x], SR.at[src], s_snd.at[src], s_rcv.at[src], reader=rx)

    def far_score(k, i):
        if i == 0:
            return remote(SF.at[k, x], FR.at[k, x], f_snd.at[k, 0], f_rcv.at[k, x], blk=buddy)
        return remote(SF.at[k, 1 - x], FR.at[k, x], f_snd.at[k, 1], f_rcv.at[k, x], blk=buddy, reader=rx)

    def post_copy(k, p):
        source, to = ((QP.at[p, c, x], rx), (QO.at[p], rc), (QO.at[p], rd))[k]
        return remote(source, QP.at[p, c, x], q_snd.at[k, p], q_rcv.at[c, x, p], reader=to)

    def post_far(i, j, p):
        return remote(QP.at[p, i, j], QF.at[p, i, j], qf_snd.at[i, j, p], qf_rcv.at[i, j, p], blk=buddy)

    def end_copy(k, t):
        return remote(TE.at[k, t], RE.at[k, t], e_snd.at[k, t], e_rcv.at[k, t], blk=buddy)

    def middle_copy(k, t):
        return remote(TM.at[k, t], RM.at[k, t], m_snd.at[k, t], m_rcv.at[k, t], blk=across)

    def inner_copy(t):
        return remote(TI.at[t], RI.at[t], i_snd.at[t], i_rcv.at[t], blk=buddy)

    def out_span(i, t):
        return out.at[:, pl.ds(pl.multiple_of(i * H + t * tile, tile), tile)]

    def out_x(src, t):
        return remote(src.at[t, 1 - x], out_span(x, t), o_snd.at[t], o_rcv.at[t], reader=rx)

    def out_own(src, t):
        return pltpu.make_async_copy(src.at[t, x], out_span(x, t), own_snd.at[t])

    own_proj = pltpu.make_async_copy(proj.at[:, pl.ds(pl.multiple_of(x * H, H), H)], PR.at[b, r], loc.at[0])
    own_image = pltpu.make_async_copy(
        images.at[:, pl.ds(pl.multiple_of(x * H, H), H)], X.at[c, x], loc.at[1]
    )
    noise_copy = pltpu.make_async_copy(
        noise_in.at[pl.ds(pl.multiple_of(x * H, H), H)], noise, loc.at[2]
    )
    routes_copy = pltpu.make_async_copy(routes_in, routes, loc.at[3])

    barrier = pltpu.get_barrier_semaphore()
    for k in (rx, rc, rd):
        pl.semaphore_signal(barrier, inc=1, device_id={"reader": k}, device_id_type=MESH)
    pl.semaphore_signal(barrier, inc=1, device_id={"blk": buddy}, device_id_type=MESH)
    pl.semaphore_signal(barrier, inc=1, device_id={"blk": buddy, "reader": rx}, device_id_type=MESH)

    @pl.when(is_inner)
    def _():
        pl.semaphore_signal(barrier, inc=1, device_id={"blk": across}, device_id_type=MESH)

    own_proj.start()
    own_image.start()
    noise_copy.start()
    routes_copy.start()
    pl.semaphore_wait(barrier, 5 + is_inner.astype(jnp.int32))

    for h in halves:
        proj_x(h).start()
        to_buddy(own_piece(h), b, r, h, whole[h]).start()

        @pl.when(is_inner)
        def _():
            to_across(own_piece(h), b, r, h).start()

    for h in halves:
        to_core(own_piece(h), b, r, h, whole[h]).start()
    own_image_core().start()
    for h in halves:
        piece = part(b, rx, whole[h])
        arrived(piece, p_rcv.at[b, rx, h])
        to_buddy(piece, b, rx, h, whole[h]).start()

        @pl.when(is_inner)
        def _():
            to_across(piece, b, rx, h).start()

        image_x(h).start()
        to_core(piece, b, rx, h, whole[h]).start()

    pieces = ((r, 0), (r, 1), (rx, 0), (rx, 1))

    def other_image(h):
        arrived(X.at[c, 1 - x, :, pl.ds(*strips[h])], x_rcv.at[c, 1 - x, h])

    def hand_over(src, g, h, cut):
        piece = part(src, g, cut)
        arrived(piece, p_rcv.at[src, g, h])
        to_core(piece, src, g, h, cut).start()

    @pl.when(is_end)
    def _():
        own_far(0).start()
        for g, h in pieces:
            hand_over(buddy, g, h, whole[h])
        other_image(0)
        other_far(0).start()
        for g, h in pieces:
            hand_over(far_inner, g, h, short[h])
        other_image(1)
        for g, h in pieces[:3]:
            hand_over(far_end, g, h, short[h])

    @pl.when(is_inner)
    def _():
        for g, h in pieces:
            hand_over(buddy, g, h, whole[h])
            to_across(part(buddy, g, whole[h]), buddy, g, h).start()
            hand_over(far_inner, g, h, whole[h])
            to_buddy(part(far_inner, g, short[h]), far_inner, g, h, short[h]).start()
        for g, h in pieces:
            hand_over(far_end, g, h, whole[h])
            to_buddy(part(far_end, g, short[h]), far_end, g, h, short[h]).start()
        for h in halves:
            other_image(h)

    other_image_core().start()
    own_proj.wait()
    own_image.wait()
    noise_copy.wait()
    routes_copy.wait()

    square = lax.broadcasted_iota(jnp.int32, (width, width), 0) == lax.broadcasted_iota(
        jnp.int32, (width, width), 1
    )

    def scores_of(block, src, tiles):
        scores = jnp.zeros((2 * rows, width), jnp.float32)
        penalty = jnp.zeros((width, 128), jnp.float32)
        for t in tiles:
            cut = pl.ds(t * tile, tile)
            refs_f = PR[src, :, :, cut].reshape(width, tile).astype(jnp.float32)
            scaled = refs_f * noise[cut][None, :]
            scores = scores + lax.dot_general(
                block[c, :, :, cut].reshape(2 * rows, tile), scaled.astype(jnp.bfloat16),
                (((1,), (1,)), ((), ())), preferred_element_type=jnp.float32,
            )
            squares = scaled * refs_f
            for lane in range(0, tile, 128):
                penalty = penalty + squares[:, lane : lane + 128]
        lanes = jnp.sum(penalty, axis=1, keepdims=True)
        penalty_row = 0.5 * jnp.sum(jnp.where(square, lanes, 0.0), axis=0, keepdims=True)
        return (scores - penalty_row).reshape(2, rows, width)

    def from_core(src, h, cut):
        for g in (rc, rd):
            arrived(part(src, g, cut), p_rcv.at[src, g, h])

    @pl.when(is_inner)
    def _():
        for i in (x, 1 - x):
            arrived(XF.at[c, i, :, pl.ds(*far_strips[0])], xf_rcv.at[c, i, 0])

        def far_source(k, carry):
            src = jnp.where(k == 0, far_inner, far_end)
            for h in halves:
                from_core(src, h, whole[h])
            SF[k] = scores_of(XF, src, range(cuts[0]))
            for i in (1, 0):
                far_score(k, i).start()
            return carry

        lax.fori_loop(0, 2, far_source, 0)

    def score_source(i, carry):
        src = jnp.where(i == 0, b, jnp.where(i == 1, buddy, jnp.where(i == 2, far_inner, far_end)))

        @pl.when(i < 2)
        def _():
            for h in halves:
                from_core(src, h, whole[h])

        @pl.when((i < 2) | is_inner)
        def _():
            S[src] = scores_of(X, src, range(T))

        @pl.when((i >= 2) & is_end)
        def _():
            from_core(src, 0, short[0])
            S[src] = scores_of(X, src, range(cuts[0], cuts[1]))

            @pl.when(i == 3)
            def _():
                for g, h in pieces[3:]:
                    hand_over(src, g, h, short[h])

            from_core(src, 1, short[1])
            S[src] = S[src] + scores_of(X, src, range(cuts[1], T))

        score_copy(src).start()
        return carry

    lax.fori_loop(0, 4, score_source, 0)

    @pl.when(is_end)
    def _():
        own_far(1).start()
        other_far(1).start()
        for k, src in enumerate((far_inner, far_end)):
            for i in range(2):
                arrived(FR.at[k, i], f_rcv.at[k, i])
            S[src, x] = S[src, x] + FR[k, 0] + FR[k, 1]

    lane = lax.broadcasted_iota(jnp.int32, (rows, width), 1)
    lane_group = lane // refs
    diagonal = lax.broadcasted_iota(jnp.int32, (rows, rows), 0) == lax.broadcasted_iota(
        jnp.int32, (rows, rows), 1
    )

    def column(row):
        return jnp.sum(jnp.where(diagonal, row, 0.0), axis=1, keepdims=True).astype(jnp.int32)

    names = routes[...].astype(jnp.float32)
    named = (column(names[0:1]) == lane_group) | (column(names[1:2]) == lane_group)
    chunks = []
    for d in range(4):
        arrived(SR.at[d], s_rcv.at[d])
        chunks.append(jnp.where(named, S[d, x] + SR[d], -jnp.inf))
    highest = jnp.maximum(jnp.maximum(chunks[0], chunks[1]), jnp.maximum(chunks[2], chunks[3]))
    highest = jnp.max(highest, axis=1, keepdims=True)
    spread = [jnp.exp(chunk - highest) for chunk in chunks]
    total = jnp.sum((spread[0] + spread[1]) + (spread[2] + spread[3]), axis=1, keepdims=True)
    normalizer = highest + jnp.log(total)
    norm[...] = jnp.sum(jnp.where(diagonal, normalizer, 0.0), axis=0, keepdims=True)
    even = lane_group % 2 == 0
    for p in halves:
        low = jnp.exp(chunks[2 * p] - normalizer)
        high = jnp.exp(chunks[2 * p + 1] - normalizer)
        zero = jnp.where(even, low, pltpu.roll(high, refs, 1))
        one = jnp.where(even, pltpu.roll(low, width - refs, 1), high)
        QP[p, c, x] = jnp.where(c == 0, zero, one).astype(jnp.bfloat16)
        QO[p] = jnp.where(c == 0, one, zero).astype(jnp.bfloat16)
        for k in (0, 2, 1):
            post_copy(k, p).start()

        @pl.when(is_end)
        def _():
            post_far(c, x, p).start()

    for h in halves:
        proj_x(h).wait_send()
        image_x(h).wait_send()
    own_image_core().wait_send()
    other_image_core().wait_send()

    def sent(src, carry):
        score_copy(src).wait_send()
        near_source = (src == b) | (src == buddy)
        for g, h in pieces:
            @pl.when(near_source | is_inner)
            def _():
                piece = part(src, g, whole[h])
                to_core(piece, src, g, h, whole[h]).wait_send()

            @pl.when(src == b)
            def _():
                piece = part(src, g, whole[h])
                to_buddy(piece, src, g, h, whole[h]).wait_send()

            @pl.when((src != b) & (src != buddy))
            def _():
                piece = part(src, g, short[h])

                @pl.when(is_inner)
                def _():
                    to_buddy(piece, src, g, h, short[h]).wait_send()

                @pl.when(is_end)
                def _():
                    to_core(piece, src, g, h, short[h]).wait_send()

            @pl.when(is_inner & near_source)
            def _():
                to_across(part(src, g, whole[h]), src, g, h).wait_send()

        return carry

    lax.fori_loop(0, 4, sent, 0)
    others = ((1 - c, x, 0), (1 - c, x, 1))
    others += tuple((i, 1 - x, p) for p in halves for i in (c, 1 - c))
    for i, j, p in others:
        arrived(QP.at[p, i, j], q_rcv.at[i, j, p])

        @pl.when(is_end)
        def _():
            post_far(i, j, p).start()

    def turned(block):
        flat = block.reshape(4 * rows, width).astype(jnp.float32)
        return flat.T.astype(jnp.bfloat16)

    for p in halves:
        QT[p] = turned(QP[p])
    for i in range(2):
        arrived(X.at[1 - c, i], x_rcv.at[1 - c, i, 0])

    def product(left, right):
        return lax.dot_general(
            left.reshape(2 * width, 4 * rows), right.reshape(4 * rows, tile),
            (((1,), (0,)), ((), ())), preferred_element_type=jnp.float32,
        )

    def span(t):
        return pl.ds(pl.multiple_of(t * tile, tile), tile)

    def near(t):
        return product(QT[...], X[:, :, :, span(t)])

    def keep(t, value):
        PROD[t] = value.reshape(2, 2, 2, refs, tile)

    def own(t, d):
        return PROD[t, d // 2, :, d % 2]

    def f32(value):
        return value.astype(jnp.float32)

    @pl.when(is_end)
    def _():
        def send(t, carry):
            keep(t, near(t))
            for k, d in ((1, far_end), (0, far_inner), (2, inner)):
                TE[k, t - TF] = own(t, d).astype(jnp.bfloat16)
                end_copy(k, t - TF).start()
            return carry

        def pass_on(t, carry):
            arrived(RI.at[t], i_rcv.at[t])
            out_x(RI, t).start()
            out_own(RI, t).start()
            return carry

        def finish(t, carry):
            arrived(RI.at[t], i_rcv.at[t])
            O[t] = (own(t, end) + f32(RI[t])).astype(jnp.bfloat16)
            out_x(O, t).start()
            out_own(O, t).start()
            return carry

        lax.fori_loop(TF, T, send, 0)
        lax.fori_loop(0, TF, pass_on, 0)
        lax.fori_loop(TF, T, finish, 0)

    @pl.when(is_inner)
    def _():
        for i in range(2):
            arrived(XF.at[c, i, :, pl.ds(*far_strips[1])], xf_rcv.at[c, i, 1])
            far_core(i).start()
        for i in range(2):
            arrived(XF.at[1 - c, i], xf_rcv.at[1 - c, i, 0])
        for p in halves:
            for i in range(2):
                for j in range(2):
                    arrived(QF.at[p, i, j], qf_rcv.at[i, j, p])
            QTF[p] = turned(QF[p])

        def outward(k, d, t):
            @pl.when(t < TF)
            def _():
                TM[k, t] = own(t, d).astype(jnp.bfloat16)

            @pl.when(t >= TF)
            def _():
                arrived(RE.at[k, t - TF], e_rcv.at[k, t - TF])
                TM[k, t] = (own(t, d) + f32(RE[k, t - TF])).astype(jnp.bfloat16)

            middle_copy(k, t).start()

        def turn(t, carry):
            @pl.when(t < TF)
            def _():
                keep(t, near(t) + product(QTF[...], XF[:, :, :, span(t)]))

            @pl.when((t >= TF) & (t < T))
            def _():
                keep(t, near(t))

            @pl.when(t < T)
            def _():
                outward(1, far_end, t)

            @pl.when((t >= 2) & (t < T + 2))
            def _():
                outward(0, far_inner, t - 2)
                n = t - 2
                arrived(RM.at[1, n], m_rcv.at[1, n])
                TI[n] = (own(n, end) + f32(RM[1, n])).astype(jnp.bfloat16)
                inner_copy(n).start()

            @pl.when(t >= 4)
            def _():
                n = t - 4
                arrived(RM.at[0, n], m_rcv.at[0, n])
                total = own(n, inner) + f32(RM[0, n])

                @pl.when(n < TF)
                def _():
                    O[n] = total.astype(jnp.bfloat16)

                @pl.when(n >= TF)
                def _():
                    arrived(RE.at[2, n - TF], e_rcv.at[2, n - TF])
                    O[n] = (total + f32(RE[2, n - TF])).astype(jnp.bfloat16)

                out_x(O, n).start()
                out_own(O, n).start()

            return carry

        lax.fori_loop(0, T + 4, turn, 0)

    for k in range(3):
        for p in halves:
            post_copy(k, p).wait_send()

    @pl.when(is_end)
    def _():
        for h in halves:
            own_far(h).wait_send()
            other_far(h).wait_send()
        for i in range(2):
            for j in range(2):
                for p in halves:
                    post_far(i, j, p).wait_send()

        def gone(t, carry):
            for k in range(3):
                end_copy(k, t).wait_send()
            return carry

        lax.fori_loop(0, T - TF, gone, 0)

    @pl.when(is_inner)
    def _():
        for i in range(2):
            far_core(i).wait_send()
            for k in range(2):
                far_score(k, i).wait_send()

        def gone(t, carry):
            for k in range(2):
                middle_copy(k, t).wait_send()
            inner_copy(t).wait_send()
            return carry

        lax.fori_loop(0, T, gone, 0)

    def done(t, carry):
        out_own(O, t).wait()
        out_x(O, t).wait_send()
        arrived(out_span(1 - x, t), o_rcv.at[t])
        return carry

    lax.fori_loop(0, T, done, 0)


def score_cuts(T):
    low = max(1, 3 * T // 8)
    return low, max(low + 1, 3 * T // 4)


def hand_out(sums_in, norm_in, sums_out, norm_out):
    sums_out[...] = sums_in[...].astype(jnp.float32)
    norm_out[...] = norm_in[...]


def paired_halves(images, routes, projections, noise_weights):
    rows, coef = images.shape
    refs = projections.shape[1]
    H, width = coef // 2, 4 * refs
    F = H // 2
    tile = min(F, 512)
    T, TF = H // tile, F // tile
    TN = T - TF
    dma = pltpu.SemaphoreType.DMA
    bf16, f32 = jnp.bfloat16, jnp.float32
    piece = (2, refs, tile)
    sums, norm = pl.pallas_call(
        paired,
        out_shape=(
            jax.ShapeDtypeStruct((refs, coef), bf16),
            jax.ShapeDtypeStruct((1, rows), f32),
        ),
        in_specs=[pl.BlockSpec(memory_space=pltpu.HBM)] * 4,
        out_specs=(
            pl.BlockSpec(memory_space=pl.ANY),
            pl.BlockSpec(memory_space=pltpu.VMEM),
        ),
        scratch_shapes=[
            pltpu.VMEM((2, rows), jnp.int32),
            pltpu.VMEM((H,), f32),
            pltpu.VMEM((2, 2, rows, H), bf16),
            pltpu.VMEM((2, 2, rows, F), bf16),
            pltpu.VMEM((4, 4, refs, H), bf16),
            pltpu.VMEM((4, 2, rows, width), f32),
            pltpu.VMEM((4, rows, width), f32),
            pltpu.VMEM((2, 2, rows, width), f32),
            pltpu.VMEM((2, 2, rows, width), f32),
            pltpu.VMEM((2, 2, 2, rows, width), bf16),
            pltpu.VMEM((2, rows, width), bf16),
            pltpu.VMEM((2, 2, 2, rows, width), bf16),
            pltpu.VMEM((2, width, 4 * rows), bf16),
            pltpu.VMEM((2, width, 4 * rows), bf16),
            pltpu.VMEM((T, 2, 2, 2, refs, tile), f32),
            pltpu.VMEM((3, TN) + piece, bf16),
            pltpu.VMEM((3, TN) + piece, bf16),
            pltpu.VMEM((2, T) + piece, bf16),
            pltpu.VMEM((2, T) + piece, bf16),
            pltpu.VMEM((T,) + piece, bf16),
            pltpu.VMEM((T,) + piece, bf16),
            pltpu.VMEM((T,) + piece, bf16),
            dma((4,)), dma((2,)), dma((4, 4, 2)), dma((4, 4, 2)), dma((4, 4, 2)), dma((4, 4, 2)),
            dma((2,)), dma((2,)), dma((2, 2, 2)), dma((2, 2)), dma((2,)), dma((2, 2, 2)),
            dma((4,)), dma((4,)), dma((2, 2)), dma((2, 2)), dma((3, 2)), dma((2, 2, 2)), dma((2, 2, 2)), dma((2, 2, 2)),
            dma((3, TN)), dma((3, TN)), dma((2, T)), dma((2, T)), dma((T,)), dma((T,)),
            dma((T,)), dma((T,)), dma((T,)),
        ],
        compiler_params=pltpu.CompilerParams(
            collective_id=0, has_side_effects=True, vmem_limit_bytes=64 * 1024 * 1024 - 65536
        ),
        cost_estimate=pl.CostEstimate(
            flops=4 * 4 * rows * 4 * width * H // 2, bytes_accessed=4 * rows * coef, transcendentals=0
        ),
    )(images, routes.T, projections[0], noise_weights)
    block = coef // 2
    sums, norm = pl.pallas_call(
        hand_out,
        grid=(coef // block,),
        out_shape=(jax.ShapeDtypeStruct((refs, coef), f32), jax.ShapeDtypeStruct((1, rows), f32)),
        in_specs=[pl.BlockSpec((refs, block), lambda i: (0, i)), pl.BlockSpec((1, rows), lambda i: (0, 0))],
        out_specs=(pl.BlockSpec((refs, block), lambda i: (0, i)), pl.BlockSpec((1, rows), lambda i: (0, 0))),
    )(sums, norm)
    return (sums[None], norm[0])


def solution(mesh):
    sizes = dict(mesh.shape)
    direct = sizes["sub"] == 1 and sizes["reader"] == 4 and sizes["blk"] == 4
    return jax.shard_map(
        paired_halves if direct else routed,
        mesh=mesh,
        in_specs=(
            P(("parts", "blk", "reader"), "sub"),
            P(("parts", "blk", "reader"), None),
            P(("parts", "reader"), "blk", "sub"),
            P(("parts", "sub")),
        ),
        out_specs=(P(("parts", "reader"), "blk", "sub"), P(("parts", "blk", "reader"))),
        check_vma=False,
    )
```

```python
from functools import partial

import jax
import jax.numpy as jnp
from jax import lax
from jax.experimental import pallas as pl
from jax.experimental.pallas import tpu as pltpu
from jax.sharding import PartitionSpec as P

MESH = pl.DeviceIdType.MESH


def from_behind(block, axis, distance):
    devices = range(lax.axis_size(axis))
    route = [((i - distance) % len(devices), i) for i in devices]
    return lax.ppermute(block, axis, route)


def slot_positions(route_block):
    flat = route_block.reshape(-1)
    order = jnp.arange(flat.shape[0], dtype=jnp.int32)
    earlier = (order[None, :] < order[:, None]) & (flat[None, :] == flat[:, None])
    return jnp.sum(earlier.astype(jnp.int32), axis=1).reshape(route_block.shape)


def combine_stats(row_peaks, row_totals):
    highest = jnp.max(row_peaks, axis=-1)
    spread = row_totals * jnp.exp(row_peaks - highest[..., None])
    return highest + jnp.log(jnp.sum(spread, axis=-1))


def routed(images, routes, projections, noise_weights):
    groups = lax.axis_size("reader")
    cycle_size = lax.axis_size("blk")
    my_group = lax.axis_index("reader")
    my_member = lax.axis_index("blk")
    per_device, top_count = routes.shape
    half_width = images.shape[1]
    capacity = min(per_device, 2 * per_device * top_count // groups)
    slot_count = groups * capacity
    ref_count = projections.shape[1]
    all_refs = ref_count * cycle_size
    anchor = jnp.zeros((), jnp.int32)
    own_index = slot_positions(routes)
    own_target = routes * capacity + own_index
    sources = jnp.broadcast_to(jnp.arange(per_device, dtype=jnp.int32)[:, None], routes.shape)
    picker = (
        jnp.full((slot_count,), per_device, jnp.int32)
        .at[own_target.reshape(-1)]
        .set(sources.reshape(-1))
    )
    padded = jnp.concatenate([images, jnp.zeros((1, half_width), images.dtype)], axis=0)
    outgoing = padded[picker].reshape(groups, capacity, half_width)
    received = lax.all_to_all(outgoing, "reader", split_axis=0, concat_axis=0, tiled=True).reshape(
        slot_count, half_width
    )
    every_route = lax.all_gather(routes, "reader", axis=0, tiled=True).reshape(
        groups, per_device, top_count
    )
    every_index = jax.vmap(slot_positions)(every_route)
    senders = jnp.arange(groups, dtype=jnp.int32)[:, None, None]
    landing = jnp.where(every_route == my_group, senders * capacity + every_index, slot_count)
    live_slot = jnp.zeros((slot_count,), jnp.int32).at[landing.reshape(-1)].set(1, mode="drop") > 0

    def score_block(ref_block):
        scaled = ref_block.astype(jnp.float32) * noise_weights[None, :]
        weighted = scaled.astype(jnp.bfloat16)
        penalty = 0.5 * jnp.sum(scaled * ref_block.astype(jnp.float32), axis=1)
        partial_scores = lax.dot_general(
            weighted, received, (((1,), (1,)), ((), ())), preferred_element_type=jnp.float32
        )
        return partial_scores - penalty[:, None]

    def cycle_turn(rotation, carry):
        ref_block, score_table = carry
        position = (my_member - rotation) % cycle_size
        score_table = lax.dynamic_update_slice(
            score_table, score_block(ref_block)[None], (position, anchor, anchor)
        )
        ref_block = from_behind(ref_block, "blk", 1)
        return (ref_block, score_table)

    empty_table = jnp.zeros((cycle_size, ref_count, slot_count), jnp.float32)
    ref_block, score_table = lax.fori_loop(
        0, cycle_size - 1, cycle_turn, (projections[0], empty_table)
    )
    position = (my_member + 1) % cycle_size
    score_table = lax.dynamic_update_slice(
        score_table, score_block(ref_block)[None], (position, anchor, anchor)
    )
    score_table = lax.psum(score_table, "sub")
    scores = score_table.reshape(all_refs, slot_count)
    row_peak = jnp.max(scores, axis=0)
    row_total = jnp.sum(jnp.exp(scores - row_peak[None, :]), axis=0)
    back_peak, back_total = (
        lax.all_to_all(
            row_peak.reshape(groups, capacity), "reader", split_axis=0, concat_axis=0, tiled=True
        ),
        lax.all_to_all(
            row_total.reshape(groups, capacity), "reader", split_axis=0, concat_axis=0, tiled=True
        ),
    )
    normalizer = combine_stats(
        back_peak.reshape(-1)[own_target], back_total.reshape(-1)[own_target]
    )
    outgoing_norm = (
        jnp.zeros((slot_count,), jnp.float32)
        .at[own_target.reshape(-1)]
        .set(jnp.repeat(normalizer, top_count))
    )
    slot_norm = lax.all_to_all(
        outgoing_norm.reshape(groups, capacity), "reader", split_axis=0, concat_axis=0, tiled=True
    ).reshape(slot_count)
    exponent = jnp.where(live_slot[None, :], scores - slot_norm[None, :], -jnp.inf)
    posterior = jnp.exp(exponent).astype(jnp.bfloat16)
    summed = lax.psum_scatter(
        jnp.dot(posterior, received, preferred_element_type=jnp.float32).astype(jnp.bfloat16),
        "blk",
        scatter_dimension=0,
        tiled=True,
    ).astype(jnp.float32)
    return (summed[None], normalizer)


LOW = 3
CUTS = (3, 5, 8)


def paired(
    images, routes_in, proj, noise_in,
    out, norm,
    routes, noise, X, XF, PR, S, SC, SR, MOVE, SAME, SF, FR, QP, QO, QF, QT, QTF, PROD, TE, RE, TM, RM, TI, RI, O,
    loc, rt_snd, rt_rcv, px_snd, pb_snd, pm_snd, pc_snd, p_rcv, c_rcv, xx_snd, xc_snd, x_rcv, xf_snd, xfc_snd, xf_rcv,
    s_snd, s_rcv, f_snd, f_rcv, q_snd, q_rcv, qf_snd, qf_rcv, e_snd, e_rcv, m_snd, m_rcv, i_snd, i_rcv,
    own_snd, o_snd, o_rcv,
):
    r = lax.axis_index("reader")
    b = lax.axis_index("blk")
    x, c = r // 2, r % 2
    rx, rc = (r + 2) % 4, x * 2 + 1 - c
    rd = (rc + 2) % 4
    side = b // 2
    inner, end = 1 + side, 3 * side
    far_inner, far_end = 2 - side, 3 - 3 * side
    buddy, across = inner + end - b, 3 - b
    is_end = b == end
    is_inner = b == inner
    rows = images.shape[0]
    refs = proj.shape[0]
    H = X.shape[4 - 1]
    F = H // 2
    T, tile = O.shape[0], O.shape[3]
    TF = F // tile
    low = LOW * tile
    width = 4 * refs
    halves = (0, 1)
    pairs = (1 - side, side)
    marks = (0,) + CUTS
    whole = tuple((a * tile, (e - a) * tile) for a, e in zip(marks, CUTS))
    bits = range(len(CUTS))
    late = bits[1:]
    queue = tuple(late) + (0,)
    strips = ((0, low), (low, H - low))
    far_strips = ((0, low), (low, F - low))

    def remote(src, dst, snd, rcv, **where):
        return pltpu.make_async_remote_copy(
            src_ref=src, dst_ref=dst, send_sem=snd, recv_sem=rcv,
            device_id=where, device_id_type=MESH,
        )

    def arrived(dst, sem):
        remote(dst, dst, sem, sem, reader=rx).wait_recv()

    def left(src, sem):
        remote(src, src, sem, sem, reader=rx).wait_send()

    def columns(i, cut):
        return pl.ds(pl.multiple_of(i * H + cut[0], tile), cut[1])

    def part(src, g, cut):
        return PR.at[src, g, :, pl.ds(*cut)]

    def own_piece(h):
        return proj.at[:, columns(x, whole[h])]

    def proj_x(h):
        return remote(
            proj.at[:, columns(1 - x, whole[h])], part(b, r, whole[h]), px_snd.at[0], p_rcv.at[b, x, h], reader=rx
        )

    def stage(h):
        return h // (len(CUTS) - 1)

    def to_core(piece, src, g, h):
        late_one = is_end & (src != b) & (src != buddy)
        return remote(
            piece, part(src, g, whole[h]), pc_snd.at[late_one.astype(jnp.int32)], c_rcv.at[src, stage(h)], reader=rc
        )

    def to_buddy(piece, src, g, h):
        return remote(
            piece, part(src, g, whole[h]), pb_snd.at[(src != b).astype(jnp.int32)], p_rcv.at[src, g // 2, h], blk=buddy
        )

    def to_across(piece, src, g, h):
        return remote(piece, part(src, g, whole[h]), pm_snd.at[0], p_rcv.at[src, g // 2, h], blk=across)

    def image_x(h):
        return remote(
            images.at[:, columns(1 - x, strips[h])], X.at[c, x, :, pl.ds(*strips[h])],
            xx_snd.at[0], x_rcv.at[h], reader=rx,
        )

    def own_image_core():
        return remote(
            images.at[:, pl.ds(pl.multiple_of(x * H, H), H)], X.at[c, x],
            xc_snd.at[0], x_rcv.at[2], reader=rc,
        )

    def other_image_core():
        return remote(X.at[c, 1 - x], X.at[c, 1 - x], xc_snd.at[0], x_rcv.at[2], reader=rc)

    def own_far(h):
        return remote(
            images.at[:, columns(x, far_strips[h])], XF.at[c, x, :, pl.ds(*far_strips[h])],
            xf_snd.at[0], xf_rcv.at[h], blk=buddy,
        )

    def other_far(h):
        return remote(
            X.at[c, 1 - x, :, pl.ds(*far_strips[h])], XF.at[c, 1 - x, :, pl.ds(*far_strips[h])],
            xf_snd.at[0], xf_rcv.at[h], blk=buddy,
        )

    def far_core(i):
        return remote(XF.at[c, i], XF.at[c, i], xfc_snd.at[0], xf_rcv.at[2], reader=rc)

    def score_copy(q):
        return remote(SC.at[q], SR.at[q], s_snd.at[0], s_rcv.at[q], reader=rx)

    def routes_x():
        return remote(routes_in, routes.at[x], rt_snd.at[0], rt_rcv.at[0], reader=rx)

    def far_score(k, i):
        if i == 0:
            return remote(SF.at[k, x], FR.at[k, x], f_snd.at[0], f_rcv.at[0], blk=buddy)
        return remote(SF.at[k, 1 - x], FR.at[k, x], f_snd.at[0], f_rcv.at[0], blk=buddy, reader=rx)

    def post_copy(k, p):
        source, to = ((QP.at[p, c, x], rx), (QO.at[p], rc), (QO.at[p], rd))[k]
        return remote(source, QP.at[p, c, x], q_snd.at[k % 2], q_rcv.at[c, x, p], reader=to)

    def post_far(i, j, p):
        return remote(QP.at[p, i, j], QF.at[p, i, j], qf_snd.at[0], qf_rcv.at[p], blk=buddy)

    def end_copy(k, t):
        return remote(TE.at[k, t], RE.at[k, t], e_snd.at[0], e_rcv.at[k, t], blk=buddy)

    def middle_copy(k, t):
        return remote(TM.at[k, t], RM.at[k, t], m_snd.at[0], m_rcv.at[k, t], blk=across)

    def inner_copy(t):
        return remote(TI.at[t], RI.at[t], i_snd.at[0], i_rcv.at[t], blk=buddy)

    def out_span(i, t):
        return out.at[:, pl.ds(pl.multiple_of(i * H + t * tile, tile), tile)]

    def out_x(src, t):
        return remote(src.at[t, 1 - x], out_span(x, t), o_snd.at[0], o_rcv.at[0], reader=rx)

    def out_own(src, t):
        return pltpu.make_async_copy(src.at[t, x], out_span(x, t), own_snd.at[0])

    own_proj = pltpu.make_async_copy(proj.at[:, pl.ds(pl.multiple_of(x * H, H), H)], PR.at[b, r], loc.at[0])
    own_image = pltpu.make_async_copy(
        images.at[:, pl.ds(pl.multiple_of(x * H, H), H)], X.at[c, x], loc.at[1]
    )
    noise_copy = pltpu.make_async_copy(
        noise_in.at[pl.ds(pl.multiple_of(x * H, H), H)], noise, loc.at[2]
    )
    routes_copy = pltpu.make_async_copy(routes_in, routes.at[x], loc.at[3])

    barrier = pltpu.get_barrier_semaphore()
    for k in (rx, rc, rd):
        pl.semaphore_signal(barrier, inc=1, device_id={"reader": k}, device_id_type=MESH)
    pl.semaphore_signal(barrier, inc=1, device_id={"blk": buddy}, device_id_type=MESH)
    pl.semaphore_signal(barrier, inc=1, device_id={"blk": buddy, "reader": rx}, device_id_type=MESH)

    @pl.when(is_inner)
    def _():
        pl.semaphore_signal(barrier, inc=1, device_id={"blk": across}, device_id_type=MESH)

    own_proj.start()
    own_image.start()
    noise_copy.start()
    routes_copy.start()
    pl.semaphore_wait(barrier, 5 + is_inner.astype(jnp.int32))

    def spread(piece, g, h):
        to_buddy(piece, b, g, h).start()

        @pl.when(is_inner)
        def _():
            to_across(piece, b, g, h).start()

    routes_x().start()
    for h in queue:
        proj_x(h).start()
        if h > 0:
            spread(own_piece(h), r, h)
    for h in queue:
        to_core(own_piece(h), b, r, h).start()
    for h in queue:
        piece = part(b, rx, whole[h])
        arrived(piece, p_rcv.at[b, 1 - x, h])
        if h == 0:
            spread(own_piece(h), r, h)
        spread(piece, rx, h)
        to_core(piece, b, rx, h).start()
        if h == queue[1]:
            for k in halves:
                image_x(k).start()
    own_image_core().start()

    late_pieces = tuple((g, h) for g in (r, rx) for h in late)
    pieces = late_pieces + ((r, 0), (rx, 0))

    def other_image(h):
        arrived(X.at[c, 1 - x, :, pl.ds(*strips[h])], x_rcv.at[h])

    def hand_over(src, g, h):
        piece = part(src, g, whole[h])
        arrived(piece, p_rcv.at[src, g // 2, h])
        to_core(piece, src, g, h).start()

    @pl.when(is_end)
    def _():
        for g, h in pieces[:4]:
            hand_over(buddy, g, h)
        own_far(0).start()
        for g, h in pieces[4:]:
            hand_over(buddy, g, h)
        other_image(0)
        other_far(0).start()
        for g, h in late_pieces:
            hand_over(far_inner, g, h)
        other_image(1)
        own_far(1).start()
        other_far(1).start()
        for g, h in late_pieces[:-2]:
            hand_over(far_end, g, h)

    @pl.when(is_inner)
    def _():
        for g, h in pieces:
            arrived(part(far_inner, g, whole[h]), p_rcv.at[far_inner, g // 2, h])
            if h > 0:
                to_buddy(part(far_inner, g, whole[h]), far_inner, g, h).start()
            to_core(part(far_inner, g, whole[h]), far_inner, g, h).start()
            arrived(part(buddy, g, whole[h]), p_rcv.at[buddy, g // 2, h])
            to_across(part(buddy, g, whole[h]), buddy, g, h).start()
            to_core(part(buddy, g, whole[h]), buddy, g, h).start()
        for g, h in pieces:
            arrived(part(far_end, g, whole[h]), p_rcv.at[far_end, g // 2, h])
            if h > 0:
                to_buddy(part(far_end, g, whole[h]), far_end, g, h).start()
            to_core(part(far_end, g, whole[h]), far_end, g, h).start()
        for h in halves:
            other_image(h)

    other_image_core().start()
    own_proj.wait()
    own_image.wait()
    noise_copy.wait()
    routes_copy.wait()

    arrived(routes.at[1 - x], rt_rcv.at[0])
    lane = lax.broadcasted_iota(jnp.int32, (rows, width), 1)
    block = lane // refs
    diagonal = lax.broadcasted_iota(jnp.int32, (rows, rows), 0) == lax.broadcasted_iota(
        jnp.int32, (rows, rows), 1
    )

    def column(row):
        return jnp.sum(jnp.where(diagonal, row, 0.0), axis=1, keepdims=True).astype(jnp.int32)

    for i in range(2):
        names = routes[i].astype(jnp.float32)
        first, second = column(names[0:1]), column(names[1:2])
        MOVE[i] = (block - jnp.where(block < 2, first, second) + 4) % 4
        @pl.when(i == x)
        def _():
            SAME[0] = jnp.where(block < 2, first, second)
            SAME[1] = jnp.where(block < 2, second, first)

    def packed(p, i):
        even = block % 2 == 0
        low, high, move = S[2 * p, i], S[2 * p + 1, i], MOVE[i]
        total = jnp.where(even, low, high)
        for m in range(1, 4):
            turned_by = jnp.where(even, pltpu.roll(low, m * refs, 1), pltpu.roll(high, m * refs, 1))
            total = jnp.where(move == m, turned_by, total)
        return total

    square = lax.broadcasted_iota(jnp.int32, (width, width), 0) == lax.broadcasted_iota(
        jnp.int32, (width, width), 1
    )

    def scores_of(block, src, tiles):
        scores = jnp.zeros((2 * rows, width), jnp.float32)
        penalty = jnp.zeros((width, 128), jnp.float32)
        for t in tiles:
            cut = pl.ds(t * tile, tile)
            refs_f = PR[src, :, :, cut].reshape(width, tile).astype(jnp.float32)
            scaled = refs_f * noise[cut][None, :]
            scores = scores + lax.dot_general(
                block[c, :, :, cut].reshape(2 * rows, tile), scaled.astype(jnp.bfloat16),
                (((1,), (1,)), ((), ())), preferred_element_type=jnp.float32,
            )
            squares = scaled * refs_f
            for lane in range(0, tile, 128):
                penalty = penalty + squares[:, lane : lane + 128]
        lanes = jnp.sum(penalty, axis=1, keepdims=True)
        penalty_row = 0.5 * jnp.sum(jnp.where(square, lanes, 0.0), axis=0, keepdims=True)
        return (scores - penalty_row).reshape(2, rows, width)

    def from_core(src, n, first):
        start = marks[first]
        both = PR.at[src, pl.ds(0, 2), :, pl.ds(start * tile, (CUTS[-2 + n] - start) * tile)]
        arrived(both, c_rcv.at[src, n])

    @pl.when(is_inner)
    def _():
        arrived(XF.at[c, :, :, pl.ds(*far_strips[0])], xf_rcv.at[0])

        def far_source(k, carry):
            src = jnp.where(k == 0, far_inner, far_end)
            from_core(src, 0, 0)
            from_core(src, 1, len(CUTS) - 1)
            SF[k] = scores_of(XF, src, range(LOW))
            for i in (1, 0):
                far_score(k, i).start()
            return carry

        lax.fori_loop(0, 2, far_source, 0)

    def score_source(i, carry):
        src = jnp.where(i == 0, b, jnp.where(i == 1, buddy, jnp.where(i == 2, far_inner, far_end)))

        @pl.when(i < 2)
        def _():
            from_core(src, 0, 0)
            from_core(src, 1, len(CUTS) - 1)

        @pl.when((i < 2) | is_inner)
        def _():
            S[src] = scores_of(X, src, range(T))

        @pl.when((i >= 2) & is_end)
        def _():
            @pl.when(i == 3)
            def _():
                hand_over(src, *late_pieces[-2])

            from_core(src, 0, 1)
            S[src] = scores_of(X, src, range(LOW, CUTS[-2]))

            @pl.when(i == 3)
            def _():
                hand_over(src, *late_pieces[-1])

            from_core(src, 1, len(CUTS) - 1)
            S[src] = S[src] + scores_of(X, src, range(CUTS[-2], T))

        @pl.when(i % 2 == 1)
        def _():
            q = i // 2
            SC[q] = packed(side + q * (1 - 2 * side), 1 - x)
            score_copy(q).start()

        return carry

    lax.fori_loop(0, 4, score_source, 0)

    @pl.when(is_end)
    def _():
        arrived(FR, f_rcv.at[0])
        for k, src in enumerate((far_inner, far_end)):
            S[src, x] = S[src, x] + FR[k, 0] + FR[k, 1]

    chunks = []
    for q, p in enumerate(pairs):
        arrived(SR.at[1 - q], s_rcv.at[1 - q])
        chunks.append(packed(p, x) + SR[1 - q])
    highest = jnp.max(jnp.maximum(chunks[0], chunks[1]), axis=1, keepdims=True)
    total = jnp.exp(chunks[0] - highest) + jnp.exp(chunks[1] - highest)
    normalizer = highest + jnp.log(jnp.sum(total, axis=1, keepdims=True))
    norm[...] = jnp.sum(jnp.where(diagonal, normalizer, 0.0), axis=0, keepdims=True)

    def for_core(value, core):
        group = core + 2 * (lane // (2 * refs))
        swapped = jnp.where(SAME[1] == group, pltpu.roll(value, 2 * refs, 1), 0.0)
        return jnp.where(SAME[0] == group, value, swapped).astype(jnp.bfloat16)

    for q, p in enumerate(pairs):
        value = jnp.exp(chunks[q] - normalizer)
        QP[p, c, x] = for_core(value, c)
        QO[p] = for_core(value, 1 - c)
        for k in (0, 2, 1):
            post_copy(k, p).start()

        @pl.when(is_end)
        def _():
            post_far(c, x, p).start()

    for p in pairs:
        for i, j in ((1 - c, x), (c, 1 - x), (1 - c, 1 - x)):
            arrived(QP.at[p, i, j], q_rcv.at[i, j, p])

            @pl.when(is_end)
            def _():
                post_far(i, j, p).start()

    left(PR.at[0, 0], px_snd.at[0])
    left(X.at[0, 0], xx_snd.at[0])
    left(X.at[0], xc_snd.at[0])
    left(SC, s_snd.at[0])
    routes_x().wait_send()
    late_columns = pl.ds(low, H - low)
    left(PR.at[0, pl.ds(0, 2)], pb_snd.at[0])

    @pl.when(is_end)
    def _():
        left(PR.at[pl.ds(0, 2), pl.ds(0, 2)], pc_snd.at[0])
        left(PR.at[pl.ds(0, 2), pl.ds(0, 2), :, late_columns], pc_snd.at[1])

    @pl.when(is_inner)
    def _():
        left(PR.at[:, pl.ds(0, 2)], pc_snd.at[0])
        left(PR.at[pl.ds(0, 2), pl.ds(0, 2), :, late_columns], pb_snd.at[1])
        left(PR.at[pl.ds(0, 2), pl.ds(0, 2)], pm_snd.at[0])

    def turned(block):
        flat = block.reshape(4 * rows, width).astype(jnp.float32)
        return flat.T.astype(jnp.bfloat16)

    for p in halves:
        QT[p] = turned(QP[p])
    arrived(X.at[1 - c], x_rcv.at[2])

    def product(left, right):
        return lax.dot_general(
            left, right.reshape(4 * rows, tile), (((1,), (0,)), ((), ())), preferred_element_type=jnp.float32
        )

    def span(t):
        return pl.ds(pl.multiple_of(t * tile, tile), tile)

    def multiply(q, t, both):
        total = product(QT[pairs[q]], X[:, :, :, span(t)])
        if both:
            total = total + product(QTF[pairs[q]], XF[:, :, :, span(t)])
        PROD[t, q] = total.reshape(2, 2, refs, tile)

    def own(t, q, d):
        return PROD[t, q, :, d % 2]

    def f32(value):
        return value.astype(jnp.float32)

    @pl.when(is_end)
    def _():
        def send(t, carry):
            for k, q, d in ((1, 0, far_end), (0, 0, far_inner), (2, 1, inner)):
                if k != 0:
                    multiply(q, t, False)
                TE[k, t - TF] = own(t, q, d).astype(jnp.bfloat16)
                end_copy(k, t - TF).start()
            return carry

        def pass_on(t, carry):
            arrived(RI.at[t], i_rcv.at[t])
            out_x(RI, t).start()
            out_own(RI, t).start()
            return carry

        def finish(t, carry):
            arrived(RI.at[t], i_rcv.at[t])
            O[t] = (own(t, 1, end) + f32(RI[t])).astype(jnp.bfloat16)
            out_x(O, t).start()
            out_own(O, t).start()
            return carry

        left(QP, qf_snd.at[0])
        lax.fori_loop(TF, T, send, 0)
        lax.fori_loop(0, TF, pass_on, 0)
        lax.fori_loop(TF, T, finish, 0)

    @pl.when(is_inner)
    def _():
        arrived(XF.at[c, :, :, pl.ds(*far_strips[1])], xf_rcv.at[1])
        for i in range(2):
            far_core(i).start()
        arrived(XF.at[1 - c], xf_rcv.at[2])

        def far_posterior(q):
            p = pairs[q]
            arrived(QF.at[p], qf_rcv.at[p])
            QTF[p] = turned(QF[p])

        def multiply_any(q, t):
            @pl.when(t < TF)
            def _():
                multiply(q, t, True)

            @pl.when(t >= TF)
            def _():
                multiply(q, t, False)

        far_posterior(0)

        def outward(k, d, t):
            @pl.when(t < TF)
            def _():
                TM[k, t] = own(t, 0, d).astype(jnp.bfloat16)

            @pl.when(t >= TF)
            def _():
                arrived(RE.at[k, t - TF], e_rcv.at[k, t - TF])
                TM[k, t] = (own(t, 0, d) + f32(RE[k, t - TF])).astype(jnp.bfloat16)

            middle_copy(k, t).start()

        def turn(t, carry):
            @pl.when(t < T)
            def _():
                multiply_any(0, t)
                outward(1, far_end, t)

            @pl.when((t >= 2) & (t < T + 2))
            def _():
                outward(0, far_inner, t - 2)

            @pl.when(t == 1)
            def _():
                far_posterior(1)

            @pl.when((t >= 1) & (t < T + 1))
            def _():
                multiply_any(1, t - 1)

            @pl.when((t >= 2) & (t < T + 2))
            def _():
                n = t - 2
                arrived(RM.at[1, n], m_rcv.at[1, n])
                TI[n] = (own(n, 1, end) + f32(RM[1, n])).astype(jnp.bfloat16)
                inner_copy(n).start()

            @pl.when(t >= 4)
            def _():
                n = t - 4
                arrived(RM.at[0, n], m_rcv.at[0, n])
                total = own(n, 1, inner) + f32(RM[0, n])

                @pl.when(n < TF)
                def _():
                    O[n] = total.astype(jnp.bfloat16)

                @pl.when(n >= TF)
                def _():
                    arrived(RE.at[2, n - TF], e_rcv.at[2, n - TF])
                    O[n] = (total + f32(RE[2, n - TF])).astype(jnp.bfloat16)

                out_x(O, n).start()
                out_own(O, n).start()

            return carry

        lax.fori_loop(0, T + 4, turn, 0)

    left(QP.at[0], q_snd.at[0])
    left(QP.at[0, 0], q_snd.at[1])

    @pl.when(is_end)
    def _():
        left(XF.at[0], xf_snd.at[0])
        left(TE, e_snd.at[0])

    @pl.when(is_inner)
    def _():
        left(XF.at[0], xfc_snd.at[0])
        left(SF, f_snd.at[0])
        left(TM, m_snd.at[0])
        left(TI, i_snd.at[0])

    left(O.at[:, 0], o_snd.at[0])
    pltpu.make_async_copy(O.at[:, 0], O.at[:, 0], own_snd.at[0]).wait()
    arrived(out.at[:, pl.ds(pl.multiple_of((1 - x) * H, H), H)], o_rcv.at[0])


def hand_out(sums_in, norm_in, sums_out, norm_out):
    sums_out[...] = sums_in[...].astype(jnp.float32)
    norm_out[...] = norm_in[...]


def paired_halves(images, routes, projections, noise_weights):
    rows, coef = images.shape
    refs = projections.shape[1]
    H, width = coef // 2, 4 * refs
    F = H // 2
    T, TF = 8, 4
    tile = H // T
    TN = T - TF
    dma = pltpu.SemaphoreType.DMA
    bf16, f32 = jnp.bfloat16, jnp.float32
    piece = (2, refs, tile)
    sums, norm = pl.pallas_call(
        paired,
        out_shape=(
            jax.ShapeDtypeStruct((refs, coef), bf16),
            jax.ShapeDtypeStruct((1, rows), f32),
        ),
        in_specs=[pl.BlockSpec(memory_space=pltpu.HBM)] * 4,
        out_specs=(
            pl.BlockSpec(memory_space=pl.ANY),
            pl.BlockSpec(memory_space=pltpu.VMEM),
        ),
        scratch_shapes=[
            pltpu.VMEM((2, 2, rows), jnp.int32),
            pltpu.VMEM((H,), f32),
            pltpu.VMEM((2, 2, rows, H), bf16),
            pltpu.VMEM((2, 2, rows, F), bf16),
            pltpu.VMEM((4, 4, refs, H), bf16),
            pltpu.VMEM((4, 2, rows, width), f32),
            pltpu.VMEM((2, rows, width), f32),
            pltpu.VMEM((2, rows, width), f32),
            pltpu.VMEM((2, rows, width), jnp.int32),
            pltpu.VMEM((2, rows, width), jnp.int32),
            pltpu.VMEM((2, 2, rows, width), f32),
            pltpu.VMEM((2, 2, rows, width), f32),
            pltpu.VMEM((2, 2, 2, rows, width), bf16),
            pltpu.VMEM((2, rows, width), bf16),
            pltpu.VMEM((2, 2, 2, rows, width), bf16),
            pltpu.VMEM((2, width, 4 * rows), bf16),
            pltpu.VMEM((2, width, 4 * rows), bf16),
            pltpu.VMEM((T, 2, 2, 2, refs, tile), f32),
            pltpu.VMEM((3, TN) + piece, bf16),
            pltpu.VMEM((3, TN) + piece, bf16),
            pltpu.VMEM((2, T) + piece, bf16),
            pltpu.VMEM((2, T) + piece, bf16),
            pltpu.VMEM((T,) + piece, bf16),
            pltpu.VMEM((T,) + piece, bf16),
            pltpu.VMEM((T,) + piece, bf16),
            dma((4,)), dma((1,)), dma((1,)), dma((1,)), dma((2,)), dma((1,)), dma((2,)),
            dma((4, 2, len(CUTS))), dma((4, 2)), dma((1,)), dma((1,)), dma((3,)), dma((1,)), dma((1,)), dma((3,)),
            dma((1,)), dma((2,)), dma((1,)), dma((1,)), dma((2,)), dma((2, 2, 2)), dma((1,)), dma((2,)),
            dma((1,)), dma((3, TN)), dma((1,)), dma((2, T)), dma((1,)), dma((T,)),
            dma((1,)), dma((1,)), dma((1,)),
        ],
        compiler_params=pltpu.CompilerParams(
            collective_id=0, has_side_effects=True, vmem_limit_bytes=64 * 1024 * 1024 - 65536
        ),
        cost_estimate=pl.CostEstimate(
            flops=4 * 4 * rows * 4 * width * H // 2, bytes_accessed=4 * rows * coef, transcendentals=0
        ),
    )(images, routes.T, projections[0], noise_weights)
    block = coef // 2
    sums, norm = pl.pallas_call(
        hand_out,
        grid=(coef // block,),
        out_shape=(jax.ShapeDtypeStruct((refs, coef), f32), jax.ShapeDtypeStruct((1, rows), f32)),
        in_specs=[pl.BlockSpec((refs, block), lambda i: (0, i)), pl.BlockSpec((1, rows), lambda i: (0, 0))],
        out_specs=(pl.BlockSpec((refs, block), lambda i: (0, i)), pl.BlockSpec((1, rows), lambda i: (0, 0))),
    )(sums, norm)
    return (sums[None], norm[0])


def solution(mesh):
    sizes = dict(mesh.shape)
    direct = sizes["sub"] == 1 and sizes["reader"] == 4 and sizes["blk"] == 4
    return jax.shard_map(
        paired_halves if direct else routed,
        mesh=mesh,
        in_specs=(
            P(("parts", "blk", "reader"), "sub"),
            P(("parts", "blk", "reader"), None),
            P(("parts", "reader"), "blk", "sub"),
            P(("parts", "sub")),
        ),
        out_specs=(P(("parts", "reader"), "blk", "sub"), P(("parts", "blk", "reader"))),
        check_vma=False,
    )
```

```python
from functools import partial

import jax
import jax.numpy as jnp
from jax import lax
from jax.experimental import pallas as pl
from jax.experimental.pallas import tpu as pltpu
from jax.sharding import PartitionSpec as P

MESH = pl.DeviceIdType.MESH


def from_behind(block, axis, distance):
    devices = range(lax.axis_size(axis))
    route = [((i - distance) % len(devices), i) for i in devices]
    return lax.ppermute(block, axis, route)


def slot_positions(route_block):
    flat = route_block.reshape(-1)
    order = jnp.arange(flat.shape[0], dtype=jnp.int32)
    earlier = (order[None, :] < order[:, None]) & (flat[None, :] == flat[:, None])
    return jnp.sum(earlier.astype(jnp.int32), axis=1).reshape(route_block.shape)


def combine_stats(row_peaks, row_totals):
    highest = jnp.max(row_peaks, axis=-1)
    spread = row_totals * jnp.exp(row_peaks - highest[..., None])
    return highest + jnp.log(jnp.sum(spread, axis=-1))


def routed(images, routes, projections, noise_weights):
    groups = lax.axis_size("reader")
    cycle_size = lax.axis_size("blk")
    my_group = lax.axis_index("reader")
    my_member = lax.axis_index("blk")
    per_device, top_count = routes.shape
    half_width = images.shape[1]
    capacity = min(per_device, 2 * per_device * top_count // groups)
    slot_count = groups * capacity
    ref_count = projections.shape[1]
    all_refs = ref_count * cycle_size
    anchor = jnp.zeros((), jnp.int32)
    own_index = slot_positions(routes)
    own_target = routes * capacity + own_index
    sources = jnp.broadcast_to(jnp.arange(per_device, dtype=jnp.int32)[:, None], routes.shape)
    picker = (
        jnp.full((slot_count,), per_device, jnp.int32)
        .at[own_target.reshape(-1)]
        .set(sources.reshape(-1))
    )
    padded = jnp.concatenate([images, jnp.zeros((1, half_width), images.dtype)], axis=0)
    outgoing = padded[picker].reshape(groups, capacity, half_width)
    received = lax.all_to_all(outgoing, "reader", split_axis=0, concat_axis=0, tiled=True).reshape(
        slot_count, half_width
    )
    every_route = lax.all_gather(routes, "reader", axis=0, tiled=True).reshape(
        groups, per_device, top_count
    )
    every_index = jax.vmap(slot_positions)(every_route)
    senders = jnp.arange(groups, dtype=jnp.int32)[:, None, None]
    landing = jnp.where(every_route == my_group, senders * capacity + every_index, slot_count)
    live_slot = jnp.zeros((slot_count,), jnp.int32).at[landing.reshape(-1)].set(1, mode="drop") > 0

    def score_block(ref_block):
        scaled = ref_block.astype(jnp.float32) * noise_weights[None, :]
        weighted = scaled.astype(jnp.bfloat16)
        penalty = 0.5 * jnp.sum(scaled * ref_block.astype(jnp.float32), axis=1)
        partial_scores = lax.dot_general(
            weighted, received, (((1,), (1,)), ((), ())), preferred_element_type=jnp.float32
        )
        return partial_scores - penalty[:, None]

    def cycle_turn(rotation, carry):
        ref_block, score_table = carry
        position = (my_member - rotation) % cycle_size
        score_table = lax.dynamic_update_slice(
            score_table, score_block(ref_block)[None], (position, anchor, anchor)
        )
        ref_block = from_behind(ref_block, "blk", 1)
        return (ref_block, score_table)

    empty_table = jnp.zeros((cycle_size, ref_count, slot_count), jnp.float32)
    ref_block, score_table = lax.fori_loop(
        0, cycle_size - 1, cycle_turn, (projections[0], empty_table)
    )
    position = (my_member + 1) % cycle_size
    score_table = lax.dynamic_update_slice(
        score_table, score_block(ref_block)[None], (position, anchor, anchor)
    )
    score_table = lax.psum(score_table, "sub")
    scores = score_table.reshape(all_refs, slot_count)
    row_peak = jnp.max(scores, axis=0)
    row_total = jnp.sum(jnp.exp(scores - row_peak[None, :]), axis=0)
    back_peak, back_total = (
        lax.all_to_all(
            row_peak.reshape(groups, capacity), "reader", split_axis=0, concat_axis=0, tiled=True
        ),
        lax.all_to_all(
            row_total.reshape(groups, capacity), "reader", split_axis=0, concat_axis=0, tiled=True
        ),
    )
    normalizer = combine_stats(
        back_peak.reshape(-1)[own_target], back_total.reshape(-1)[own_target]
    )
    outgoing_norm = (
        jnp.zeros((slot_count,), jnp.float32)
        .at[own_target.reshape(-1)]
        .set(jnp.repeat(normalizer, top_count))
    )
    slot_norm = lax.all_to_all(
        outgoing_norm.reshape(groups, capacity), "reader", split_axis=0, concat_axis=0, tiled=True
    ).reshape(slot_count)
    exponent = jnp.where(live_slot[None, :], scores - slot_norm[None, :], -jnp.inf)
    posterior = jnp.exp(exponent).astype(jnp.bfloat16)
    summed = lax.psum_scatter(
        jnp.dot(posterior, received, preferred_element_type=jnp.float32).astype(jnp.bfloat16),
        "blk",
        scatter_dimension=0,
        tiled=True,
    ).astype(jnp.float32)
    return (summed[None], normalizer)


LOW = 3
CUTS = (3, 6, 8)


def paired(
    images, routes_in, proj, noise_in,
    out, norm,
    routes, noise, X, XF, PR, S, SC, SR, MOVE, SAME, SF, FR, QP, QO, QF, QT, QTF, PROD, TE, RE, TM, RM, TI, RI, O,
    loc, rt_snd, rt_rcv, px_snd, pb_snd, pm_snd, pc_snd, p_rcv, c_rcv, xx_snd, xc_snd, x_rcv, xf_snd, xfc_snd, xf_rcv,
    s_snd, s_rcv, f_snd, f_rcv, q_snd, q_rcv, qf_snd, qf_rcv, e_snd, e_rcv, m_snd, m_rcv, i_snd, i_rcv,
    own_snd, o_snd, o_rcv,
):
    r = lax.axis_index("reader")
    b = lax.axis_index("blk")
    x, c = r // 2, r % 2
    rx, rc = (r + 2) % 4, x * 2 + 1 - c
    rd = (rc + 2) % 4
    side = b // 2
    inner, end = 1 + side, 3 * side
    far_inner, far_end = 2 - side, 3 - 3 * side
    buddy, across = inner + end - b, 3 - b
    is_end = b == end
    is_inner = b == inner
    rows = images.shape[0]
    refs = proj.shape[0]
    H = X.shape[4 - 1]
    F = H // 2
    T, tile = O.shape[0], O.shape[3]
    TF = F // tile
    low = LOW * tile
    width = 4 * refs
    halves = (0, 1)
    pairs = (1 - side, side)
    marks = (0,) + CUTS
    whole = tuple((a * tile, (e - a) * tile) for a, e in zip(marks, CUTS))
    bits = range(len(CUTS))
    late = bits[1:]
    strips = ((0, low), (low, H - low))
    far_strips = ((0, low), (low, F - low))

    def remote(src, dst, snd, rcv, **where):
        return pltpu.make_async_remote_copy(
            src_ref=src, dst_ref=dst, send_sem=snd, recv_sem=rcv,
            device_id=where, device_id_type=MESH,
        )

    def arrived(dst, sem):
        remote(dst, dst, sem, sem, reader=rx).wait_recv()

    def left(src, sem):
        remote(src, src, sem, sem, reader=rx).wait_send()

    def columns(i, cut):
        return pl.ds(pl.multiple_of(i * H + cut[0], tile), cut[1])

    def part(src, g, cut):
        return PR.at[src, g, :, pl.ds(*cut)]

    def own_piece(h):
        return proj.at[:, columns(x, whole[h])]

    def proj_x(h):
        return remote(
            proj.at[:, columns(1 - x, whole[h])], part(b, r, whole[h]), px_snd.at[0], p_rcv.at[b, x, h], reader=rx
        )

    def stage(h):
        return h // (len(CUTS) - 1)

    def to_core(piece, src, g, h):
        late_one = is_end & (src != b) & (src != buddy)
        return remote(
            piece, part(src, g, whole[h]), pc_snd.at[late_one.astype(jnp.int32)], c_rcv.at[src, stage(h)], reader=rc
        )

    def to_buddy(piece, src, g, h):
        return remote(
            piece, part(src, g, whole[h]), pb_snd.at[(src != b).astype(jnp.int32)], p_rcv.at[src, g // 2, h], blk=buddy
        )

    def to_across(piece, src, g, h):
        return remote(piece, part(src, g, whole[h]), pm_snd.at[0], p_rcv.at[src, g // 2, h], blk=across)

    def image_x(h):
        return remote(
            images.at[:, columns(1 - x, strips[h])], X.at[c, x, :, pl.ds(*strips[h])],
            xx_snd.at[0], x_rcv.at[h], reader=rx,
        )

    def own_image_core():
        return remote(
            images.at[:, pl.ds(pl.multiple_of(x * H, H), H)], X.at[c, x],
            xc_snd.at[0], x_rcv.at[2], reader=rc,
        )

    def other_image_core():
        return remote(X.at[c, 1 - x], X.at[c, 1 - x], xc_snd.at[0], x_rcv.at[2], reader=rc)

    def own_far(h):
        return remote(
            images.at[:, columns(x, far_strips[h])], XF.at[c, x, :, pl.ds(*far_strips[h])],
            xf_snd.at[0], xf_rcv.at[h], blk=buddy,
        )

    def other_far(h):
        return remote(
            X.at[c, 1 - x, :, pl.ds(*far_strips[h])], XF.at[c, 1 - x, :, pl.ds(*far_strips[h])],
            xf_snd.at[0], xf_rcv.at[h], blk=buddy,
        )

    def far_core(i):
        return remote(XF.at[c, i], XF.at[c, i], xfc_snd.at[0], xf_rcv.at[2], reader=rc)

    def score_copy(q):
        return remote(SC.at[q], SR.at[q], s_snd.at[0], s_rcv.at[q], reader=rx)

    def routes_x():
        return remote(routes_in, routes.at[x], rt_snd.at[0], rt_rcv.at[0], reader=rx)

    def far_score(k, i):
        if i == 0:
            return remote(SF.at[k, x], FR.at[k, x], f_snd.at[0], f_rcv.at[0], blk=buddy)
        return remote(SF.at[k, 1 - x], FR.at[k, x], f_snd.at[0], f_rcv.at[0], blk=buddy, reader=rx)

    def post_copy(k, p):
        source, to = ((QP.at[p, c, x], rx), (QO.at[p], rc), (QO.at[p], rd))[k]
        return remote(source, QP.at[p, c, x], q_snd.at[k % 2], q_rcv.at[c, x, p], reader=to)

    def post_far(i, j, p):
        return remote(QP.at[p, i, j], QF.at[p, i, j], qf_snd.at[0], qf_rcv.at[p], blk=buddy)

    def end_copy(k, t):
        return remote(TE.at[k, t], RE.at[k, t], e_snd.at[0], e_rcv.at[k, t], blk=buddy)

    def middle_copy(k, t):
        return remote(TM.at[k, t], RM.at[k, t], m_snd.at[0], m_rcv.at[k, t], blk=across)

    def inner_copy(t):
        return remote(TI.at[t], RI.at[t], i_snd.at[0], i_rcv.at[t], blk=buddy)

    def out_span(i, t):
        return out.at[:, pl.ds(pl.multiple_of(i * H + t * tile, tile), tile)]

    def out_x(src, t):
        return remote(src.at[t, 1 - x], out_span(x, t), o_snd.at[0], o_rcv.at[0], reader=rx)

    def out_own(src, t):
        return pltpu.make_async_copy(src.at[t, x], out_span(x, t), own_snd.at[0])

    own_proj = pltpu.make_async_copy(proj.at[:, pl.ds(pl.multiple_of(x * H, H), H)], PR.at[b, r], loc.at[0])
    own_image = pltpu.make_async_copy(
        images.at[:, pl.ds(pl.multiple_of(x * H, H), H)], X.at[c, x], loc.at[1]
    )
    noise_copy = pltpu.make_async_copy(
        noise_in.at[pl.ds(pl.multiple_of(x * H, H), H)], noise, loc.at[2]
    )
    routes_copy = pltpu.make_async_copy(routes_in, routes.at[x], loc.at[3])

    barrier = pltpu.get_barrier_semaphore()
    for k in (rx, rc, rd):
        pl.semaphore_signal(barrier, inc=1, device_id={"reader": k}, device_id_type=MESH)
    pl.semaphore_signal(barrier, inc=1, device_id={"blk": buddy}, device_id_type=MESH)
    pl.semaphore_signal(barrier, inc=1, device_id={"blk": buddy, "reader": rx}, device_id_type=MESH)

    @pl.when(is_inner)
    def _():
        pl.semaphore_signal(barrier, inc=1, device_id={"blk": across}, device_id_type=MESH)

    own_proj.start()
    own_image.start()
    noise_copy.start()
    routes_copy.start()
    pl.semaphore_wait(barrier, 5 + is_inner.astype(jnp.int32))

    def spread(piece, g, h):
        to_buddy(piece, b, g, h).start()

        @pl.when(is_inner)
        def _():
            to_across(piece, b, g, h).start()

    routes_x().start()
    for h in bits:
        proj_x(h).start()
        spread(own_piece(h), r, h)
    for h in bits:
        to_core(own_piece(h), b, r, h).start()
    for h in bits:
        piece = part(b, rx, whole[h])
        arrived(piece, p_rcv.at[b, 1 - x, h])
        spread(piece, rx, h)
        to_core(piece, b, rx, h).start()
        if h == 0:
            for k in halves:
                image_x(k).start()
    own_image_core().start()

    late_pieces = tuple((g, h) for g in (r, rx) for h in late)
    pieces = tuple((g, h) for g in (r, rx) for h in bits)

    def other_image(h):
        arrived(X.at[c, 1 - x, :, pl.ds(*strips[h])], x_rcv.at[h])

    def hand_over(src, g, h):
        piece = part(src, g, whole[h])
        arrived(piece, p_rcv.at[src, g // 2, h])
        to_core(piece, src, g, h).start()

    @pl.when(is_end)
    def _():
        for g, h in pieces[:4]:
            hand_over(buddy, g, h)
        own_far(0).start()
        for g, h in pieces[4:]:
            hand_over(buddy, g, h)
        other_image(0)
        other_far(0).start()
        for g, h in late_pieces:
            hand_over(far_inner, g, h)
        other_image(1)
        for g, h in late_pieces[:-2]:
            hand_over(far_end, g, h)

    @pl.when(is_inner)
    def _():
        for g, h in pieces:
            arrived(part(far_inner, g, whole[h]), p_rcv.at[far_inner, g // 2, h])
            if h > 0:
                to_buddy(part(far_inner, g, whole[h]), far_inner, g, h).start()
            to_core(part(far_inner, g, whole[h]), far_inner, g, h).start()
            arrived(part(buddy, g, whole[h]), p_rcv.at[buddy, g // 2, h])
            to_across(part(buddy, g, whole[h]), buddy, g, h).start()
            to_core(part(buddy, g, whole[h]), buddy, g, h).start()
        for g, h in pieces:
            arrived(part(far_end, g, whole[h]), p_rcv.at[far_end, g // 2, h])
            if h > 0:
                to_buddy(part(far_end, g, whole[h]), far_end, g, h).start()
            to_core(part(far_end, g, whole[h]), far_end, g, h).start()
        for h in halves:
            other_image(h)

    other_image_core().start()
    own_proj.wait()
    own_image.wait()
    noise_copy.wait()
    routes_copy.wait()

    arrived(routes.at[1 - x], rt_rcv.at[0])
    lane = lax.broadcasted_iota(jnp.int32, (rows, width), 1)
    block = lane // refs
    diagonal = lax.broadcasted_iota(jnp.int32, (rows, rows), 0) == lax.broadcasted_iota(
        jnp.int32, (rows, rows), 1
    )

    def column(row):
        return jnp.sum(jnp.where(diagonal, row, 0.0), axis=1, keepdims=True).astype(jnp.int32)

    for i in range(2):
        names = routes[i].astype(jnp.float32)
        first, second = column(names[0:1]), column(names[1:2])
        MOVE[i] = (block - jnp.where(block < 2, first, second) + 4) % 4
        @pl.when(i == x)
        def _():
            SAME[0] = jnp.where(block < 2, first, second)
            SAME[1] = jnp.where(block < 2, second, first)

    def packed(p, i):
        even = block % 2 == 0
        low, high, move = S[2 * p, i], S[2 * p + 1, i], MOVE[i]
        total = jnp.where(even, low, high)
        for m in range(1, 4):
            turned_by = jnp.where(even, pltpu.roll(low, m * refs, 1), pltpu.roll(high, m * refs, 1))
            total = jnp.where(move == m, turned_by, total)
        return total

    square = lax.broadcasted_iota(jnp.int32, (width, width), 0) == lax.broadcasted_iota(
        jnp.int32, (width, width), 1
    )

    def scores_of(block, src, tiles):
        scores = jnp.zeros((2 * rows, width), jnp.float32)
        penalty = jnp.zeros((width, 128), jnp.float32)
        for t in tiles:
            cut = pl.ds(t * tile, tile)
            refs_f = PR[src, :, :, cut].reshape(width, tile).astype(jnp.float32)
            scaled = refs_f * noise[cut][None, :]
            scores = scores + lax.dot_general(
                block[c, :, :, cut].reshape(2 * rows, tile), scaled.astype(jnp.bfloat16),
                (((1,), (1,)), ((), ())), preferred_element_type=jnp.float32,
            )
            squares = scaled * refs_f
            for lane in range(0, tile, 128):
                penalty = penalty + squares[:, lane : lane + 128]
        lanes = jnp.sum(penalty, axis=1, keepdims=True)
        penalty_row = 0.5 * jnp.sum(jnp.where(square, lanes, 0.0), axis=0, keepdims=True)
        return (scores - penalty_row).reshape(2, rows, width)

    def from_core(src, n, first):
        start = marks[first]
        both = PR.at[src, pl.ds(0, 2), :, pl.ds(start * tile, (CUTS[-2 + n] - start) * tile)]
        arrived(both, c_rcv.at[src, n])

    @pl.when(is_inner)
    def _():
        arrived(XF.at[c, :, :, pl.ds(*far_strips[0])], xf_rcv.at[0])

        def far_source(k, carry):
            src = jnp.where(k == 0, far_inner, far_end)
            from_core(src, 0, 0)
            from_core(src, 1, len(CUTS) - 1)
            SF[k] = scores_of(XF, src, range(LOW))
            for i in (1, 0):
                far_score(k, i).start()
            return carry

        lax.fori_loop(0, 2, far_source, 0)

    def score_source(i, carry):
        src = jnp.where(i == 0, b, jnp.where(i == 1, buddy, jnp.where(i == 2, far_inner, far_end)))

        @pl.when(i < 2)
        def _():
            from_core(src, 0, 0)
            from_core(src, 1, len(CUTS) - 1)

        @pl.when((i < 2) | is_inner)
        def _():
            S[src] = scores_of(X, src, range(T))

        @pl.when((i >= 2) & is_end)
        def _():
            @pl.when(i == 3)
            def _():
                hand_over(src, *late_pieces[-2])

            from_core(src, 0, 1)
            S[src] = scores_of(X, src, range(LOW, CUTS[-2]))

            @pl.when(i == 3)
            def _():
                hand_over(src, *late_pieces[-1])

            from_core(src, 1, len(CUTS) - 1)
            S[src] = S[src] + scores_of(X, src, range(CUTS[-2], T))

        @pl.when(i % 2 == 1)
        def _():
            q = i // 2
            SC[q] = packed(side + q * (1 - 2 * side), 1 - x)
            score_copy(q).start()

        return carry

    lax.fori_loop(0, 4, score_source, 0)

    @pl.when(is_end)
    def _():
        own_far(1).start()
        other_far(1).start()
        arrived(FR, f_rcv.at[0])
        for k, src in enumerate((far_inner, far_end)):
            S[src, x] = S[src, x] + FR[k, 0] + FR[k, 1]

    chunks = []
    for q, p in enumerate(pairs):
        arrived(SR.at[1 - q], s_rcv.at[1 - q])
        chunks.append(packed(p, x) + SR[1 - q])
    highest = jnp.max(jnp.maximum(chunks[0], chunks[1]), axis=1, keepdims=True)
    total = jnp.exp(chunks[0] - highest) + jnp.exp(chunks[1] - highest)
    normalizer = highest + jnp.log(jnp.sum(total, axis=1, keepdims=True))
    norm[...] = jnp.sum(jnp.where(diagonal, normalizer, 0.0), axis=0, keepdims=True)

    def for_core(value, core):
        group = core + 2 * (lane // (2 * refs))
        swapped = jnp.where(SAME[1] == group, pltpu.roll(value, 2 * refs, 1), 0.0)
        return jnp.where(SAME[0] == group, value, swapped).astype(jnp.bfloat16)

    for q, p in enumerate(pairs):
        value = jnp.exp(chunks[q] - normalizer)
        QP[p, c, x] = for_core(value, c)
        QO[p] = for_core(value, 1 - c)
        for k in (0, 2, 1):
            post_copy(k, p).start()

        @pl.when(is_end)
        def _():
            post_far(c, x, p).start()

    for p in pairs:
        for i, j in ((1 - c, x), (c, 1 - x), (1 - c, 1 - x)):
            arrived(QP.at[p, i, j], q_rcv.at[i, j, p])

            @pl.when(is_end)
            def _():
                post_far(i, j, p).start()

    left(PR.at[0, 0], px_snd.at[0])
    left(X.at[0, 0], xx_snd.at[0])
    left(X.at[0], xc_snd.at[0])
    left(SC, s_snd.at[0])
    routes_x().wait_send()
    late_columns = pl.ds(low, H - low)
    left(PR.at[0, pl.ds(0, 2)], pb_snd.at[0])

    @pl.when(is_end)
    def _():
        left(PR.at[pl.ds(0, 2), pl.ds(0, 2)], pc_snd.at[0])
        left(PR.at[pl.ds(0, 2), pl.ds(0, 2), :, late_columns], pc_snd.at[1])

    @pl.when(is_inner)
    def _():
        left(PR.at[:, pl.ds(0, 2)], pc_snd.at[0])
        left(PR.at[pl.ds(0, 2), pl.ds(0, 2), :, late_columns], pb_snd.at[1])
        left(PR.at[pl.ds(0, 2), pl.ds(0, 2)], pm_snd.at[0])

    def turned(block):
        flat = block.reshape(4 * rows, width).astype(jnp.float32)
        return flat.T.astype(jnp.bfloat16)

    for p in halves:
        QT[p] = turned(QP[p])
    arrived(X.at[1 - c], x_rcv.at[2])

    def product(left, right):
        return lax.dot_general(
            left, right.reshape(4 * rows, tile), (((1,), (0,)), ((), ())), preferred_element_type=jnp.float32
        )

    def span(t):
        return pl.ds(pl.multiple_of(t * tile, tile), tile)

    def multiply(q, t, both):
        total = product(QT[pairs[q]], X[:, :, :, span(t)])
        if both:
            total = total + product(QTF[pairs[q]], XF[:, :, :, span(t)])
        PROD[t, q] = total.reshape(2, 2, refs, tile)

    def own(t, q, d):
        return PROD[t, q, :, d % 2]

    def f32(value):
        return value.astype(jnp.float32)

    @pl.when(is_end)
    def _():
        def send(t, carry):
            for k, q, d in ((1, 0, far_end), (0, 0, far_inner), (2, 1, inner)):
                if k != 0:
                    multiply(q, t, False)
                TE[k, t - TF] = own(t, q, d).astype(jnp.bfloat16)
                end_copy(k, t - TF).start()
            return carry

        def pass_on(t, carry):
            arrived(RI.at[t], i_rcv.at[t])
            out_x(RI, t).start()
            out_own(RI, t).start()
            return carry

        def finish(t, carry):
            arrived(RI.at[t], i_rcv.at[t])
            O[t] = (own(t, 1, end) + f32(RI[t])).astype(jnp.bfloat16)
            out_x(O, t).start()
            out_own(O, t).start()
            return carry

        left(QP, qf_snd.at[0])
        lax.fori_loop(TF, T, send, 0)
        lax.fori_loop(0, TF, pass_on, 0)
        lax.fori_loop(TF, T, finish, 0)

    @pl.when(is_inner)
    def _():
        arrived(XF.at[c, :, :, pl.ds(*far_strips[1])], xf_rcv.at[1])
        for i in range(2):
            far_core(i).start()
        arrived(XF.at[1 - c], xf_rcv.at[2])

        def far_posterior(q):
            p = pairs[q]
            arrived(QF.at[p], qf_rcv.at[p])
            QTF[p] = turned(QF[p])

        def multiply_any(q, t):
            @pl.when(t < TF)
            def _():
                multiply(q, t, True)

            @pl.when(t >= TF)
            def _():
                multiply(q, t, False)

        far_posterior(0)

        def outward(k, d, t):
            @pl.when(t < TF)
            def _():
                TM[k, t] = own(t, 0, d).astype(jnp.bfloat16)

            @pl.when(t >= TF)
            def _():
                arrived(RE.at[k, t - TF], e_rcv.at[k, t - TF])
                TM[k, t] = (own(t, 0, d) + f32(RE[k, t - TF])).astype(jnp.bfloat16)

            middle_copy(k, t).start()

        def turn(t, carry):
            @pl.when(t < T)
            def _():
                multiply_any(0, t)
                outward(1, far_end, t)

            @pl.when((t >= 2) & (t < T + 2))
            def _():
                outward(0, far_inner, t - 2)

            @pl.when(t == 1)
            def _():
                far_posterior(1)

            @pl.when((t >= 1) & (t < T + 1))
            def _():
                multiply_any(1, t - 1)

            @pl.when((t >= 2) & (t < T + 2))
            def _():
                n = t - 2
                arrived(RM.at[1, n], m_rcv.at[1, n])
                TI[n] = (own(n, 1, end) + f32(RM[1, n])).astype(jnp.bfloat16)
                inner_copy(n).start()

            @pl.when(t >= 4)
            def _():
                n = t - 4
                arrived(RM.at[0, n], m_rcv.at[0, n])
                total = own(n, 1, inner) + f32(RM[0, n])

                @pl.when(n < TF)
                def _():
                    O[n] = total.astype(jnp.bfloat16)

                @pl.when(n >= TF)
                def _():
                    arrived(RE.at[2, n - TF], e_rcv.at[2, n - TF])
                    O[n] = (total + f32(RE[2, n - TF])).astype(jnp.bfloat16)

                out_x(O, n).start()
                out_own(O, n).start()

            return carry

        lax.fori_loop(0, T + 4, turn, 0)

    left(QP.at[0], q_snd.at[0])
    left(QP.at[0, 0], q_snd.at[1])

    @pl.when(is_end)
    def _():
        left(XF.at[0], xf_snd.at[0])
        left(TE, e_snd.at[0])

    @pl.when(is_inner)
    def _():
        left(XF.at[0], xfc_snd.at[0])
        left(SF, f_snd.at[0])
        left(TM, m_snd.at[0])
        left(TI, i_snd.at[0])

    left(O.at[:, 0], o_snd.at[0])
    pltpu.make_async_copy(O.at[:, 0], O.at[:, 0], own_snd.at[0]).wait()
    arrived(out.at[:, pl.ds(pl.multiple_of((1 - x) * H, H), H)], o_rcv.at[0])


def hand_out(sums_in, norm_in, sums_out, norm_out):
    sums_out[...] = sums_in[...].astype(jnp.float32)
    norm_out[...] = norm_in[...]


def paired_halves(images, routes, projections, noise_weights):
    rows, coef = images.shape
    refs = projections.shape[1]
    H, width = coef // 2, 4 * refs
    F = H // 2
    T, TF = 8, 4
    tile = H // T
    TN = T - TF
    dma = pltpu.SemaphoreType.DMA
    bf16, f32 = jnp.bfloat16, jnp.float32
    piece = (2, refs, tile)
    sums, norm = pl.pallas_call(
        paired,
        out_shape=(
            jax.ShapeDtypeStruct((refs, coef), bf16),
            jax.ShapeDtypeStruct((1, rows), f32),
        ),
        in_specs=[pl.BlockSpec(memory_space=pltpu.HBM)] * 4,
        out_specs=(
            pl.BlockSpec(memory_space=pl.ANY),
            pl.BlockSpec(memory_space=pltpu.VMEM),
        ),
        scratch_shapes=[
            pltpu.VMEM((2, 2, rows), jnp.int32),
            pltpu.VMEM((H,), f32),
            pltpu.VMEM((2, 2, rows, H), bf16),
            pltpu.VMEM((2, 2, rows, F), bf16),
            pltpu.VMEM((4, 4, refs, H), bf16),
            pltpu.VMEM((4, 2, rows, width), f32),
            pltpu.VMEM((2, rows, width), f32),
            pltpu.VMEM((2, rows, width), f32),
            pltpu.VMEM((2, rows, width), jnp.int32),
            pltpu.VMEM((2, rows, width), jnp.int32),
            pltpu.VMEM((2, 2, rows, width), f32),
            pltpu.VMEM((2, 2, rows, width), f32),
            pltpu.VMEM((2, 2, 2, rows, width), bf16),
            pltpu.VMEM((2, rows, width), bf16),
            pltpu.VMEM((2, 2, 2, rows, width), bf16),
            pltpu.VMEM((2, width, 4 * rows), bf16),
            pltpu.VMEM((2, width, 4 * rows), bf16),
            pltpu.VMEM((T, 2, 2, 2, refs, tile), f32),
            pltpu.VMEM((3, TN) + piece, bf16),
            pltpu.VMEM((3, TN) + piece, bf16),
            pltpu.VMEM((2, T) + piece, bf16),
            pltpu.VMEM((2, T) + piece, bf16),
            pltpu.VMEM((T,) + piece, bf16),
            pltpu.VMEM((T,) + piece, bf16),
            pltpu.VMEM((T,) + piece, bf16),
            dma((4,)), dma((1,)), dma((1,)), dma((1,)), dma((2,)), dma((1,)), dma((2,)),
            dma((4, 2, len(CUTS))), dma((4, 2)), dma((1,)), dma((1,)), dma((3,)), dma((1,)), dma((1,)), dma((3,)),
            dma((1,)), dma((2,)), dma((1,)), dma((1,)), dma((2,)), dma((2, 2, 2)), dma((1,)), dma((2,)),
            dma((1,)), dma((3, TN)), dma((1,)), dma((2, T)), dma((1,)), dma((T,)),
            dma((1,)), dma((1,)), dma((1,)),
        ],
        compiler_params=pltpu.CompilerParams(
            collective_id=0, has_side_effects=True, vmem_limit_bytes=64 * 1024 * 1024 - 65536
        ),
        cost_estimate=pl.CostEstimate(
            flops=4 * 4 * rows * 4 * width * H // 2, bytes_accessed=4 * rows * coef, transcendentals=0
        ),
    )(images, routes.T, projections[0], noise_weights)
    block = coef // 2
    sums, norm = pl.pallas_call(
        hand_out,
        grid=(coef // block,),
        out_shape=(jax.ShapeDtypeStruct((refs, coef), f32), jax.ShapeDtypeStruct((1, rows), f32)),
        in_specs=[pl.BlockSpec((refs, block), lambda i: (0, i)), pl.BlockSpec((1, rows), lambda i: (0, 0))],
        out_specs=(pl.BlockSpec((refs, block), lambda i: (0, i)), pl.BlockSpec((1, rows), lambda i: (0, 0))),
    )(sums, norm)
    return (sums[None], norm[0])


def solution(mesh):
    sizes = dict(mesh.shape)
    direct = sizes["sub"] == 1 and sizes["reader"] == 4 and sizes["blk"] == 4
    return jax.shard_map(
        paired_halves if direct else routed,
        mesh=mesh,
        in_specs=(
            P(("parts", "blk", "reader"), "sub"),
            P(("parts", "blk", "reader"), None),
            P(("parts", "reader"), "blk", "sub"),
            P(("parts", "sub")),
        ),
        out_specs=(P(("parts", "reader"), "blk", "sub"), P(("parts", "blk", "reader"))),
        check_vma=False,
    )
```

```python
from functools import partial

import jax
import jax.numpy as jnp
from jax import lax
from jax.experimental import pallas as pl
from jax.experimental.pallas import tpu as pltpu
from jax.sharding import PartitionSpec as P

MESH = pl.DeviceIdType.MESH


def from_behind(block, axis, distance):
    devices = range(lax.axis_size(axis))
    route = [((i - distance) % len(devices), i) for i in devices]
    return lax.ppermute(block, axis, route)


def slot_positions(route_block):
    flat = route_block.reshape(-1)
    order = jnp.arange(flat.shape[0], dtype=jnp.int32)
    earlier = (order[None, :] < order[:, None]) & (flat[None, :] == flat[:, None])
    return jnp.sum(earlier.astype(jnp.int32), axis=1).reshape(route_block.shape)


def combine_stats(row_peaks, row_totals):
    highest = jnp.max(row_peaks, axis=-1)
    spread = row_totals * jnp.exp(row_peaks - highest[..., None])
    return highest + jnp.log(jnp.sum(spread, axis=-1))


def routed(images, routes, projections, noise_weights):
    groups = lax.axis_size("reader")
    cycle_size = lax.axis_size("blk")
    my_group = lax.axis_index("reader")
    my_member = lax.axis_index("blk")
    per_device, top_count = routes.shape
    half_width = images.shape[1]
    capacity = min(per_device, 2 * per_device * top_count // groups)
    slot_count = groups * capacity
    ref_count = projections.shape[1]
    all_refs = ref_count * cycle_size
    anchor = jnp.zeros((), jnp.int32)
    own_index = slot_positions(routes)
    own_target = routes * capacity + own_index
    sources = jnp.broadcast_to(jnp.arange(per_device, dtype=jnp.int32)[:, None], routes.shape)
    picker = (
        jnp.full((slot_count,), per_device, jnp.int32)
        .at[own_target.reshape(-1)]
        .set(sources.reshape(-1))
    )
    padded = jnp.concatenate([images, jnp.zeros((1, half_width), images.dtype)], axis=0)
    outgoing = padded[picker].reshape(groups, capacity, half_width)
    received = lax.all_to_all(outgoing, "reader", split_axis=0, concat_axis=0, tiled=True).reshape(
        slot_count, half_width
    )
    every_route = lax.all_gather(routes, "reader", axis=0, tiled=True).reshape(
        groups, per_device, top_count
    )
    every_index = jax.vmap(slot_positions)(every_route)
    senders = jnp.arange(groups, dtype=jnp.int32)[:, None, None]
    landing = jnp.where(every_route == my_group, senders * capacity + every_index, slot_count)
    live_slot = jnp.zeros((slot_count,), jnp.int32).at[landing.reshape(-1)].set(1, mode="drop") > 0

    def score_block(ref_block):
        scaled = ref_block.astype(jnp.float32) * noise_weights[None, :]
        weighted = scaled.astype(jnp.bfloat16)
        penalty = 0.5 * jnp.sum(scaled * ref_block.astype(jnp.float32), axis=1)
        partial_scores = lax.dot_general(
            weighted, received, (((1,), (1,)), ((), ())), preferred_element_type=jnp.float32
        )
        return partial_scores - penalty[:, None]

    def cycle_turn(rotation, carry):
        ref_block, score_table = carry
        position = (my_member - rotation) % cycle_size
        score_table = lax.dynamic_update_slice(
            score_table, score_block(ref_block)[None], (position, anchor, anchor)
        )
        ref_block = from_behind(ref_block, "blk", 1)
        return (ref_block, score_table)

    empty_table = jnp.zeros((cycle_size, ref_count, slot_count), jnp.float32)
    ref_block, score_table = lax.fori_loop(
        0, cycle_size - 1, cycle_turn, (projections[0], empty_table)
    )
    position = (my_member + 1) % cycle_size
    score_table = lax.dynamic_update_slice(
        score_table, score_block(ref_block)[None], (position, anchor, anchor)
    )
    score_table = lax.psum(score_table, "sub")
    scores = score_table.reshape(all_refs, slot_count)
    row_peak = jnp.max(scores, axis=0)
    row_total = jnp.sum(jnp.exp(scores - row_peak[None, :]), axis=0)
    back_peak, back_total = (
        lax.all_to_all(
            row_peak.reshape(groups, capacity), "reader", split_axis=0, concat_axis=0, tiled=True
        ),
        lax.all_to_all(
            row_total.reshape(groups, capacity), "reader", split_axis=0, concat_axis=0, tiled=True
        ),
    )
    normalizer = combine_stats(
        back_peak.reshape(-1)[own_target], back_total.reshape(-1)[own_target]
    )
    outgoing_norm = (
        jnp.zeros((slot_count,), jnp.float32)
        .at[own_target.reshape(-1)]
        .set(jnp.repeat(normalizer, top_count))
    )
    slot_norm = lax.all_to_all(
        outgoing_norm.reshape(groups, capacity), "reader", split_axis=0, concat_axis=0, tiled=True
    ).reshape(slot_count)
    exponent = jnp.where(live_slot[None, :], scores - slot_norm[None, :], -jnp.inf)
    posterior = jnp.exp(exponent).astype(jnp.bfloat16)
    summed = lax.psum_scatter(
        jnp.dot(posterior, received, preferred_element_type=jnp.float32).astype(jnp.bfloat16),
        "blk",
        scatter_dimension=0,
        tiled=True,
    ).astype(jnp.float32)
    return (summed[None], normalizer)


LOW = 3
CUTS = (3, 6, 8)


def paired(
    images, routes_in, proj, noise_in,
    out, norm,
    routes, noise, X, XF, PR, S, SC, SR, MOVE, SAME, SF, FR, QP, QO, QF, QT, QTF, PROD, TE, RE, TM, RM, TI, RI, O,
    loc, rt_snd, rt_rcv, px_snd, pb_snd, pm_snd, pc_snd, p_rcv, c_rcv, xx_snd, xc_snd, x_rcv, xf_snd, xfc_snd, xf_rcv,
    s_snd, s_rcv, f_snd, f_rcv, q_snd, q_rcv, qf_snd, qf_rcv, e_snd, e_rcv, m_snd, m_rcv, i_snd, i_rcv,
    own_snd, o_snd, o_rcv,
):
    r = lax.axis_index("reader")
    b = lax.axis_index("blk")
    x, c = r // 2, r % 2
    rx, rc = (r + 2) % 4, x * 2 + 1 - c
    rd = (rc + 2) % 4
    side = b // 2
    inner, end = 1 + side, 3 * side
    far_inner, far_end = 2 - side, 3 - 3 * side
    buddy, across = inner + end - b, 3 - b
    is_end = b == end
    is_inner = b == inner
    rows = images.shape[0]
    refs = proj.shape[0]
    H = X.shape[4 - 1]
    F = H // 2
    T, tile = O.shape[0], O.shape[3]
    TF = F // tile
    low = LOW * tile
    width = 4 * refs
    halves = (0, 1)
    pairs = (1 - side, side)
    marks = (0,) + CUTS
    whole = tuple((a * tile, (e - a) * tile) for a, e in zip(marks, CUTS))
    bits = range(len(CUTS))
    late = bits[1:]
    strips = ((0, low), (low, H - low))
    far_strips = ((0, low), (low, F - low))

    def remote(src, dst, snd, rcv, **where):
        return pltpu.make_async_remote_copy(
            src_ref=src, dst_ref=dst, send_sem=snd, recv_sem=rcv,
            device_id=where, device_id_type=MESH,
        )

    def arrived(dst, sem):
        remote(dst, dst, sem, sem, reader=rx).wait_recv()

    def left(src, sem):
        remote(src, src, sem, sem, reader=rx).wait_send()

    def columns(i, cut):
        return pl.ds(pl.multiple_of(i * H + cut[0], tile), cut[1])

    def part(src, g, cut):
        return PR.at[src, g, :, pl.ds(*cut)]

    def own_piece(h):
        return proj.at[:, columns(x, whole[h])]

    def proj_x(h):
        return remote(
            proj.at[:, columns(1 - x, whole[h])], part(b, r, whole[h]), px_snd.at[0], p_rcv.at[b, x, h], reader=rx
        )

    def stage(h):
        return h // (len(CUTS) - 1)

    def to_core(piece, src, g, h):
        late_one = is_end & (src != b) & (src != buddy)
        return remote(
            piece, part(src, g, whole[h]), pc_snd.at[late_one.astype(jnp.int32)], c_rcv.at[src, stage(h)], reader=rc
        )

    def to_buddy(piece, src, g, h):
        return remote(
            piece, part(src, g, whole[h]), pb_snd.at[(src != b).astype(jnp.int32)], p_rcv.at[src, g // 2, h], blk=buddy
        )

    def to_across(piece, src, g, h):
        return remote(piece, part(src, g, whole[h]), pm_snd.at[0], p_rcv.at[src, g // 2, h], blk=across)

    def image_x(h):
        return remote(
            images.at[:, columns(1 - x, strips[h])], X.at[c, x, :, pl.ds(*strips[h])],
            xx_snd.at[0], x_rcv.at[h], reader=rx,
        )

    def own_image_core():
        return remote(
            images.at[:, pl.ds(pl.multiple_of(x * H, H), H)], X.at[c, x],
            xc_snd.at[0], x_rcv.at[2], reader=rc,
        )

    def other_image_core():
        return remote(X.at[c, 1 - x], X.at[c, 1 - x], xc_snd.at[0], x_rcv.at[2], reader=rc)

    def own_far(h):
        return remote(
            images.at[:, columns(x, far_strips[h])], XF.at[c, x, :, pl.ds(*far_strips[h])],
            xf_snd.at[0], xf_rcv.at[h], blk=buddy,
        )

    def other_far(h):
        return remote(
            X.at[c, 1 - x, :, pl.ds(*far_strips[h])], XF.at[c, 1 - x, :, pl.ds(*far_strips[h])],
            xf_snd.at[0], xf_rcv.at[h], blk=buddy,
        )

    def far_core(i):
        return remote(XF.at[c, i], XF.at[c, i], xfc_snd.at[0], xf_rcv.at[2], reader=rc)

    def score_copy(q):
        return remote(SC.at[q], SR.at[q], s_snd.at[0], s_rcv.at[q], reader=rx)

    def routes_x():
        return remote(routes_in, routes.at[x], rt_snd.at[0], rt_rcv.at[0], reader=rx)

    def far_score(k, i):
        if i == 0:
            return remote(SF.at[k, x], FR.at[k, x], f_snd.at[0], f_rcv.at[0], blk=buddy)
        return remote(SF.at[k, 1 - x], FR.at[k, x], f_snd.at[0], f_rcv.at[0], blk=buddy, reader=rx)

    def post_copy(k, p):
        source, to = ((QP.at[p, c, x], rx), (QO.at[p], rc), (QO.at[p], rd))[k]
        return remote(source, QP.at[p, c, x], q_snd.at[k % 2], q_rcv.at[c, x, p], reader=to)

    def post_far(i, j, p):
        return remote(QP.at[p, i, j], QF.at[p, i, j], qf_snd.at[0], qf_rcv.at[p], blk=buddy)

    def end_copy(k, t):
        return remote(TE.at[k, t], RE.at[k, t], e_snd.at[0], e_rcv.at[k, t], blk=buddy)

    def middle_copy(k, t):
        return remote(TM.at[k, t], RM.at[k, t], m_snd.at[0], m_rcv.at[k, t], blk=across)

    def inner_copy(t):
        return remote(TI.at[t], RI.at[t], i_snd.at[0], i_rcv.at[t], blk=buddy)

    def out_span(i, t):
        return out.at[:, pl.ds(pl.multiple_of(i * H + t * tile, tile), tile)]

    def out_x(src, t):
        return remote(src.at[t, 1 - x], out_span(x, t), o_snd.at[0], o_rcv.at[0], reader=rx)

    def out_own(src, t):
        return pltpu.make_async_copy(src.at[t, x], out_span(x, t), own_snd.at[0])

    own_proj = pltpu.make_async_copy(proj.at[:, pl.ds(pl.multiple_of(x * H, H), H)], PR.at[b, r], loc.at[0])
    own_image = pltpu.make_async_copy(
        images.at[:, pl.ds(pl.multiple_of(x * H, H), H)], X.at[c, x], loc.at[1]
    )
    noise_copy = pltpu.make_async_copy(
        noise_in.at[pl.ds(pl.multiple_of(x * H, H), H)], noise, loc.at[2]
    )
    routes_copy = pltpu.make_async_copy(routes_in, routes.at[x], loc.at[3])

    barrier = pltpu.get_barrier_semaphore()
    for k in (rx, rc, rd):
        pl.semaphore_signal(barrier, inc=1, device_id={"reader": k}, device_id_type=MESH)
    pl.semaphore_signal(barrier, inc=1, device_id={"blk": buddy}, device_id_type=MESH)
    pl.semaphore_signal(barrier, inc=1, device_id={"blk": buddy, "reader": rx}, device_id_type=MESH)

    @pl.when(is_inner)
    def _():
        pl.semaphore_signal(barrier, inc=1, device_id={"blk": across}, device_id_type=MESH)

    own_proj.start()
    own_image.start()
    noise_copy.start()
    routes_copy.start()
    pl.semaphore_wait(barrier, 5 + is_inner.astype(jnp.int32))

    def spread(piece, g, h):
        to_buddy(piece, b, g, h).start()

        @pl.when(is_inner)
        def _():
            to_across(piece, b, g, h).start()

    routes_x().start()
    for h in bits:
        proj_x(h).start()
        spread(own_piece(h), r, h)
    for h in bits:
        to_core(own_piece(h), b, r, h).start()
    for h in bits:
        piece = part(b, rx, whole[h])
        arrived(piece, p_rcv.at[b, 1 - x, h])
        spread(piece, rx, h)
        to_core(piece, b, rx, h).start()
        if h == 0:
            for k in halves:
                image_x(k).start()
    own_image_core().start()

    late_pieces = tuple((g, h) for g in (r, rx) for h in late)
    pieces = tuple((g, h) for g in (r, rx) for h in bits)

    def other_image(h):
        arrived(X.at[c, 1 - x, :, pl.ds(*strips[h])], x_rcv.at[h])

    def hand_over(src, g, h):
        piece = part(src, g, whole[h])
        arrived(piece, p_rcv.at[src, g // 2, h])
        to_core(piece, src, g, h).start()

    @pl.when(is_end)
    def _():
        for g, h in pieces[:4]:
            hand_over(buddy, g, h)
        own_far(0).start()
        for g, h in pieces[4:]:
            hand_over(buddy, g, h)
        other_image(0)
        other_far(0).start()
        for g, h in late_pieces:
            hand_over(far_inner, g, h)
        other_image(1)
        own_far(1).start()
        other_far(1).start()
        for g, h in late_pieces[:-2]:
            hand_over(far_end, g, h)

    @pl.when(is_inner)
    def _():
        for g, h in pieces:
            arrived(part(far_inner, g, whole[h]), p_rcv.at[far_inner, g // 2, h])
            if h > 0:
                to_buddy(part(far_inner, g, whole[h]), far_inner, g, h).start()
            to_core(part(far_inner, g, whole[h]), far_inner, g, h).start()
            arrived(part(buddy, g, whole[h]), p_rcv.at[buddy, g // 2, h])
            to_across(part(buddy, g, whole[h]), buddy, g, h).start()
            to_core(part(buddy, g, whole[h]), buddy, g, h).start()
        for g, h in pieces:
            arrived(part(far_end, g, whole[h]), p_rcv.at[far_end, g // 2, h])
            if h > 0:
                to_buddy(part(far_end, g, whole[h]), far_end, g, h).start()
            to_core(part(far_end, g, whole[h]), far_end, g, h).start()
        for h in halves:
            other_image(h)

    other_image_core().start()
    own_proj.wait()
    own_image.wait()
    noise_copy.wait()
    routes_copy.wait()

    arrived(routes.at[1 - x], rt_rcv.at[0])
    lane = lax.broadcasted_iota(jnp.int32, (rows, width), 1)
    block = lane // refs
    diagonal = lax.broadcasted_iota(jnp.int32, (rows, rows), 0) == lax.broadcasted_iota(
        jnp.int32, (rows, rows), 1
    )

    def column(row):
        return jnp.sum(jnp.where(diagonal, row, 0.0), axis=1, keepdims=True).astype(jnp.int32)

    for i in range(2):
        names = routes[i].astype(jnp.float32)
        first, second = column(names[0:1]), column(names[1:2])
        MOVE[i] = (block - jnp.where(block < 2, first, second) + 4) % 4
        @pl.when(i == x)
        def _():
            SAME[0] = jnp.where(block < 2, first, second)
            SAME[1] = jnp.where(block < 2, second, first)

    def packed(p, i):
        even = block % 2 == 0
        low, high, move = S[2 * p, i], S[2 * p + 1, i], MOVE[i]
        total = jnp.where(even, low, high)
        for m in range(1, 4):
            turned_by = jnp.where(even, pltpu.roll(low, m * refs, 1), pltpu.roll(high, m * refs, 1))
            total = jnp.where(move == m, turned_by, total)
        return total

    square = lax.broadcasted_iota(jnp.int32, (width, width), 0) == lax.broadcasted_iota(
        jnp.int32, (width, width), 1
    )

    def scores_of(block, src, tiles):
        scores = jnp.zeros((2 * rows, width), jnp.float32)
        penalty = jnp.zeros((width, 128), jnp.float32)
        for t in tiles:
            cut = pl.ds(t * tile, tile)
            refs_f = PR[src, :, :, cut].reshape(width, tile).astype(jnp.float32)
            scaled = refs_f * noise[cut][None, :]
            scores = scores + lax.dot_general(
                block[c, :, :, cut].reshape(2 * rows, tile), scaled.astype(jnp.bfloat16),
                (((1,), (1,)), ((), ())), preferred_element_type=jnp.float32,
            )
            squares = scaled * refs_f
            for lane in range(0, tile, 128):
                penalty = penalty + squares[:, lane : lane + 128]
        lanes = jnp.sum(penalty, axis=1, keepdims=True)
        penalty_row = 0.5 * jnp.sum(jnp.where(square, lanes, 0.0), axis=0, keepdims=True)
        return (scores - penalty_row).reshape(2, rows, width)

    def from_core(src, n, first):
        start = marks[first]
        both = PR.at[src, pl.ds(0, 2), :, pl.ds(start * tile, (CUTS[-2 + n] - start) * tile)]
        arrived(both, c_rcv.at[src, n])

    def score_source(i, carry):
        src = jnp.where(i == 0, b, jnp.where(i == 1, buddy, jnp.where(i == 2, far_inner, far_end)))

        @pl.when(i < 2)
        def _():
            from_core(src, 0, 0)
            from_core(src, 1, len(CUTS) - 1)

        @pl.when((i < 2) | is_inner)
        def _():
            S[src] = scores_of(X, src, range(T))

        @pl.when((i >= 2) & is_end)
        def _():
            @pl.when(i == 3)
            def _():
                hand_over(src, *late_pieces[-2])

            from_core(src, 0, 1)
            S[src] = scores_of(X, src, range(LOW, CUTS[-2]))

            @pl.when(i == 3)
            def _():
                hand_over(src, *late_pieces[-1])

            from_core(src, 1, len(CUTS) - 1)
            S[src] = S[src] + scores_of(X, src, range(CUTS[-2], T))

        @pl.when(i % 2 == 1)
        def _():
            q = i // 2
            SC[q] = packed(side + q * (1 - 2 * side), 1 - x)
            score_copy(q).start()

        return carry

    lax.fori_loop(0, 2, score_source, 0)
    @pl.when(is_inner)
    def _():
        arrived(XF.at[c, :, :, pl.ds(*far_strips[0])], xf_rcv.at[0])

        def far_source(k, carry):
            src = jnp.where(k == 0, far_inner, far_end)
            from_core(src, 0, 0)
            from_core(src, 1, len(CUTS) - 1)
            SF[k] = scores_of(XF, src, range(LOW))
            for i in (1, 0):
                far_score(k, i).start()
            return carry

        lax.fori_loop(0, 2, far_source, 0)

    lax.fori_loop(2, 4, score_source, 0)

    @pl.when(is_end)
    def _():
        arrived(FR, f_rcv.at[0])
        for k, src in enumerate((far_inner, far_end)):
            S[src, x] = S[src, x] + FR[k, 0] + FR[k, 1]

    chunks = []
    for q, p in enumerate(pairs):
        arrived(SR.at[1 - q], s_rcv.at[1 - q])
        chunks.append(packed(p, x) + SR[1 - q])
    highest = jnp.max(jnp.maximum(chunks[0], chunks[1]), axis=1, keepdims=True)
    total = jnp.exp(chunks[0] - highest) + jnp.exp(chunks[1] - highest)
    normalizer = highest + jnp.log(jnp.sum(total, axis=1, keepdims=True))
    norm[...] = jnp.sum(jnp.where(diagonal, normalizer, 0.0), axis=0, keepdims=True)

    def for_core(value, core):
        group = core + 2 * (lane // (2 * refs))
        swapped = jnp.where(SAME[1] == group, pltpu.roll(value, 2 * refs, 1), 0.0)
        return jnp.where(SAME[0] == group, value, swapped).astype(jnp.bfloat16)

    for q, p in enumerate(pairs):
        value = jnp.exp(chunks[q] - normalizer)
        QP[p, c, x] = for_core(value, c)
        QO[p] = for_core(value, 1 - c)
        for k in (0, 2, 1):
            post_copy(k, p).start()

        @pl.when(is_end)
        def _():
            post_far(c, x, p).start()

    for p in pairs:
        for i, j in ((1 - c, x), (c, 1 - x), (1 - c, 1 - x)):
            arrived(QP.at[p, i, j], q_rcv.at[i, j, p])

            @pl.when(is_end)
            def _():
                post_far(i, j, p).start()

    left(PR.at[0, 0], px_snd.at[0])
    left(X.at[0, 0], xx_snd.at[0])
    left(X.at[0], xc_snd.at[0])
    left(SC, s_snd.at[0])
    routes_x().wait_send()
    late_columns = pl.ds(low, H - low)
    left(PR.at[0, pl.ds(0, 2)], pb_snd.at[0])

    @pl.when(is_end)
    def _():
        left(PR.at[pl.ds(0, 2), pl.ds(0, 2)], pc_snd.at[0])
        left(PR.at[pl.ds(0, 2), pl.ds(0, 2), :, late_columns], pc_snd.at[1])

    @pl.when(is_inner)
    def _():
        left(PR.at[:, pl.ds(0, 2)], pc_snd.at[0])
        left(PR.at[pl.ds(0, 2), pl.ds(0, 2), :, late_columns], pb_snd.at[1])
        left(PR.at[pl.ds(0, 2), pl.ds(0, 2)], pm_snd.at[0])

    def turned(block):
        flat = block.reshape(4 * rows, width).astype(jnp.float32)
        return flat.T.astype(jnp.bfloat16)

    for p in halves:
        QT[p] = turned(QP[p])
    arrived(X.at[1 - c], x_rcv.at[2])

    def product(left, right):
        return lax.dot_general(
            left, right.reshape(4 * rows, tile), (((1,), (0,)), ((), ())), preferred_element_type=jnp.float32
        )

    def span(t):
        return pl.ds(pl.multiple_of(t * tile, tile), tile)

    def multiply(q, t, both):
        total = product(QT[pairs[q]], X[:, :, :, span(t)])
        if both:
            total = total + product(QTF[pairs[q]], XF[:, :, :, span(t)])
        PROD[t, q] = total.reshape(2, 2, refs, tile)

    def own(t, q, d):
        return PROD[t, q, :, d % 2]

    def f32(value):
        return value.astype(jnp.float32)

    @pl.when(is_end)
    def _():
        def send(k, q, d, t):
            TE[k, t - TF] = own(t, q, d).astype(jnp.bfloat16)
            end_copy(k, t - TF).start()

        def send_far(t, carry):
            multiply(0, t, False)
            send(1, 0, far_end, t)
            send(0, 0, far_inner, t)
            return carry

        def send_near(t, carry):
            multiply(1, t, False)
            send(2, 1, inner, t)
            return carry

        def pass_on(t, carry):
            arrived(RI.at[t], i_rcv.at[t])
            out_x(RI, t).start()
            out_own(RI, t).start()
            return carry

        def finish(t, carry):
            arrived(RI.at[t], i_rcv.at[t])
            O[t] = (own(t, 1, end) + f32(RI[t])).astype(jnp.bfloat16)
            out_x(O, t).start()
            out_own(O, t).start()
            return carry

        left(QP, qf_snd.at[0])
        lax.fori_loop(TF, T, send_far, 0)
        lax.fori_loop(TF, T, send_near, 0)
        lax.fori_loop(0, TF, pass_on, 0)
        lax.fori_loop(TF, T, finish, 0)

    @pl.when(is_inner)
    def _():
        arrived(XF.at[c, :, :, pl.ds(*far_strips[1])], xf_rcv.at[1])
        for i in range(2):
            far_core(i).start()
        arrived(XF.at[1 - c], xf_rcv.at[2])

        def far_posterior(q):
            p = pairs[q]
            arrived(QF.at[p], qf_rcv.at[p])
            QTF[p] = turned(QF[p])

        def multiply_any(q, t):
            @pl.when(t < TF)
            def _():
                multiply(q, t, True)

            @pl.when(t >= TF)
            def _():
                multiply(q, t, False)

        far_posterior(0)

        def outward(k, d, t):
            @pl.when(t < TF)
            def _():
                TM[k, t] = own(t, 0, d).astype(jnp.bfloat16)

            @pl.when(t >= TF)
            def _():
                arrived(RE.at[k, t - TF], e_rcv.at[k, t - TF])
                TM[k, t] = (own(t, 0, d) + f32(RE[k, t - TF])).astype(jnp.bfloat16)

            middle_copy(k, t).start()

        def turn(t, carry):
            @pl.when(t < T)
            def _():
                multiply_any(0, t)
                outward(1, far_end, t)

            @pl.when((t >= 3) & (t < T + 3))
            def _():
                outward(0, far_inner, t - 3)

            @pl.when(t == 1)
            def _():
                far_posterior(1)

            @pl.when((t >= 1) & (t < T + 1))
            def _():
                multiply_any(1, t - 1)

            @pl.when((t >= 2) & (t < T + 2))
            def _():
                n = t - 2
                arrived(RM.at[1, n], m_rcv.at[1, n])
                TI[n] = (own(n, 1, end) + f32(RM[1, n])).astype(jnp.bfloat16)
                inner_copy(n).start()

            @pl.when(t >= 5)
            def _():
                n = t - 5
                arrived(RM.at[0, n], m_rcv.at[0, n])
                total = own(n, 1, inner) + f32(RM[0, n])

                @pl.when(n < TF)
                def _():
                    O[n] = total.astype(jnp.bfloat16)

                @pl.when(n >= TF)
                def _():
                    arrived(RE.at[2, n - TF], e_rcv.at[2, n - TF])
                    O[n] = (total + f32(RE[2, n - TF])).astype(jnp.bfloat16)

                out_x(O, n).start()
                out_own(O, n).start()

            return carry

        lax.fori_loop(0, T + 5, turn, 0)

    left(QP.at[0], q_snd.at[0])
    left(QP.at[0, 0], q_snd.at[1])

    @pl.when(is_end)
    def _():
        left(XF.at[0], xf_snd.at[0])
        left(TE, e_snd.at[0])

    @pl.when(is_inner)
    def _():
        left(XF.at[0], xfc_snd.at[0])
        left(SF, f_snd.at[0])
        left(TM, m_snd.at[0])
        left(TI, i_snd.at[0])

    left(O.at[:, 0], o_snd.at[0])
    pltpu.make_async_copy(O.at[:, 0], O.at[:, 0], own_snd.at[0]).wait()
    arrived(out.at[:, pl.ds(pl.multiple_of((1 - x) * H, H), H)], o_rcv.at[0])


def hand_out(sums_in, norm_in, sums_out, norm_out):
    sums_out[...] = sums_in[...].astype(jnp.float32)
    norm_out[...] = norm_in[...]


def paired_halves(images, routes, projections, noise_weights):
    rows, coef = images.shape
    refs = projections.shape[1]
    H, width = coef // 2, 4 * refs
    F = H // 2
    T, TF = 8, 4
    tile = H // T
    TN = T - TF
    dma = pltpu.SemaphoreType.DMA
    bf16, f32 = jnp.bfloat16, jnp.float32
    piece = (2, refs, tile)
    sums, norm = pl.pallas_call(
        paired,
        out_shape=(
            jax.ShapeDtypeStruct((refs, coef), bf16),
            jax.ShapeDtypeStruct((1, rows), f32),
        ),
        in_specs=[pl.BlockSpec(memory_space=pltpu.HBM)] * 4,
        out_specs=(
            pl.BlockSpec(memory_space=pl.ANY),
            pl.BlockSpec(memory_space=pltpu.VMEM),
        ),
        scratch_shapes=[
            pltpu.VMEM((2, 2, rows), jnp.int32),
            pltpu.VMEM((H,), f32),
            pltpu.VMEM((2, 2, rows, H), bf16),
            pltpu.VMEM((2, 2, rows, F), bf16),
            pltpu.VMEM((4, 4, refs, H), bf16),
            pltpu.VMEM((4, 2, rows, width), f32),
            pltpu.VMEM((2, rows, width), f32),
            pltpu.VMEM((2, rows, width), f32),
            pltpu.VMEM((2, rows, width), jnp.int32),
            pltpu.VMEM((2, rows, width), jnp.int32),
            pltpu.VMEM((2, 2, rows, width), f32),
            pltpu.VMEM((2, 2, rows, width), f32),
            pltpu.VMEM((2, 2, 2, rows, width), bf16),
            pltpu.VMEM((2, rows, width), bf16),
            pltpu.VMEM((2, 2, 2, rows, width), bf16),
            pltpu.VMEM((2, width, 4 * rows), bf16),
            pltpu.VMEM((2, width, 4 * rows), bf16),
            pltpu.VMEM((T, 2, 2, 2, refs, tile), f32),
            pltpu.VMEM((3, TN) + piece, bf16),
            pltpu.VMEM((3, TN) + piece, bf16),
            pltpu.VMEM((2, T) + piece, bf16),
            pltpu.VMEM((2, T) + piece, bf16),
            pltpu.VMEM((T,) + piece, bf16),
            pltpu.VMEM((T,) + piece, bf16),
            pltpu.VMEM((T,) + piece, bf16),
            dma((4,)), dma((1,)), dma((1,)), dma((1,)), dma((2,)), dma((1,)), dma((2,)),
            dma((4, 2, len(CUTS))), dma((4, 2)), dma((1,)), dma((1,)), dma((3,)), dma((1,)), dma((1,)), dma((3,)),
            dma((1,)), dma((2,)), dma((1,)), dma((1,)), dma((2,)), dma((2, 2, 2)), dma((1,)), dma((2,)),
            dma((1,)), dma((3, TN)), dma((1,)), dma((2, T)), dma((1,)), dma((T,)),
            dma((1,)), dma((1,)), dma((1,)),
        ],
        compiler_params=pltpu.CompilerParams(
            collective_id=0, has_side_effects=True, vmem_limit_bytes=64 * 1024 * 1024 - 65536
        ),
        cost_estimate=pl.CostEstimate(
            flops=4 * 4 * rows * 4 * width * H // 2, bytes_accessed=4 * rows * coef, transcendentals=0
        ),
    )(images, routes.T, projections[0], noise_weights)
    block = coef // 2
    sums, norm = pl.pallas_call(
        hand_out,
        grid=(coef // block,),
        out_shape=(jax.ShapeDtypeStruct((refs, coef), f32), jax.ShapeDtypeStruct((1, rows), f32)),
        in_specs=[pl.BlockSpec((refs, block), lambda i: (0, i)), pl.BlockSpec((1, rows), lambda i: (0, 0))],
        out_specs=(pl.BlockSpec((refs, block), lambda i: (0, i)), pl.BlockSpec((1, rows), lambda i: (0, 0))),
    )(sums, norm)
    return (sums[None], norm[0])


def solution(mesh):
    sizes = dict(mesh.shape)
    direct = sizes["sub"] == 1 and sizes["reader"] == 4 and sizes["blk"] == 4
    return jax.shard_map(
        paired_halves if direct else routed,
        mesh=mesh,
        in_specs=(
            P(("parts", "blk", "reader"), "sub"),
            P(("parts", "blk", "reader"), None),
            P(("parts", "reader"), "blk", "sub"),
            P(("parts", "sub")),
        ),
        out_specs=(P(("parts", "reader"), "blk", "sub"), P(("parts", "blk", "reader"))),
        check_vma=False,
    )
```

```python
from functools import partial

import jax
import jax.numpy as jnp
from jax import lax
from jax.experimental import pallas as pl
from jax.experimental.pallas import tpu as pltpu
from jax.sharding import PartitionSpec as P

MESH = pl.DeviceIdType.MESH


def from_behind(block, axis, distance):
    devices = range(lax.axis_size(axis))
    route = [((i - distance) % len(devices), i) for i in devices]
    return lax.ppermute(block, axis, route)


def slot_positions(route_block):
    flat = route_block.reshape(-1)
    order = jnp.arange(flat.shape[0], dtype=jnp.int32)
    earlier = (order[None, :] < order[:, None]) & (flat[None, :] == flat[:, None])
    return jnp.sum(earlier.astype(jnp.int32), axis=1).reshape(route_block.shape)


def combine_stats(row_peaks, row_totals):
    highest = jnp.max(row_peaks, axis=-1)
    spread = row_totals * jnp.exp(row_peaks - highest[..., None])
    return highest + jnp.log(jnp.sum(spread, axis=-1))


def routed(images, routes, projections, noise_weights):
    groups = lax.axis_size("reader")
    cycle_size = lax.axis_size("blk")
    my_group = lax.axis_index("reader")
    my_member = lax.axis_index("blk")
    per_device, top_count = routes.shape
    half_width = images.shape[1]
    capacity = min(per_device, 2 * per_device * top_count // groups)
    slot_count = groups * capacity
    ref_count = projections.shape[1]
    all_refs = ref_count * cycle_size
    anchor = jnp.zeros((), jnp.int32)
    own_index = slot_positions(routes)
    own_target = routes * capacity + own_index
    sources = jnp.broadcast_to(jnp.arange(per_device, dtype=jnp.int32)[:, None], routes.shape)
    picker = (
        jnp.full((slot_count,), per_device, jnp.int32)
        .at[own_target.reshape(-1)]
        .set(sources.reshape(-1))
    )
    padded = jnp.concatenate([images, jnp.zeros((1, half_width), images.dtype)], axis=0)
    outgoing = padded[picker].reshape(groups, capacity, half_width)
    received = lax.all_to_all(outgoing, "reader", split_axis=0, concat_axis=0, tiled=True).reshape(
        slot_count, half_width
    )
    every_route = lax.all_gather(routes, "reader", axis=0, tiled=True).reshape(
        groups, per_device, top_count
    )
    every_index = jax.vmap(slot_positions)(every_route)
    senders = jnp.arange(groups, dtype=jnp.int32)[:, None, None]
    landing = jnp.where(every_route == my_group, senders * capacity + every_index, slot_count)
    live_slot = jnp.zeros((slot_count,), jnp.int32).at[landing.reshape(-1)].set(1, mode="drop") > 0

    def score_block(ref_block):
        scaled = ref_block.astype(jnp.float32) * noise_weights[None, :]
        weighted = scaled.astype(jnp.bfloat16)
        penalty = 0.5 * jnp.sum(scaled * ref_block.astype(jnp.float32), axis=1)
        partial_scores = lax.dot_general(
            weighted, received, (((1,), (1,)), ((), ())), preferred_element_type=jnp.float32
        )
        return partial_scores - penalty[:, None]

    def cycle_turn(rotation, carry):
        ref_block, score_table = carry
        position = (my_member - rotation) % cycle_size
        score_table = lax.dynamic_update_slice(
            score_table, score_block(ref_block)[None], (position, anchor, anchor)
        )
        ref_block = from_behind(ref_block, "blk", 1)
        return (ref_block, score_table)

    empty_table = jnp.zeros((cycle_size, ref_count, slot_count), jnp.float32)
    ref_block, score_table = lax.fori_loop(
        0, cycle_size - 1, cycle_turn, (projections[0], empty_table)
    )
    position = (my_member + 1) % cycle_size
    score_table = lax.dynamic_update_slice(
        score_table, score_block(ref_block)[None], (position, anchor, anchor)
    )
    score_table = lax.psum(score_table, "sub")
    scores = score_table.reshape(all_refs, slot_count)
    row_peak = jnp.max(scores, axis=0)
    row_total = jnp.sum(jnp.exp(scores - row_peak[None, :]), axis=0)
    back_peak, back_total = (
        lax.all_to_all(
            row_peak.reshape(groups, capacity), "reader", split_axis=0, concat_axis=0, tiled=True
        ),
        lax.all_to_all(
            row_total.reshape(groups, capacity), "reader", split_axis=0, concat_axis=0, tiled=True
        ),
    )
    normalizer = combine_stats(
        back_peak.reshape(-1)[own_target], back_total.reshape(-1)[own_target]
    )
    outgoing_norm = (
        jnp.zeros((slot_count,), jnp.float32)
        .at[own_target.reshape(-1)]
        .set(jnp.repeat(normalizer, top_count))
    )
    slot_norm = lax.all_to_all(
        outgoing_norm.reshape(groups, capacity), "reader", split_axis=0, concat_axis=0, tiled=True
    ).reshape(slot_count)
    exponent = jnp.where(live_slot[None, :], scores - slot_norm[None, :], -jnp.inf)
    posterior = jnp.exp(exponent).astype(jnp.bfloat16)
    summed = lax.psum_scatter(
        jnp.dot(posterior, received, preferred_element_type=jnp.float32).astype(jnp.bfloat16),
        "blk",
        scatter_dimension=0,
        tiled=True,
    ).astype(jnp.float32)
    return (summed[None], normalizer)


LOW = 3
CUTS = (3, 6, 8)


def paired(
    images, routes_in, proj, noise_in,
    out, norm,
    routes, noise, X, XF, PR, S, SC, SR, MOVE, SAME, SF, FR, QP, QO, QF, QT, QTF, PROD, TE, RE, TM, RM, TI, RI, O,
    loc, rt_snd, rt_rcv, px_snd, pb_snd, pm_snd, pc_snd, p_rcv, c_rcv, xx_snd, xc_snd, x_rcv, xf_snd, xfc_snd, xf_rcv,
    s_snd, s_rcv, f_snd, f_rcv, q_snd, q_rcv, qf_snd, qf_rcv, e_snd, e_rcv, m_snd, m_rcv, i_snd, i_rcv,
    own_snd, o_snd, o_rcv,
):
    r = lax.axis_index("reader")
    b = lax.axis_index("blk")
    x, c = r // 2, r % 2
    rx, rc = (r + 2) % 4, x * 2 + 1 - c
    rd = (rc + 2) % 4
    side = b // 2
    inner, end = 1 + side, 3 * side
    far_inner, far_end = 2 - side, 3 - 3 * side
    buddy, across = inner + end - b, 3 - b
    is_end = b == end
    is_inner = b == inner
    rows = images.shape[0]
    refs = proj.shape[0]
    H = X.shape[4 - 1]
    F = H // 2
    T, tile = O.shape[0], O.shape[3]
    TF = F // tile
    low = LOW * tile
    width = 4 * refs
    halves = (0, 1)
    pairs = (1 - side, side)
    marks = (0,) + CUTS
    whole = tuple((a * tile, (e - a) * tile) for a, e in zip(marks, CUTS))
    bits = range(len(CUTS))
    late = bits[1:]
    strips = ((0, low), (low, H - low))
    far_strips = ((0, low), (low, F - low))

    def remote(src, dst, snd, rcv, **where):
        return pltpu.make_async_remote_copy(
            src_ref=src, dst_ref=dst, send_sem=snd, recv_sem=rcv,
            device_id=where, device_id_type=MESH,
        )

    def arrived(dst, sem):
        remote(dst, dst, sem, sem, reader=rx).wait_recv()

    def left(src, sem):
        remote(src, src, sem, sem, reader=rx).wait_send()

    def columns(i, cut):
        return pl.ds(pl.multiple_of(i * H + cut[0], tile), cut[1])

    def part(src, g, cut):
        return PR.at[src, g, :, pl.ds(*cut)]

    def own_piece(h):
        return proj.at[:, columns(x, whole[h])]

    def proj_x(h):
        return remote(
            proj.at[:, columns(1 - x, whole[h])], part(b, r, whole[h]), px_snd.at[0], p_rcv.at[b, x, h], reader=rx
        )

    def stage(h):
        return h // (len(CUTS) - 1)

    def to_core(piece, src, g, h):
        late_one = is_end & (src != b) & (src != buddy)
        return remote(
            piece, part(src, g, whole[h]), pc_snd.at[late_one.astype(jnp.int32)], c_rcv.at[src, stage(h)], reader=rc
        )

    def to_buddy(piece, src, g, h):
        return remote(
            piece, part(src, g, whole[h]), pb_snd.at[(src != b).astype(jnp.int32)], p_rcv.at[src, g // 2, h], blk=buddy
        )

    def to_across(piece, src, g, h):
        return remote(piece, part(src, g, whole[h]), pm_snd.at[0], p_rcv.at[src, g // 2, h], blk=across)

    def image_x(h):
        return remote(
            images.at[:, columns(1 - x, strips[h])], X.at[c, x, :, pl.ds(*strips[h])],
            xx_snd.at[0], x_rcv.at[h], reader=rx,
        )

    def own_image_core():
        return remote(
            images.at[:, pl.ds(pl.multiple_of(x * H, H), H)], X.at[c, x],
            xc_snd.at[0], x_rcv.at[2], reader=rc,
        )

    def other_image_core():
        return remote(X.at[c, 1 - x], X.at[c, 1 - x], xc_snd.at[0], x_rcv.at[2], reader=rc)

    def own_far(h):
        return remote(
            images.at[:, columns(x, far_strips[h])], XF.at[c, x, :, pl.ds(*far_strips[h])],
            xf_snd.at[0], xf_rcv.at[h], blk=buddy,
        )

    def other_far(h):
        return remote(
            X.at[c, 1 - x, :, pl.ds(*far_strips[h])], XF.at[c, 1 - x, :, pl.ds(*far_strips[h])],
            xf_snd.at[0], xf_rcv.at[h], blk=buddy,
        )

    def far_core(i):
        return remote(XF.at[c, i], XF.at[c, i], xfc_snd.at[0], xf_rcv.at[2], reader=rc)

    def score_copy(q):
        return remote(SC.at[q], SR.at[q], s_snd.at[0], s_rcv.at[q], reader=rx)

    def routes_x():
        return remote(routes_in, routes.at[x], rt_snd.at[0], rt_rcv.at[0], reader=rx)

    def far_score(k, i):
        if i == 0:
            return remote(SF.at[k, x], FR.at[k, x], f_snd.at[0], f_rcv.at[0], blk=buddy)
        return remote(SF.at[k, 1 - x], FR.at[k, x], f_snd.at[0], f_rcv.at[0], blk=buddy, reader=rx)

    def post_copy(k, p):
        source, to = ((QP.at[p, c, x], rx), (QO.at[p], rc), (QO.at[p], rd))[k]
        return remote(source, QP.at[p, c, x], q_snd.at[k % 2], q_rcv.at[c, x, p], reader=to)

    def post_far(i, j, p):
        return remote(QP.at[p, i, j], QF.at[p, i, j], qf_snd.at[0], qf_rcv.at[p], blk=buddy)

    def end_copy(k, t):
        return remote(TE.at[k, t], RE.at[k, t], e_snd.at[0], e_rcv.at[k, t], blk=buddy)

    def middle_copy(k, t):
        return remote(TM.at[k, t], RM.at[k, t], m_snd.at[0], m_rcv.at[k, t], blk=across)

    def inner_copy(t):
        return remote(TI.at[t], RI.at[t], i_snd.at[0], i_rcv.at[t], blk=buddy)

    def out_span(i, t):
        return out.at[:, pl.ds(pl.multiple_of(i * H + t * tile, tile), tile)]

    def out_x(src, t):
        return remote(src.at[t, 1 - x], out_span(x, t), o_snd.at[0], o_rcv.at[0], reader=rx)

    def out_own(src, t):
        return pltpu.make_async_copy(src.at[t, x], out_span(x, t), own_snd.at[0])

    own_proj = pltpu.make_async_copy(proj.at[:, pl.ds(pl.multiple_of(x * H, H), H)], PR.at[b, r], loc.at[0])
    own_image = pltpu.make_async_copy(
        images.at[:, pl.ds(pl.multiple_of(x * H, H), H)], X.at[c, x], loc.at[1]
    )
    noise_copy = pltpu.make_async_copy(
        noise_in.at[pl.ds(pl.multiple_of(x * H, H), H)], noise, loc.at[2]
    )
    routes_copy = pltpu.make_async_copy(routes_in, routes.at[x], loc.at[3])

    barrier = pltpu.get_barrier_semaphore()
    for k in (rx, rc, rd):
        pl.semaphore_signal(barrier, inc=1, device_id={"reader": k}, device_id_type=MESH)
    pl.semaphore_signal(barrier, inc=1, device_id={"blk": buddy}, device_id_type=MESH)
    pl.semaphore_signal(barrier, inc=1, device_id={"blk": buddy, "reader": rx}, device_id_type=MESH)

    @pl.when(is_inner)
    def _():
        pl.semaphore_signal(barrier, inc=1, device_id={"blk": across}, device_id_type=MESH)

    own_proj.start()
    own_image.start()
    noise_copy.start()
    routes_copy.start()
    pl.semaphore_wait(barrier, 5 + is_inner.astype(jnp.int32))

    def spread(piece, g, h):
        to_buddy(piece, b, g, h).start()

        @pl.when(is_inner)
        def _():
            to_across(piece, b, g, h).start()

    routes_x().start()
    for h in bits:
        proj_x(h).start()
        spread(own_piece(h), r, h)
    for h in bits:
        to_core(own_piece(h), b, r, h).start()
    for h in bits:
        piece = part(b, rx, whole[h])
        arrived(piece, p_rcv.at[b, 1 - x, h])
        spread(piece, rx, h)
        to_core(piece, b, rx, h).start()
        if h == 0:
            for k in halves:
                image_x(k).start()
    own_image_core().start()

    late_pieces = tuple((g, h) for g in (r, rx) for h in late)
    pieces = tuple((g, h) for g in (r, rx) for h in bits)

    def other_image(h):
        arrived(X.at[c, 1 - x, :, pl.ds(*strips[h])], x_rcv.at[h])

    def hand_over(src, g, h):
        piece = part(src, g, whole[h])
        arrived(piece, p_rcv.at[src, g // 2, h])
        to_core(piece, src, g, h).start()

    @pl.when(is_end)
    def _():
        for g, h in pieces[:4]:
            hand_over(buddy, g, h)
        own_far(0).start()
        for g, h in pieces[4:]:
            hand_over(buddy, g, h)
        other_image(0)
        other_far(0).start()
        for g, h in late_pieces:
            hand_over(far_inner, g, h)
        own_far(1).start()
        other_image(1)
        other_far(1).start()
        for g, h in late_pieces[:-2]:
            hand_over(far_end, g, h)

    @pl.when(is_inner)
    def _():
        for g, h in pieces:
            arrived(part(far_inner, g, whole[h]), p_rcv.at[far_inner, g // 2, h])
            if h > 0:
                to_buddy(part(far_inner, g, whole[h]), far_inner, g, h).start()
            to_core(part(far_inner, g, whole[h]), far_inner, g, h).start()
            arrived(part(buddy, g, whole[h]), p_rcv.at[buddy, g // 2, h])
            to_across(part(buddy, g, whole[h]), buddy, g, h).start()
            to_core(part(buddy, g, whole[h]), buddy, g, h).start()
        for g, h in pieces:
            arrived(part(far_end, g, whole[h]), p_rcv.at[far_end, g // 2, h])
            if h > 0:
                to_buddy(part(far_end, g, whole[h]), far_end, g, h).start()
            to_core(part(far_end, g, whole[h]), far_end, g, h).start()
        for h in halves:
            other_image(h)

    other_image_core().start()
    own_proj.wait()
    own_image.wait()
    noise_copy.wait()
    routes_copy.wait()

    arrived(routes.at[1 - x], rt_rcv.at[0])
    lane = lax.broadcasted_iota(jnp.int32, (rows, width), 1)
    block = lane // refs
    diagonal = lax.broadcasted_iota(jnp.int32, (rows, rows), 0) == lax.broadcasted_iota(
        jnp.int32, (rows, rows), 1
    )

    def column(row):
        return jnp.sum(jnp.where(diagonal, row, 0.0), axis=1, keepdims=True).astype(jnp.int32)

    for i in range(2):
        names = routes[i].astype(jnp.float32)
        first, second = column(names[0:1]), column(names[1:2])
        MOVE[i] = (block - jnp.where(block < 2, first, second) + 4) % 4
        @pl.when(i == x)
        def _():
            SAME[0] = jnp.where(block < 2, first, second)
            SAME[1] = jnp.where(block < 2, second, first)

    def packed(p, i):
        even = block % 2 == 0
        low, high, move = S[2 * p, i], S[2 * p + 1, i], MOVE[i]
        total = jnp.where(even, low, high)
        for m in range(1, 4):
            turned_by = jnp.where(even, pltpu.roll(low, m * refs, 1), pltpu.roll(high, m * refs, 1))
            total = jnp.where(move == m, turned_by, total)
        return total

    square = lax.broadcasted_iota(jnp.int32, (width, width), 0) == lax.broadcasted_iota(
        jnp.int32, (width, width), 1
    )

    def scores_of(block, src, tiles):
        scores = jnp.zeros((2 * rows, width), jnp.float32)
        penalty = jnp.zeros((width, 128), jnp.float32)
        for t in tiles:
            cut = pl.ds(t * tile, tile)
            refs_f = PR[src, :, :, cut].reshape(width, tile).astype(jnp.float32)
            scaled = refs_f * noise[cut][None, :]
            scores = scores + lax.dot_general(
                block[c, :, :, cut].reshape(2 * rows, tile), scaled.astype(jnp.bfloat16),
                (((1,), (1,)), ((), ())), preferred_element_type=jnp.float32,
            )
            squares = scaled * refs_f
            for lane in range(0, tile, 128):
                penalty = penalty + squares[:, lane : lane + 128]
        lanes = jnp.sum(penalty, axis=1, keepdims=True)
        penalty_row = 0.5 * jnp.sum(jnp.where(square, lanes, 0.0), axis=0, keepdims=True)
        return (scores - penalty_row).reshape(2, rows, width)

    def from_core(src, n, first):
        start = marks[first]
        both = PR.at[src, pl.ds(0, 2), :, pl.ds(start * tile, (CUTS[-2 + n] - start) * tile)]
        arrived(both, c_rcv.at[src, n])

    def score_source(i, carry):
        src = jnp.where(i == 0, b, jnp.where(i == 1, buddy, jnp.where(i == 2, far_inner, far_end)))

        @pl.when(i < 2)
        def _():
            from_core(src, 0, 0)
            from_core(src, 1, len(CUTS) - 1)

        @pl.when((i < 2) | is_inner)
        def _():
            S[src] = scores_of(X, src, range(T))

        @pl.when((i >= 2) & is_end)
        def _():
            @pl.when(i == 3)
            def _():
                hand_over(src, *late_pieces[-2])

            from_core(src, 0, 1)
            S[src] = scores_of(X, src, range(LOW, CUTS[-2]))

            @pl.when(i == 3)
            def _():
                hand_over(src, *late_pieces[-1])

            from_core(src, 1, len(CUTS) - 1)
            S[src] = S[src] + scores_of(X, src, range(CUTS[-2], T))

        @pl.when(i % 2 == 1)
        def _():
            q = i // 2
            SC[q] = packed(side + q * (1 - 2 * side), 1 - x)
            score_copy(q).start()

        return carry

    lax.fori_loop(0, 2, score_source, 0)
    @pl.when(is_inner)
    def _():
        arrived(XF.at[c, :, :, pl.ds(*far_strips[0])], xf_rcv.at[0])

        def far_source(k, carry):
            src = jnp.where(k == 0, far_inner, far_end)
            from_core(src, 0, 0)
            from_core(src, 1, len(CUTS) - 1)
            SF[k] = scores_of(XF, src, range(LOW))
            for i in (1, 0):
                far_score(k, i).start()
            return carry

        lax.fori_loop(0, 2, far_source, 0)

    lax.fori_loop(2, 4, score_source, 0)

    @pl.when(is_end)
    def _():
        arrived(FR, f_rcv.at[0])
        for k, src in enumerate((far_inner, far_end)):
            S[src, x] = S[src, x] + FR[k, 0] + FR[k, 1]

    chunks = []
    for q, p in enumerate(pairs):
        arrived(SR.at[1 - q], s_rcv.at[1 - q])
        chunks.append(packed(p, x) + SR[1 - q])
    highest = jnp.max(jnp.maximum(chunks[0], chunks[1]), axis=1, keepdims=True)
    total = jnp.exp(chunks[0] - highest) + jnp.exp(chunks[1] - highest)
    normalizer = highest + jnp.log(jnp.sum(total, axis=1, keepdims=True))
    norm[...] = jnp.sum(jnp.where(diagonal, normalizer, 0.0), axis=0, keepdims=True)

    def for_core(value, core):
        group = core + 2 * (lane // (2 * refs))
        swapped = jnp.where(SAME[1] == group, pltpu.roll(value, 2 * refs, 1), 0.0)
        return jnp.where(SAME[0] == group, value, swapped).astype(jnp.bfloat16)

    for q, p in enumerate(pairs):
        value = jnp.exp(chunks[q] - normalizer)
        QP[p, c, x] = for_core(value, c)
        QO[p] = for_core(value, 1 - c)
        for k in (2, 0, 1):
            post_copy(k, p).start()

        @pl.when(is_end)
        def _():
            post_far(c, x, p).start()

    for p in pairs:
        for i, j in ((1 - c, x), (c, 1 - x), (1 - c, 1 - x)):
            arrived(QP.at[p, i, j], q_rcv.at[i, j, p])

            @pl.when(is_end)
            def _():
                post_far(i, j, p).start()

    left(PR.at[0, 0], px_snd.at[0])
    left(X.at[0, 0], xx_snd.at[0])
    left(X.at[0], xc_snd.at[0])
    left(SC, s_snd.at[0])
    routes_x().wait_send()
    late_columns = pl.ds(low, H - low)
    left(PR.at[0, pl.ds(0, 2)], pb_snd.at[0])

    @pl.when(is_end)
    def _():
        left(PR.at[pl.ds(0, 2), pl.ds(0, 2)], pc_snd.at[0])
        left(PR.at[pl.ds(0, 2), pl.ds(0, 2), :, late_columns], pc_snd.at[1])

    @pl.when(is_inner)
    def _():
        left(PR.at[:, pl.ds(0, 2)], pc_snd.at[0])
        left(PR.at[pl.ds(0, 2), pl.ds(0, 2), :, late_columns], pb_snd.at[1])
        left(PR.at[pl.ds(0, 2), pl.ds(0, 2)], pm_snd.at[0])

    def turned(block):
        flat = block.reshape(4 * rows, width).astype(jnp.float32)
        return flat.T.astype(jnp.bfloat16)

    for p in halves:
        QT[p] = turned(QP[p])
    arrived(X.at[1 - c], x_rcv.at[2])

    def product(left, right):
        return lax.dot_general(
            left, right.reshape(4 * rows, tile), (((1,), (0,)), ((), ())), preferred_element_type=jnp.float32
        )

    def span(t):
        return pl.ds(pl.multiple_of(t * tile, tile), tile)

    def multiply(q, t, both):
        total = product(QT[pairs[q]], X[:, :, :, span(t)])
        if both:
            total = total + product(QTF[pairs[q]], XF[:, :, :, span(t)])
        PROD[t, q] = total.reshape(2, 2, refs, tile)

    def own(t, q, d):
        return PROD[t, q, :, d % 2]

    def f32(value):
        return value.astype(jnp.float32)

    @pl.when(is_end)
    def _():
        def send(k, q, d, t):
            TE[k, t - TF] = own(t, q, d).astype(jnp.bfloat16)
            end_copy(k, t - TF).start()

        def send_far(t, carry):
            multiply(0, t, False)
            send(1, 0, far_end, t)
            send(0, 0, far_inner, t)
            return carry

        def send_near(t, carry):
            multiply(1, t, False)
            send(2, 1, inner, t)
            return carry

        def pass_on(t, carry):
            arrived(RI.at[t], i_rcv.at[t])
            out_x(RI, t).start()
            out_own(RI, t).start()
            return carry

        def finish(t, carry):
            arrived(RI.at[t], i_rcv.at[t])
            O[t] = (own(t, 1, end) + f32(RI[t])).astype(jnp.bfloat16)
            out_x(O, t).start()
            out_own(O, t).start()
            return carry

        left(QP, qf_snd.at[0])
        lax.fori_loop(TF, T, send_far, 0)
        lax.fori_loop(TF, T, send_near, 0)
        lax.fori_loop(0, TF, pass_on, 0)
        lax.fori_loop(TF, T, finish, 0)

    @pl.when(is_inner)
    def _():
        arrived(XF.at[c, :, :, pl.ds(*far_strips[1])], xf_rcv.at[1])
        for i in range(2):
            far_core(i).start()
        arrived(XF.at[1 - c], xf_rcv.at[2])

        def far_posterior(q):
            p = pairs[q]
            arrived(QF.at[p], qf_rcv.at[p])
            QTF[p] = turned(QF[p])

        def multiply_any(q, t):
            @pl.when(t < TF)
            def _():
                multiply(q, t, True)

            @pl.when(t >= TF)
            def _():
                multiply(q, t, False)

        far_posterior(0)

        def outward(k, d, t):
            @pl.when(t < TF)
            def _():
                TM[k, t] = own(t, 0, d).astype(jnp.bfloat16)

            @pl.when(t >= TF)
            def _():
                arrived(RE.at[k, t - TF], e_rcv.at[k, t - TF])
                TM[k, t] = (own(t, 0, d) + f32(RE[k, t - TF])).astype(jnp.bfloat16)

            middle_copy(k, t).start()

        def turn(t, carry):
            @pl.when(t < T)
            def _():
                multiply_any(0, t)
                outward(1, far_end, t)

            @pl.when((t >= 3) & (t < T + 3))
            def _():
                outward(0, far_inner, t - 3)

            @pl.when(t == 1)
            def _():
                far_posterior(1)

            @pl.when((t >= 1) & (t < T + 1))
            def _():
                multiply_any(1, t - 1)

            @pl.when((t >= 2) & (t < T + 2))
            def _():
                n = t - 2
                arrived(RM.at[1, n], m_rcv.at[1, n])
                TI[n] = (own(n, 1, end) + f32(RM[1, n])).astype(jnp.bfloat16)
                inner_copy(n).start()

            @pl.when(t >= 5)
            def _():
                n = t - 5
                arrived(RM.at[0, n], m_rcv.at[0, n])
                total = own(n, 1, inner) + f32(RM[0, n])

                @pl.when(n < TF)
                def _():
                    O[n] = total.astype(jnp.bfloat16)

                @pl.when(n >= TF)
                def _():
                    arrived(RE.at[2, n - TF], e_rcv.at[2, n - TF])
                    O[n] = (total + f32(RE[2, n - TF])).astype(jnp.bfloat16)

                out_x(O, n).start()
                out_own(O, n).start()

            return carry

        lax.fori_loop(0, T + 5, turn, 0)

    left(QP.at[0], q_snd.at[0])
    left(QP.at[0, 0], q_snd.at[1])

    @pl.when(is_end)
    def _():
        left(XF.at[0], xf_snd.at[0])
        left(TE, e_snd.at[0])

    @pl.when(is_inner)
    def _():
        left(XF.at[0], xfc_snd.at[0])
        left(SF, f_snd.at[0])
        left(TM, m_snd.at[0])
        left(TI, i_snd.at[0])

    left(O.at[:, 0], o_snd.at[0])
    pltpu.make_async_copy(O.at[:, 0], O.at[:, 0], own_snd.at[0]).wait()
    arrived(out.at[:, pl.ds(pl.multiple_of((1 - x) * H, H), H)], o_rcv.at[0])


def hand_out(sums_in, norm_in, sums_out, norm_out):
    sums_out[...] = sums_in[...].astype(jnp.float32)
    norm_out[...] = norm_in[...]


def paired_halves(images, routes, projections, noise_weights):
    rows, coef = images.shape
    refs = projections.shape[1]
    H, width = coef // 2, 4 * refs
    F = H // 2
    T, TF = 8, 4
    tile = H // T
    TN = T - TF
    dma = pltpu.SemaphoreType.DMA
    bf16, f32 = jnp.bfloat16, jnp.float32
    piece = (2, refs, tile)
    sums, norm = pl.pallas_call(
        paired,
        out_shape=(
            jax.ShapeDtypeStruct((refs, coef), bf16),
            jax.ShapeDtypeStruct((1, rows), f32),
        ),
        in_specs=[pl.BlockSpec(memory_space=pltpu.HBM)] * 4,
        out_specs=(
            pl.BlockSpec(memory_space=pl.ANY),
            pl.BlockSpec(memory_space=pltpu.VMEM),
        ),
        scratch_shapes=[
            pltpu.VMEM((2, 2, rows), jnp.int32),
            pltpu.VMEM((H,), f32),
            pltpu.VMEM((2, 2, rows, H), bf16),
            pltpu.VMEM((2, 2, rows, F), bf16),
            pltpu.VMEM((4, 4, refs, H), bf16),
            pltpu.VMEM((4, 2, rows, width), f32),
            pltpu.VMEM((2, rows, width), f32),
            pltpu.VMEM((2, rows, width), f32),
            pltpu.VMEM((2, rows, width), jnp.int32),
            pltpu.VMEM((2, rows, width), jnp.int32),
            pltpu.VMEM((2, 2, rows, width), f32),
            pltpu.VMEM((2, 2, rows, width), f32),
            pltpu.VMEM((2, 2, 2, rows, width), bf16),
            pltpu.VMEM((2, rows, width), bf16),
            pltpu.VMEM((2, 2, 2, rows, width), bf16),
            pltpu.VMEM((2, width, 4 * rows), bf16),
            pltpu.VMEM((2, width, 4 * rows), bf16),
            pltpu.VMEM((T, 2, 2, 2, refs, tile), f32),
            pltpu.VMEM((3, TN) + piece, bf16),
            pltpu.VMEM((3, TN) + piece, bf16),
            pltpu.VMEM((2, T) + piece, bf16),
            pltpu.VMEM((2, T) + piece, bf16),
            pltpu.VMEM((T,) + piece, bf16),
            pltpu.VMEM((T,) + piece, bf16),
            pltpu.VMEM((T,) + piece, bf16),
            dma((4,)), dma((1,)), dma((1,)), dma((1,)), dma((2,)), dma((1,)), dma((2,)),
            dma((4, 2, len(CUTS))), dma((4, 2)), dma((1,)), dma((1,)), dma((3,)), dma((1,)), dma((1,)), dma((3,)),
            dma((1,)), dma((2,)), dma((1,)), dma((1,)), dma((2,)), dma((2, 2, 2)), dma((1,)), dma((2,)),
            dma((1,)), dma((3, TN)), dma((1,)), dma((2, T)), dma((1,)), dma((T,)),
            dma((1,)), dma((1,)), dma((1,)),
        ],
        compiler_params=pltpu.CompilerParams(
            collective_id=0, has_side_effects=True, vmem_limit_bytes=64 * 1024 * 1024 - 65536
        ),
        cost_estimate=pl.CostEstimate(
            flops=4 * 4 * rows * 4 * width * H // 2, bytes_accessed=4 * rows * coef, transcendentals=0
        ),
    )(images, routes.T, projections[0], noise_weights)
    block = coef // 2
    sums, norm = pl.pallas_call(
        hand_out,
        grid=(coef // block,),
        out_shape=(jax.ShapeDtypeStruct((refs, coef), f32), jax.ShapeDtypeStruct((1, rows), f32)),
        in_specs=[pl.BlockSpec((refs, block), lambda i: (0, i)), pl.BlockSpec((1, rows), lambda i: (0, 0))],
        out_specs=(pl.BlockSpec((refs, block), lambda i: (0, i)), pl.BlockSpec((1, rows), lambda i: (0, 0))),
    )(sums, norm)
    return (sums[None], norm[0])


def solution(mesh):
    sizes = dict(mesh.shape)
    direct = sizes["sub"] == 1 and sizes["reader"] == 4 and sizes["blk"] == 4
    return jax.shard_map(
        paired_halves if direct else routed,
        mesh=mesh,
        in_specs=(
            P(("parts", "blk", "reader"), "sub"),
            P(("parts", "blk", "reader"), None),
            P(("parts", "reader"), "blk", "sub"),
            P(("parts", "sub")),
        ),
        out_specs=(P(("parts", "reader"), "blk", "sub"), P(("parts", "blk", "reader"))),
        check_vma=False,
    )
```

```python
from functools import partial

import jax
import jax.numpy as jnp
from jax import lax
from jax.experimental import pallas as pl
from jax.experimental.pallas import tpu as pltpu
from jax.sharding import PartitionSpec as P

MESH = pl.DeviceIdType.MESH


def from_behind(block, axis, distance):
    devices = range(lax.axis_size(axis))
    route = [((i - distance) % len(devices), i) for i in devices]
    return lax.ppermute(block, axis, route)


def slot_positions(route_block):
    flat = route_block.reshape(-1)
    order = jnp.arange(flat.shape[0], dtype=jnp.int32)
    earlier = (order[None, :] < order[:, None]) & (flat[None, :] == flat[:, None])
    return jnp.sum(earlier.astype(jnp.int32), axis=1).reshape(route_block.shape)


def combine_stats(row_peaks, row_totals):
    highest = jnp.max(row_peaks, axis=-1)
    spread = row_totals * jnp.exp(row_peaks - highest[..., None])
    return highest + jnp.log(jnp.sum(spread, axis=-1))


def routed(images, routes, projections, noise_weights):
    groups = lax.axis_size("reader")
    cycle_size = lax.axis_size("blk")
    my_group = lax.axis_index("reader")
    my_member = lax.axis_index("blk")
    per_device, top_count = routes.shape
    half_width = images.shape[1]
    capacity = min(per_device, 2 * per_device * top_count // groups)
    slot_count = groups * capacity
    ref_count = projections.shape[1]
    all_refs = ref_count * cycle_size
    anchor = jnp.zeros((), jnp.int32)
    own_index = slot_positions(routes)
    own_target = routes * capacity + own_index
    sources = jnp.broadcast_to(jnp.arange(per_device, dtype=jnp.int32)[:, None], routes.shape)
    picker = (
        jnp.full((slot_count,), per_device, jnp.int32)
        .at[own_target.reshape(-1)]
        .set(sources.reshape(-1))
    )
    padded = jnp.concatenate([images, jnp.zeros((1, half_width), images.dtype)], axis=0)
    outgoing = padded[picker].reshape(groups, capacity, half_width)
    received = lax.all_to_all(outgoing, "reader", split_axis=0, concat_axis=0, tiled=True).reshape(
        slot_count, half_width
    )
    every_route = lax.all_gather(routes, "reader", axis=0, tiled=True).reshape(
        groups, per_device, top_count
    )
    every_index = jax.vmap(slot_positions)(every_route)
    senders = jnp.arange(groups, dtype=jnp.int32)[:, None, None]
    landing = jnp.where(every_route == my_group, senders * capacity + every_index, slot_count)
    live_slot = jnp.zeros((slot_count,), jnp.int32).at[landing.reshape(-1)].set(1, mode="drop") > 0

    def score_block(ref_block):
        scaled = ref_block.astype(jnp.float32) * noise_weights[None, :]
        weighted = scaled.astype(jnp.bfloat16)
        penalty = 0.5 * jnp.sum(scaled * ref_block.astype(jnp.float32), axis=1)
        partial_scores = lax.dot_general(
            weighted, received, (((1,), (1,)), ((), ())), preferred_element_type=jnp.float32
        )
        return partial_scores - penalty[:, None]

    def cycle_turn(rotation, carry):
        ref_block, score_table = carry
        position = (my_member - rotation) % cycle_size
        score_table = lax.dynamic_update_slice(
            score_table, score_block(ref_block)[None], (position, anchor, anchor)
        )
        ref_block = from_behind(ref_block, "blk", 1)
        return (ref_block, score_table)

    empty_table = jnp.zeros((cycle_size, ref_count, slot_count), jnp.float32)
    ref_block, score_table = lax.fori_loop(
        0, cycle_size - 1, cycle_turn, (projections[0], empty_table)
    )
    position = (my_member + 1) % cycle_size
    score_table = lax.dynamic_update_slice(
        score_table, score_block(ref_block)[None], (position, anchor, anchor)
    )
    score_table = lax.psum(score_table, "sub")
    scores = score_table.reshape(all_refs, slot_count)
    row_peak = jnp.max(scores, axis=0)
    row_total = jnp.sum(jnp.exp(scores - row_peak[None, :]), axis=0)
    back_peak, back_total = (
        lax.all_to_all(
            row_peak.reshape(groups, capacity), "reader", split_axis=0, concat_axis=0, tiled=True
        ),
        lax.all_to_all(
            row_total.reshape(groups, capacity), "reader", split_axis=0, concat_axis=0, tiled=True
        ),
    )
    normalizer = combine_stats(
        back_peak.reshape(-1)[own_target], back_total.reshape(-1)[own_target]
    )
    outgoing_norm = (
        jnp.zeros((slot_count,), jnp.float32)
        .at[own_target.reshape(-1)]
        .set(jnp.repeat(normalizer, top_count))
    )
    slot_norm = lax.all_to_all(
        outgoing_norm.reshape(groups, capacity), "reader", split_axis=0, concat_axis=0, tiled=True
    ).reshape(slot_count)
    exponent = jnp.where(live_slot[None, :], scores - slot_norm[None, :], -jnp.inf)
    posterior = jnp.exp(exponent).astype(jnp.bfloat16)
    summed = lax.psum_scatter(
        jnp.dot(posterior, received, preferred_element_type=jnp.float32).astype(jnp.bfloat16),
        "blk",
        scatter_dimension=0,
        tiled=True,
    ).astype(jnp.float32)
    return (summed[None], normalizer)


LOW = 3
CUTS = (3, 6, 8)


def paired(
    images, routes_in, proj, noise_in,
    out, norm,
    routes, noise, X, XF, PR, S, SC, SR, MOVE, SAME, SF, FR, QP, QO, QF, QT, QTF, PROD, TE, RE, TM, RM, TI, RI, O,
    loc, rt_snd, rt_rcv, px_snd, pb_snd, pm_snd, pc_snd, p_rcv, c_rcv, xx_snd, xc_snd, x_rcv, xf_snd, xfc_snd, xf_rcv,
    s_snd, s_rcv, f_snd, f_rcv, q_snd, q_rcv, qf_snd, qf_rcv, e_snd, e_rcv, m_snd, m_rcv, i_snd, i_rcv,
    own_snd, o_snd, o_rcv,
):
    r = lax.axis_index("reader")
    b = lax.axis_index("blk")
    x, c = r // 2, r % 2
    rx, rc = (r + 2) % 4, x * 2 + 1 - c
    rd = (rc + 2) % 4
    side = b // 2
    inner, end = 1 + side, 3 * side
    far_inner, far_end = 2 - side, 3 - 3 * side
    buddy, across = inner + end - b, 3 - b
    is_end = b == end
    is_inner = b == inner
    rows = images.shape[0]
    refs = proj.shape[0]
    H = X.shape[4 - 1]
    F = H // 2
    T, tile = O.shape[0], O.shape[3]
    TF = F // tile
    low = LOW * tile
    width = 4 * refs
    halves = (0, 1)
    pairs = (1 - side, side)
    marks = (0,) + CUTS
    whole = tuple((a * tile, (e - a) * tile) for a, e in zip(marks, CUTS))
    bits = range(len(CUTS))
    late = bits[1:]
    strips = ((0, low), (low, H - low))
    far_strips = ((0, low), (low, F - low))

    def remote(src, dst, snd, rcv, **where):
        return pltpu.make_async_remote_copy(
            src_ref=src, dst_ref=dst, send_sem=snd, recv_sem=rcv,
            device_id=where, device_id_type=MESH,
        )

    def arrived(dst, sem):
        remote(dst, dst, sem, sem, reader=rx).wait_recv()

    def left(src, sem):
        remote(src, src, sem, sem, reader=rx).wait_send()

    def columns(i, cut):
        return pl.ds(pl.multiple_of(i * H + cut[0], tile), cut[1])

    def part(src, g, cut):
        return PR.at[src, g, :, pl.ds(*cut)]

    def own_piece(h):
        return proj.at[:, columns(x, whole[h])]

    def proj_x(h):
        return remote(
            proj.at[:, columns(1 - x, whole[h])], part(b, r, whole[h]), px_snd.at[0], p_rcv.at[b, x, h], reader=rx
        )

    def stage(h):
        return h // (len(CUTS) - 1)

    def to_core(piece, src, g, h):
        late_one = is_end & (src != b) & (src != buddy)
        return remote(
            piece, part(src, g, whole[h]), pc_snd.at[late_one.astype(jnp.int32)], c_rcv.at[src, stage(h)], reader=rc
        )

    def to_buddy(piece, src, g, h):
        return remote(
            piece, part(src, g, whole[h]), pb_snd.at[(src != b).astype(jnp.int32)], p_rcv.at[src, g // 2, h], blk=buddy
        )

    def to_across(piece, src, g, h):
        return remote(piece, part(src, g, whole[h]), pm_snd.at[0], p_rcv.at[src, g // 2, h], blk=across)

    def image_x(h):
        return remote(
            images.at[:, columns(1 - x, strips[h])], X.at[c, x, :, pl.ds(*strips[h])],
            xx_snd.at[0], x_rcv.at[h], reader=rx,
        )

    def own_image_core():
        return remote(
            images.at[:, pl.ds(pl.multiple_of(x * H, H), H)], X.at[c, x],
            xc_snd.at[0], x_rcv.at[2], reader=rc,
        )

    def other_image_core():
        return remote(X.at[c, 1 - x], X.at[c, 1 - x], xc_snd.at[0], x_rcv.at[2], reader=rc)

    def own_far(h):
        return remote(
            images.at[:, columns(x, far_strips[h])], XF.at[c, x, :, pl.ds(*far_strips[h])],
            xf_snd.at[0], xf_rcv.at[h], blk=buddy,
        )

    def other_far(h):
        return remote(
            X.at[c, 1 - x, :, pl.ds(*far_strips[h])], XF.at[c, 1 - x, :, pl.ds(*far_strips[h])],
            xf_snd.at[0], xf_rcv.at[h], blk=buddy,
        )

    def far_core(i):
        return remote(XF.at[c, i], XF.at[c, i], xfc_snd.at[0], xf_rcv.at[2], reader=rc)

    def score_copy(q):
        return remote(SC.at[q], SR.at[q], s_snd.at[0], s_rcv.at[q], reader=rx)

    def routes_x():
        return remote(routes_in, routes.at[x], rt_snd.at[0], rt_rcv.at[0], reader=rx)

    def far_score(k, i):
        if i == 0:
            return remote(SF.at[k, x], FR.at[k, x], f_snd.at[0], f_rcv.at[0], blk=buddy)
        return remote(SF.at[k, 1 - x], FR.at[k, x], f_snd.at[0], f_rcv.at[0], blk=buddy, reader=rx)

    def post_copy(k, p):
        source, to = ((QP.at[p, c, x], rx), (QO.at[p], rc), (QO.at[p], rd))[k]
        return remote(source, QP.at[p, c, x], q_snd.at[k % 2], q_rcv.at[c, x, p], reader=to)

    def post_far(i, j, p):
        return remote(QP.at[p, i, j], QF.at[p, i, j], qf_snd.at[0], qf_rcv.at[p], blk=buddy)

    def end_copy(k, t):
        return remote(TE.at[k, t], RE.at[k, t], e_snd.at[0], e_rcv.at[k, t], blk=buddy)

    def middle_copy(k, t):
        return remote(TM.at[k, t], RM.at[k, t], m_snd.at[0], m_rcv.at[k, t], blk=across)

    def inner_copy(t):
        return remote(TI.at[t], RI.at[t], i_snd.at[0], i_rcv.at[t], blk=buddy)

    def out_span(i, t):
        return out.at[:, pl.ds(pl.multiple_of(i * H + t * tile, tile), tile)]

    def out_x(src, t):
        return remote(src.at[t, 1 - x], out_span(x, t), o_snd.at[0], o_rcv.at[0], reader=rx)

    def out_own(src, t):
        return pltpu.make_async_copy(src.at[t, x], out_span(x, t), own_snd.at[0])

    own_proj = pltpu.make_async_copy(proj.at[:, pl.ds(pl.multiple_of(x * H, H), H)], PR.at[b, r], loc.at[0])
    own_image = pltpu.make_async_copy(
        images.at[:, pl.ds(pl.multiple_of(x * H, H), H)], X.at[c, x], loc.at[1]
    )
    noise_copy = pltpu.make_async_copy(
        noise_in.at[pl.ds(pl.multiple_of(x * H, H), H)], noise, loc.at[2]
    )
    routes_copy = pltpu.make_async_copy(routes_in, routes.at[x], loc.at[3])

    barrier = pltpu.get_barrier_semaphore()
    for k in (rx, rc, rd):
        pl.semaphore_signal(barrier, inc=1, device_id={"reader": k}, device_id_type=MESH)
    pl.semaphore_signal(barrier, inc=1, device_id={"blk": buddy}, device_id_type=MESH)
    pl.semaphore_signal(barrier, inc=1, device_id={"blk": buddy, "reader": rx}, device_id_type=MESH)

    @pl.when(is_inner)
    def _():
        pl.semaphore_signal(barrier, inc=1, device_id={"blk": across}, device_id_type=MESH)

    own_proj.start()
    own_image.start()
    noise_copy.start()
    routes_copy.start()
    pl.semaphore_wait(barrier, 5 + is_inner.astype(jnp.int32))

    def spread(piece, g, h):
        to_buddy(piece, b, g, h).start()

        @pl.when(is_inner)
        def _():
            to_across(piece, b, g, h).start()

    routes_x().start()
    for h in bits:
        proj_x(h).start()
        spread(own_piece(h), r, h)
    for h in bits:
        to_core(own_piece(h), b, r, h).start()
    for h in bits:
        piece = part(b, rx, whole[h])
        arrived(piece, p_rcv.at[b, 1 - x, h])
        spread(piece, rx, h)
        to_core(piece, b, rx, h).start()
        if h == 0:
            for k in halves:
                image_x(k).start()
    own_image_core().start()

    late_pieces = tuple((g, h) for g in (r, rx) for h in late)
    pieces = tuple((g, h) for g in (r, rx) for h in bits)

    def other_image(h):
        arrived(X.at[c, 1 - x, :, pl.ds(*strips[h])], x_rcv.at[h])

    def hand_over(src, g, h):
        piece = part(src, g, whole[h])
        arrived(piece, p_rcv.at[src, g // 2, h])
        to_core(piece, src, g, h).start()

    @pl.when(is_end)
    def _():
        for g, h in pieces[:4]:
            hand_over(buddy, g, h)
        own_far(0).start()
        for g, h in pieces[4:]:
            hand_over(buddy, g, h)
        other_image(0)
        other_far(0).start()
        for g, h in late_pieces:
            hand_over(far_inner, g, h)
        own_far(1).start()
        other_image(1)
        other_far(1).start()
        for g, h in late_pieces[:-2]:
            hand_over(far_end, g, h)

    @pl.when(is_inner)
    def _():
        for g, h in pieces:
            arrived(part(far_inner, g, whole[h]), p_rcv.at[far_inner, g // 2, h])
            if h > 0:
                to_buddy(part(far_inner, g, whole[h]), far_inner, g, h).start()
            to_core(part(far_inner, g, whole[h]), far_inner, g, h).start()
            arrived(part(buddy, g, whole[h]), p_rcv.at[buddy, g // 2, h])
            to_across(part(buddy, g, whole[h]), buddy, g, h).start()
            to_core(part(buddy, g, whole[h]), buddy, g, h).start()
        for g, h in pieces:
            arrived(part(far_end, g, whole[h]), p_rcv.at[far_end, g // 2, h])
            if h > 0:
                to_buddy(part(far_end, g, whole[h]), far_end, g, h).start()
            to_core(part(far_end, g, whole[h]), far_end, g, h).start()
        for h in halves:
            other_image(h)

    other_image_core().start()
    own_proj.wait()
    own_image.wait()
    noise_copy.wait()
    routes_copy.wait()

    arrived(routes.at[1 - x], rt_rcv.at[0])
    lane = lax.broadcasted_iota(jnp.int32, (rows, width), 1)
    block = lane // refs
    diagonal = lax.broadcasted_iota(jnp.int32, (rows, rows), 0) == lax.broadcasted_iota(
        jnp.int32, (rows, rows), 1
    )

    def column(row):
        return jnp.sum(jnp.where(diagonal, row, 0.0), axis=1, keepdims=True).astype(jnp.int32)

    for i in range(2):
        names = routes[i].astype(jnp.float32)
        first, second = column(names[0:1]), column(names[1:2])
        MOVE[i] = (block - jnp.where(block < 2, first, second) + 4) % 4
        @pl.when(i == x)
        def _():
            SAME[0] = jnp.where(block < 2, first, second)
            SAME[1] = jnp.where(block < 2, second, first)

    def packed(p, i):
        even = block % 2 == 0
        low, high, move = S[2 * p, i], S[2 * p + 1, i], MOVE[i]
        total = jnp.where(even, low, high)
        for m in range(1, 4):
            turned_by = jnp.where(even, pltpu.roll(low, m * refs, 1), pltpu.roll(high, m * refs, 1))
            total = jnp.where(move == m, turned_by, total)
        return total

    square = lax.broadcasted_iota(jnp.int32, (width, width), 0) == lax.broadcasted_iota(
        jnp.int32, (width, width), 1
    )

    def scores_of(block, src, tiles):
        scores = jnp.zeros((2 * rows, width), jnp.float32)
        penalty = jnp.zeros((width, 128), jnp.float32)
        for t in tiles:
            cut = pl.ds(t * tile, tile)
            refs_f = PR[src, :, :, cut].reshape(width, tile).astype(jnp.float32)
            scaled = refs_f * noise[cut][None, :]
            scores = scores + lax.dot_general(
                block[c, :, :, cut].reshape(2 * rows, tile), scaled.astype(jnp.bfloat16),
                (((1,), (1,)), ((), ())), preferred_element_type=jnp.float32,
            )
            squares = scaled * refs_f
            for lane in range(0, tile, 128):
                penalty = penalty + squares[:, lane : lane + 128]
        lanes = jnp.sum(penalty, axis=1, keepdims=True)
        penalty_row = 0.5 * jnp.sum(jnp.where(square, lanes, 0.0), axis=0, keepdims=True)
        return (scores - penalty_row).reshape(2, rows, width)

    def from_core(src, n, first):
        start = marks[first]
        both = PR.at[src, pl.ds(0, 2), :, pl.ds(start * tile, (CUTS[-2 + n] - start) * tile)]
        arrived(both, c_rcv.at[src, n])

    def score_source(i, carry):
        src = jnp.where(i == 0, b, jnp.where(i == 1, buddy, jnp.where(i == 2, far_inner, far_end)))

        @pl.when(i < 2)
        def _():
            from_core(src, 0, 0)
            from_core(src, 1, len(CUTS) - 1)

        @pl.when((i < 2) | is_inner)
        def _():
            S[src] = scores_of(X, src, range(T))

        @pl.when((i >= 2) & is_end)
        def _():
            @pl.when(i == 3)
            def _():
                hand_over(src, *late_pieces[-2])

            from_core(src, 0, 1)
            S[src] = scores_of(X, src, range(LOW, CUTS[-2]))

            @pl.when(i == 3)
            def _():
                hand_over(src, *late_pieces[-1])

            from_core(src, 1, len(CUTS) - 1)
            S[src] = S[src] + scores_of(X, src, range(CUTS[-2], T))

        @pl.when(i % 2 == 1)
        def _():
            q = i // 2
            SC[q] = packed(side + q * (1 - 2 * side), 1 - x)
            score_copy(q).start()

        return carry

    lax.fori_loop(0, 2, score_source, 0)
    @pl.when(is_inner)
    def _():
        arrived(XF.at[c, :, :, pl.ds(*far_strips[0])], xf_rcv.at[0])

        def far_source(k, carry):
            src = jnp.where(k == 0, far_inner, far_end)
            from_core(src, 0, 0)
            from_core(src, 1, len(CUTS) - 1)
            SF[k] = scores_of(XF, src, range(LOW))
            for i in (1, 0):
                far_score(k, i).start()
            return carry

        lax.fori_loop(0, 2, far_source, 0)

    lax.fori_loop(2, 4, score_source, 0)

    @pl.when(is_end)
    def _():
        arrived(FR, f_rcv.at[0])
        for k, src in enumerate((far_inner, far_end)):
            S[src, x] = S[src, x] + FR[k, 0] + FR[k, 1]

    chunks = []
    for q, p in enumerate(pairs):
        arrived(SR.at[1 - q], s_rcv.at[1 - q])
        chunks.append(packed(p, x) + SR[1 - q])
    highest = jnp.max(jnp.maximum(chunks[0], chunks[1]), axis=1, keepdims=True)
    total = jnp.exp(chunks[0] - highest) + jnp.exp(chunks[1] - highest)
    normalizer = highest + jnp.log(jnp.sum(total, axis=1, keepdims=True))
    norm[...] = jnp.sum(jnp.where(diagonal, normalizer, 0.0), axis=0, keepdims=True)

    def for_core(value, core):
        group = core + 2 * (lane // (2 * refs))
        swapped = jnp.where(SAME[1] == group, pltpu.roll(value, 2 * refs, 1), 0.0)
        return jnp.where(SAME[0] == group, value, swapped).astype(jnp.bfloat16)

    for q, p in enumerate(pairs):
        value = jnp.exp(chunks[q] - normalizer)
        QP[p, c, x] = for_core(value, c)
        QO[p] = for_core(value, 1 - c)
        for k in (2, 0, 1):
            post_copy(k, p).start()

        @pl.when(is_end)
        def _():
            post_far(c, x, p).start()

    for p in pairs:
        for i, j in ((1 - c, x), (c, 1 - x), (1 - c, 1 - x)):
            arrived(QP.at[p, i, j], q_rcv.at[i, j, p])

            @pl.when(is_end)
            def _():
                post_far(i, j, p).start()

    left(PR.at[0, 0], px_snd.at[0])
    left(X.at[0, 0], xx_snd.at[0])
    left(X.at[0], xc_snd.at[0])
    left(SC, s_snd.at[0])
    routes_x().wait_send()
    late_columns = pl.ds(low, H - low)
    left(PR.at[0, pl.ds(0, 2)], pb_snd.at[0])

    @pl.when(is_end)
    def _():
        left(PR.at[pl.ds(0, 2), pl.ds(0, 2)], pc_snd.at[0])
        left(PR.at[pl.ds(0, 2), pl.ds(0, 2), :, late_columns], pc_snd.at[1])

    @pl.when(is_inner)
    def _():
        left(PR.at[:, pl.ds(0, 2)], pc_snd.at[0])
        left(PR.at[pl.ds(0, 2), pl.ds(0, 2), :, late_columns], pb_snd.at[1])
        left(PR.at[pl.ds(0, 2), pl.ds(0, 2)], pm_snd.at[0])

    def turned(block):
        flat = block.reshape(4 * rows, width).astype(jnp.float32)
        return flat.T.astype(jnp.bfloat16)

    for p in halves:
        QT[p] = turned(QP[p])
    arrived(X.at[1 - c], x_rcv.at[2])

    def product(left, right):
        return lax.dot_general(
            left, right.reshape(4 * rows, tile), (((1,), (0,)), ((), ())), preferred_element_type=jnp.float32
        )

    def span(t):
        return pl.ds(pl.multiple_of(t * tile, tile), tile)

    def multiply(q, t, both):
        total = product(QT[pairs[q]], X[:, :, :, span(t)])
        if both:
            total = total + product(QTF[pairs[q]], XF[:, :, :, span(t)])
        PROD[t, q] = total.reshape(2, 2, refs, tile)

    def own(t, q, d):
        return PROD[t, q, :, d % 2]

    def f32(value):
        return value.astype(jnp.float32)

    @pl.when(is_end)
    def _():
        def send(k, q, d, t):
            TE[k, t - TF] = own(t, q, d).astype(jnp.bfloat16)
            end_copy(k, t - TF).start()

        def send_far(t, carry):
            multiply(0, t, False)
            send(1, 0, far_end, t)
            send(0, 0, far_inner, t)
            return carry

        def send_near(t, carry):
            multiply(1, t, False)
            send(2, 1, inner, t)
            return carry

        def pass_on(t, carry):
            arrived(RI.at[t], i_rcv.at[t])
            out_x(RI, t).start()
            out_own(RI, t).start()
            return carry

        def finish(t, carry):
            arrived(RI.at[t], i_rcv.at[t])
            O[t] = (own(t, 1, end) + f32(RI[t])).astype(jnp.bfloat16)
            out_x(O, t).start()
            out_own(O, t).start()
            return carry

        left(QP, qf_snd.at[0])
        lax.fori_loop(TF, T, send_far, 0)
        lax.fori_loop(TF, T, send_near, 0)
        lax.fori_loop(0, TF, pass_on, 0)
        lax.fori_loop(TF, T, finish, 0)

    @pl.when(is_inner)
    def _():
        arrived(XF.at[c, :, :, pl.ds(*far_strips[1])], xf_rcv.at[1])
        for i in range(2):
            far_core(i).start()
        arrived(XF.at[1 - c], xf_rcv.at[2])

        def far_posterior(q):
            p = pairs[q]
            arrived(QF.at[p], qf_rcv.at[p])
            QTF[p] = turned(QF[p])

        def multiply_any(q, t):
            @pl.when(t < TF)
            def _():
                multiply(q, t, True)

            @pl.when(t >= TF)
            def _():
                multiply(q, t, False)

        far_posterior(0)

        def outward(k, d, t):
            @pl.when(t < TF)
            def _():
                TM[k, t] = own(t, 0, d).astype(jnp.bfloat16)

            @pl.when(t >= TF)
            def _():
                arrived(RE.at[k, t - TF], e_rcv.at[k, t - TF])
                TM[k, t] = (own(t, 0, d) + f32(RE[k, t - TF])).astype(jnp.bfloat16)

            middle_copy(k, t).start()

        lead = 4

        def turn(t, carry):
            @pl.when(t < T)
            def _():
                multiply_any(0, t)
                outward(1, far_end, t)

            @pl.when((t >= lead) & (t < T + lead))
            def _():
                outward(0, far_inner, t - lead)

            @pl.when(t == 1)
            def _():
                far_posterior(1)

            @pl.when((t >= 1) & (t < T + 1))
            def _():
                multiply_any(1, t - 1)

            @pl.when((t >= 2) & (t < T + 2))
            def _():
                n = t - 2
                arrived(RM.at[1, n], m_rcv.at[1, n])
                TI[n] = (own(n, 1, end) + f32(RM[1, n])).astype(jnp.bfloat16)
                inner_copy(n).start()

            @pl.when(t >= 8)
            def _():
                n = t - 8
                arrived(RM.at[0, n], m_rcv.at[0, n])
                total = own(n, 1, inner) + f32(RM[0, n])

                @pl.when(n < TF)
                def _():
                    O[n] = total.astype(jnp.bfloat16)

                @pl.when(n >= TF)
                def _():
                    arrived(RE.at[2, n - TF], e_rcv.at[2, n - TF])
                    O[n] = (total + f32(RE[2, n - TF])).astype(jnp.bfloat16)

                out_x(O, n).start()
                out_own(O, n).start()

            return carry

        lax.fori_loop(0, T + 8, turn, 0)

    left(QP.at[0], q_snd.at[0])
    left(QP.at[0, 0], q_snd.at[1])

    @pl.when(is_end)
    def _():
        left(XF.at[0], xf_snd.at[0])
        left(TE, e_snd.at[0])

    @pl.when(is_inner)
    def _():
        left(XF.at[0], xfc_snd.at[0])
        left(SF, f_snd.at[0])
        left(TM, m_snd.at[0])
        left(TI, i_snd.at[0])

    left(O.at[:, 0], o_snd.at[0])
    pltpu.make_async_copy(O.at[:, 0], O.at[:, 0], own_snd.at[0]).wait()
    arrived(out.at[:, pl.ds(pl.multiple_of((1 - x) * H, H), H)], o_rcv.at[0])


def hand_out(sums_in, norm_in, sums_out, norm_out):
    sums_out[...] = sums_in[...].astype(jnp.float32)
    norm_out[...] = norm_in[...]


def paired_halves(images, routes, projections, noise_weights):
    rows, coef = images.shape
    refs = projections.shape[1]
    H, width = coef // 2, 4 * refs
    F = H // 2
    T, TF = 8, 4
    tile = H // T
    TN = T - TF
    dma = pltpu.SemaphoreType.DMA
    bf16, f32 = jnp.bfloat16, jnp.float32
    piece = (2, refs, tile)
    sums, norm = pl.pallas_call(
        paired,
        out_shape=(
            jax.ShapeDtypeStruct((refs, coef), bf16),
            jax.ShapeDtypeStruct((1, rows), f32),
        ),
        in_specs=[pl.BlockSpec(memory_space=pltpu.HBM)] * 4,
        out_specs=(
            pl.BlockSpec(memory_space=pl.ANY),
            pl.BlockSpec(memory_space=pltpu.VMEM),
        ),
        scratch_shapes=[
            pltpu.VMEM((2, 2, rows), jnp.int32),
            pltpu.VMEM((H,), f32),
            pltpu.VMEM((2, 2, rows, H), bf16),
            pltpu.VMEM((2, 2, rows, F), bf16),
            pltpu.VMEM((4, 4, refs, H), bf16),
            pltpu.VMEM((4, 2, rows, width), f32),
            pltpu.VMEM((2, rows, width), f32),
            pltpu.VMEM((2, rows, width), f32),
            pltpu.VMEM((2, rows, width), jnp.int32),
            pltpu.VMEM((2, rows, width), jnp.int32),
            pltpu.VMEM((2, 2, rows, width), f32),
            pltpu.VMEM((2, 2, rows, width), f32),
            pltpu.VMEM((2, 2, 2, rows, width), bf16),
            pltpu.VMEM((2, rows, width), bf16),
            pltpu.VMEM((2, 2, 2, rows, width), bf16),
            pltpu.VMEM((2, width, 4 * rows), bf16),
            pltpu.VMEM((2, width, 4 * rows), bf16),
            pltpu.VMEM((T, 2, 2, 2, refs, tile), f32),
            pltpu.VMEM((3, TN) + piece, bf16),
            pltpu.VMEM((3, TN) + piece, bf16),
            pltpu.VMEM((2, T) + piece, bf16),
            pltpu.VMEM((2, T) + piece, bf16),
            pltpu.VMEM((T,) + piece, bf16),
            pltpu.VMEM((T,) + piece, bf16),
            pltpu.VMEM((T,) + piece, bf16),
            dma((4,)), dma((1,)), dma((1,)), dma((1,)), dma((2,)), dma((1,)), dma((2,)),
            dma((4, 2, len(CUTS))), dma((4, 2)), dma((1,)), dma((1,)), dma((3,)), dma((1,)), dma((1,)), dma((3,)),
            dma((1,)), dma((2,)), dma((1,)), dma((1,)), dma((2,)), dma((2, 2, 2)), dma((1,)), dma((2,)),
            dma((1,)), dma((3, TN)), dma((1,)), dma((2, T)), dma((1,)), dma((T,)),
            dma((1,)), dma((1,)), dma((1,)),
        ],
        compiler_params=pltpu.CompilerParams(
            collective_id=0, has_side_effects=True, vmem_limit_bytes=64 * 1024 * 1024 - 65536
        ),
        cost_estimate=pl.CostEstimate(
            flops=4 * 4 * rows * 4 * width * H // 2, bytes_accessed=4 * rows * coef, transcendentals=0
        ),
    )(images, routes.T, projections[0], noise_weights)
    block = coef // 2
    sums, norm = pl.pallas_call(
        hand_out,
        grid=(coef // block,),
        out_shape=(jax.ShapeDtypeStruct((refs, coef), f32), jax.ShapeDtypeStruct((1, rows), f32)),
        in_specs=[pl.BlockSpec((refs, block), lambda i: (0, i)), pl.BlockSpec((1, rows), lambda i: (0, 0))],
        out_specs=(pl.BlockSpec((refs, block), lambda i: (0, i)), pl.BlockSpec((1, rows), lambda i: (0, 0))),
    )(sums, norm)
    return (sums[None], norm[0])


def solution(mesh):
    sizes = dict(mesh.shape)
    direct = sizes["sub"] == 1 and sizes["reader"] == 4 and sizes["blk"] == 4
    return jax.shard_map(
        paired_halves if direct else routed,
        mesh=mesh,
        in_specs=(
            P(("parts", "blk", "reader"), "sub"),
            P(("parts", "blk", "reader"), None),
            P(("parts", "reader"), "blk", "sub"),
            P(("parts", "sub")),
        ),
        out_specs=(P(("parts", "reader"), "blk", "sub"), P(("parts", "blk", "reader"))),
        check_vma=False,
    )
```
